256 devices in a mesh: ctx: 32 (over z, y_lo, core), grp: 8 (over x, y_hi).
Axes of the slice: x: 4, y: 4 (y_hi: 2, y_lo: 2; y = y_hi * 2 + y_lo), z: 8, core: 2. Of those that a mesh axis runs over, the one named last changes fastest.
Arguments:
- queries: bfloat16 [8, 4096, 1792], P('grp', 'ctx'), may hold values from -160 to 160
- keys: bfloat16 [8, 4096, 256], P('grp', 'ctx'), may hold values from -6 to 6
- values: bfloat16 [8, 4096, 256], P('grp', 'ctx'), may hold values from -6 to 6
- segment_ids: int32 [8, 4096], P('grp', 'ctx'), may hold values from 0 to 3, never falling along the last dimension, each value on 1 to 3072 neighbouring positions
- turn_start: int32 [8, 32], P('grp'), may hold values from 0 to 4095, as said below
- turn_len: int32 [8, 32], P('grp'), may hold values from 1 to 40, as said below
- w_proj: bfloat16 [1792, 896], replicated, may hold values from -0.125 to 0.125
- gain: float32 [896], replicated, may hold values from 0.1 to 1.9
- gate_w: bfloat16 [9472, 896], P('ctx'), may hold values from -0.1875 to 0.1875
- up_w: bfloat16 [9472, 896], P('ctx'), may hold values from -0.1875 to 0.1875
- down_w: bfloat16 [9472, 896], P('ctx'), may hold values from -0.0625 to 0.0625
- cotangent: bfloat16 [8, 4096, 896], P('grp', 'ctx'), may hold values from -0.1875 to 0.1875
Outputs:
- context: bfloat16 [8, 4096, 1792], P('grp', 'ctx')
- talker_out: bfloat16 [8, 4096, 896], P('grp', 'ctx')
- grad_gate: float32 [9472, 896], P('ctx')
- grad_up: float32 [9472, 896], P('ctx')
- grad_down: float32 [9472, 896], P('ctx')
The draws below stay inside these ranges and needn't reach their ends.
Inputs may be any that keep to these rules, and one draw needn't show every extreme that they name: `turn_start`: turn t of a dialogue lies inside positions t * 128 to (t + 1) * 128 - 1, so turns don't intersect. `turn_len`: every dialogue has a turn of exactly 40 positions.
All inputs are finite; a program needn't handle non-finite values.
Results may differ from the reference program's by a relative error of at most 0.03.
Values may be sent and summed in bfloat16 or wider, within the bound.
A program may use at most 128 MiB of HBM per device.

```python
import math
import jax
import jax.numpy as jnp
import numpy as np
from jax import lax

HEADS = 14
KV_HEADS = 2
HEAD_DIM = 128
TD = 896
FF = 9472
TOK_DEV = 128
SEQ = 4096
DIALOGS = 8
TURNS = 32
ASSIST_DEV = 40
QW = 1792
KW = 256
N_CTX = 32
N_GRP = 8


def keys_base(key):
    shape = (DIALOGS, SEQ, KV_HEADS * HEAD_DIM)
    return jnp.clip(jax.random.normal(key, shape, jnp.float32), -5.0, 5.0)


def turn_table(key):
    first_key, second_key, third_key = jax.random.split(key, 3)
    lowest = max(1, ASSIST_DEV // 3)
    lengths = jax.random.randint(first_key, (DIALOGS, TURNS), lowest, ASSIST_DEV + 1)
    chosen = jax.random.randint(second_key, (DIALOGS, 1), 0, TURNS)
    turn_ids = jnp.arange(TURNS, dtype=jnp.int32)[None, :]
    lengths = jnp.where(turn_ids == chosen, ASSIST_DEV, lengths)
    offsets = jax.random.randint(third_key, (DIALOGS, TURNS), 0, TOK_DEV - lengths + 1)
    starts = turn_ids * TOK_DEV + offsets
    return (starts.astype(jnp.int32), lengths.astype(jnp.int32))


def draw_turn_start(key, part):
    starts, lengths = turn_table(key)
    return starts


def draw_turn_len(key, part):
    starts, lengths = turn_table(key)
    return lengths


def draw_keys(key, part):
    base_keys = keys_base(key)
    return base_keys.astype(jnp.bfloat16)


def draw_queries(key, part):
    key = jax.random.fold_in(key, 5)
    shape = (DIALOGS, SEQ, HEADS * HEAD_DIM)
    result_draw = jnp.clip(jax.random.normal(key, shape, jnp.float32), -5.0, 5.0)
    return result_draw.astype(jnp.bfloat16)


def block_scale(key, extent, cuts, smallest, top_value):
    def one(dim, shards_of):
        steps = jax.random.uniform(jax.random.fold_in(jax.random.fold_in(key, 6), dim), (shards_of,), jnp.float32, smallest / len(cuts), top_value / len(cuts))
        return jnp.repeat(jnp.exp(steps), extent[dim] // shards_of).reshape((-1,) + (1,) * (len(extent) - dim - 1))

    factor_of = one(*cuts[0])
    for cut in cuts[1:]:
        factor_of = factor_of * one(*cut)
    return factor_of


def length_profile(number_of, total, most, skew):
    weights = [(1 << 20) // math.isqrt(grade ** skew) + 1 for grade in range(2, number_of + 1)]
    rest, given = total - most - (number_of - 1), [1] * (number_of - 1)
    while rest > 0:
        candidates = [i for i in range(number_of - 1) if given[i] < most]
        mass, remaining = sum([weights[i] for i in candidates]), rest
        for i in candidates:
            addition = min(most - given[i], max(1, remaining * weights[i] // mass), rest)
            given[i] = given[i] + addition
            rest = rest - addition
    return np.array([most] + given)


def uneven_parts(key, count, total, bound, skew):
    if count == 2:
        one = jax.random.randint(key, (), max(1, total - bound), min(bound, total - 1) + 1)
        return jnp.stack([one, total - one])
    tallies = jnp.asarray(length_profile(count, total, bound, skew), jnp.int32)
    pairs = (count - 1) // 2
    donor, sink = tallies[1:1 + 2 * pairs:2], tallies[2:2 + 2 * pairs:2]
    slack = jnp.minimum(donor - 1, bound - sink)
    moved = jax.random.randint(jax.random.fold_in(key, 1), (pairs,), 0, 1 << 20) % (slack + 1)
    tallies = tallies.at[1:1 + 2 * pairs:2].set(donor - moved).at[2:2 + 2 * pairs:2].set(sink + moved)
    return tallies[jax.random.permutation(jax.random.fold_in(key, 2), count)]


def gaussian(own_key, dims, deviation, reach, shards=(), kind=jnp.bfloat16):
    values = deviation * jax.random.normal(own_key, dims, jnp.float32)
    if shards:
        values = values * block_scale(own_key, dims, shards, -0.22, 0.18)
    return jnp.clip(values, -reach, reach).astype(kind)


def setup_inputs(seed: int = 0) -> dict:
    key_list = jax.random.split(jax.random.key(seed), 13)
    return {
        "queries": draw_queries(jax.random.fold_in(key_list[12], 71), 0),
        "keys": draw_keys(jax.random.fold_in(key_list[12], 71), 0),
        "values": gaussian(key_list[2], (DIALOGS, SEQ, KW), 1.0, 6.0, ((0, 8), (1, 32))),
        "segment_ids": jax.vmap(lambda own: jnp.searchsorted(jnp.cumsum(uneven_parts(own, 4, SEQ, 3 * SEQ // 4, 0)), jnp.arange(SEQ), side="right"))(jax.random.split(key_list[3], DIALOGS)).reshape((DIALOGS, SEQ)).astype(jnp.int32),
        "turn_start": draw_turn_start(jax.random.fold_in(key_list[12], 71), 0),
        "turn_len": draw_turn_len(jax.random.fold_in(key_list[12], 71), 0),
        "w_proj": gaussian(key_list[6], (QW, TD), QW ** -0.5, 0.125),
        "gain": jnp.clip(1.0 + 0.18 * jax.random.normal(key_list[7], (TD,), jnp.float32), 0.1, 1.9),
        "gate_w": gaussian(key_list[8], (FF, TD), TD ** -0.5, 0.1875, ((0, 32),)),
        "up_w": gaussian(key_list[9], (FF, TD), TD ** -0.5, 0.1875, ((0, 32),)),
        "down_w": gaussian(key_list[10], (FF, TD), FF ** -0.5, 0.0625, ((0, 32),)),
        "cotangent": gaussian(key_list[11], (DIALOGS, SEQ, TD), ((5.0 / (N_GRP * SEQ)) ** 0.5), 0.1875, ((0, 8), (1, 32))),
    }


def reference(queries, keys, values, segment_ids, turn_start, turn_len, w_proj, gain, gate_w, up_w, down_w, cotangent):
    group_size = HEADS // KV_HEADS
    att_scale = 1.0 / math.sqrt(HEAD_DIM)
    positions = jnp.arange(SEQ, dtype=jnp.int32)

    def attend_dialog(inputs):
        query_all, key_all, value_all, segment = inputs
        keys_f32 = key_all.astype(jnp.float32).reshape(SEQ, KV_HEADS, HEAD_DIM)
        values_f32 = value_all.astype(jnp.float32).reshape(SEQ, KV_HEADS, HEAD_DIM)

        def attend_block(block_index):
            offset = (block_index * TOK_DEV).astype(jnp.int32)
            query_block = lax.dynamic_slice_in_dim(query_all, offset, TOK_DEV, 0).astype(jnp.float32)
            query_block = query_block.reshape(TOK_DEV, KV_HEADS, group_size, HEAD_DIM)
            seg_block = lax.dynamic_slice_in_dim(segment, offset, TOK_DEV, 0)
            query_pos = offset + jnp.arange(TOK_DEV, dtype=jnp.int32)
            allowed = (positions[None, :] <= query_pos[:, None]) & (segment[None, :] == seg_block[:, None])
            allowed = allowed[:, None, None, :]
            scores = jnp.einsum('tkgd,skd->tkgs', query_block, keys_f32) * att_scale
            scores = jnp.where(allowed, scores, -1e+30)
            row_max = lax.optimization_barrier(jnp.max(scores, axis=-1, keepdims=True))
            probs = jnp.where(allowed, jnp.exp(scores - row_max), 0.0)
            row_sum = lax.optimization_barrier(jnp.sum(probs, axis=-1))
            probs_bf = lax.optimization_barrier(probs.astype(jnp.bfloat16)).astype(jnp.float32)
            mixed = jnp.einsum('tkgs,skd->tkgd', probs_bf, values_f32) / row_sum[..., None]
            return mixed.reshape(TOK_DEV, HEADS * HEAD_DIM).astype(jnp.bfloat16)
        blocks = lax.map(attend_block, jnp.arange(SEQ // TOK_DEV, dtype=jnp.int32))
        return blocks.reshape(SEQ, HEADS * HEAD_DIM)
    context = lax.map(attend_dialog, (queries, keys, values, segment_ids))
    talker_in = jnp.dot(context.reshape(DIALOGS * SEQ, HEADS * HEAD_DIM), w_proj, preferred_element_type=jnp.float32).astype(jnp.bfloat16)
    turn_end = turn_start + turn_len
    inside = (positions[None, :, None] >= turn_start[:, None, :]) & (positions[None, :, None] < turn_end[:, None, :])
    assistant = jnp.any(inside, axis=-1).reshape(DIALOGS * SEQ)
    row_total = DIALOGS * N_CTX * ASSIST_DEV
    row_index = jnp.nonzero(assistant, size=row_total, fill_value=0)[0].astype(jnp.int32)
    live_count = jnp.sum(assistant.astype(jnp.int32))
    valid_row = (jnp.arange(row_total, dtype=jnp.int32) < live_count)[:, None]
    rows_in = jnp.where(valid_row, talker_in[row_index], jnp.zeros((), talker_in.dtype))
    rows_f32 = rows_in.astype(jnp.float32)
    normed = (rows_f32 * lax.rsqrt(lax.optimization_barrier(jnp.mean(rows_f32 * rows_f32, axis=-1, keepdims=True)) + 1e-06) * gain).astype(jnp.bfloat16)
    gate_pre = jnp.dot(normed, gate_w.T, preferred_element_type=jnp.float32)
    up_pre = jnp.dot(normed, up_w.T, preferred_element_type=jnp.float32)
    sigmoid_gate = jax.nn.sigmoid(gate_pre)
    activated = gate_pre * sigmoid_gate
    hidden = (activated * up_pre).astype(jnp.bfloat16)
    out_rows = (rows_f32 + jnp.dot(hidden, down_w, preferred_element_type=jnp.float32)).astype(jnp.bfloat16)
    out_rows = jnp.where(valid_row, out_rows, jnp.zeros((), out_rows.dtype))
    talker_out = jnp.zeros((DIALOGS * SEQ, TD), out_rows.dtype).at[row_index].add(out_rows)
    talker_out = talker_out.reshape(DIALOGS, SEQ, TD)
    cot_rows = jnp.where(valid_row, cotangent.reshape(DIALOGS * SEQ, TD)[row_index], jnp.zeros((), cotangent.dtype))
    d_hidden = jnp.dot(cot_rows, down_w.T, preferred_element_type=jnp.float32)
    d_gate = (d_hidden * up_pre * sigmoid_gate * (1.0 + gate_pre * (1.0 - sigmoid_gate))).astype(jnp.bfloat16)
    d_up = (d_hidden * activated).astype(jnp.bfloat16)
    grad_gate = jnp.dot(d_gate.T, normed, preferred_element_type=jnp.float32)
    grad_up = jnp.dot(d_up.T, normed, preferred_element_type=jnp.float32)
    grad_down = jnp.dot(hidden.T, cot_rows, preferred_element_type=jnp.float32)
    return (context, talker_out, grad_gate, grad_up, grad_down)
```

```python
import functools
import math

import jax
import jax.numpy as jnp
from jax import lax
from jax.experimental import pallas as pl
from jax.experimental.pallas import tpu as pltpu
from jax.sharding import PartitionSpec as P

HEADS = 14
KV_HEADS = 2
GROUP = HEADS // KV_HEADS
D = 128
TOK = 128
TD = 896
QW = HEADS * D
KW = KV_HEADS * D
SLOTS = 48
NZ = 8
AUX = 16
NEG = -1e30
MESH = pl.DeviceIdType.MESH
BF = jnp.bfloat16
F32 = jnp.float32


class Net:
    def __init__(self, send_sems, recv_sems):
        c = lax.axis_index("ctx")
        self.g = lax.axis_index("grp")
        self.ctx = c
        self.z = c // 4
        self.r = c % 4
        self.y = self.r // 2
        self.k = self.r % 2
        self.send_sems = send_sems
        self.recv_sems = recv_sems
        self.ids = {}
        self.sent = []

    def zmod(self, d):
        return lax.rem(self.z + d + NZ, NZ)

    def dev(self, where):
        z, y, k = self.z, self.y, self.k
        if where == "+":
            z = self.zmod(1)
        elif where == "-":
            z = self.zmod(-1)
        elif where == "y":
            y = 1 - y
        elif where == "c":
            k = 1 - k
        return (z * 4 + y * 2 + k, self.g)

    def copy(self, key, ref, where):
        n = self.ids.setdefault(key, len(self.ids))
        return pltpu.make_async_remote_copy(
            src_ref=ref,
            dst_ref=ref,
            send_sem=self.send_sems.at[n],
            recv_sem=self.recv_sems.at[n],
            device_id=self.dev(where),
            device_id_type=MESH,
        )

    def send(self, key, ref, where):
        copy = self.copy(key, ref, where)
        copy.start()
        self.sent.append(copy)

    def recv(self, key, ref, where):
        self.copy(key, ref, where).wait_recv()

    def drain(self):
        for copy in self.sent:
            copy.wait_send()
        self.sent = []


class Gather:
    def __init__(self, net, name, buf, early):
        self.net, self.name, self.buf, self.early = net, name, buf, early

    def slot(self, d, lane, other_core=False):
        net = self.net
        y = net.y if lane == "o" else 1 - net.y
        k = 1 - net.k if other_core else net.k
        return self.buf.at[net.zmod(d), y * 2 + k]

    def limit(self, way, lane):
        return 4 if (way == "+") == (lane == "o") else 3

    def to_core(self, d, lane):
        self.net.send((self.name, "c", d, lane), self.slot(d, lane), "c")

    def to_z(self, way, lane, step):
        d = -(step - 1) if way == "+" else step - 1
        self.net.send((self.name, way, lane, step), self.slot(d, lane), way)

    def to_y(self, d):
        self.net.send((self.name, "y", d), self.slot(d, "o"), "y")

    def start(self):
        if self.early:
            self.to_y(0)
        self.to_z("+", "o", 1)
        self.to_z("-", "o", 1)
        if not self.early:
            self.to_y(0)
        self.to_core(0, "o")

    def cross(self, d):
        self.net.recv((self.name, "y", d), self.slot(d, "x"), "y")
        if self.early:
            self.to_z("+", "x", 1)
            self.to_z("-", "x", 1)
        self.to_core(d, "x")

    def arrive(self, way, lane, step):
        top = self.limit(way, lane)
        if step > top:
            return
        d = -step if way == "+" else step
        if d == -4:
            d = 4
        self.net.recv((self.name, way, lane, step), self.slot(d, lane), way)
        if step < top:
            self.to_z(way, lane, step + 1)
        if not self.early:
            self.to_y(d)
        self.to_core(d, lane)

    def ring(self, step):
        for lane in ("o", "x") if self.early else ("o",):
            for way in ("+", "-"):
                self.arrive(way, lane, step)

    def crosses(self, step):
        if not self.early:
            for d in around(step):
                self.cross(d)

    def from_core(self, d):
        for lane in ("o", "x"):
            self.net.recv(
                (self.name, "c", d, lane), self.slot(d, lane, other_core=True), "c"
            )


def around(step):
    if step == 0:
        return (0,)
    if step == 4:
        return (4,)
    return (-step, step)


def attend_kernel(
    q_hbm,
    k_hbm,
    v_hbm,
    seg_ref,
    start_ref,
    len_ref,
    w_hbm,
    gain_ref,
    cot_hbm,
    ctx_ref,
    own_ref,
    rows_out,
    cot_out,
    gk,
    gv,
    gr,
    gc,
    q_raw,
    q_buf,
    w_buf,
    cot_buf,
    segq_ref,
    bias_ref,
    m_ref,
    acc_ref,
    send_sems,
    recv_sems,
    local_sems,
):
    net = Net(send_sems, recv_sems)
    z, r = net.z, net.r

    loads = [
        pltpu.make_async_copy(k_hbm.at[0], gk.at[z, r, pl.ds(0, TOK)], local_sems.at[0]),
        pltpu.make_async_copy(v_hbm.at[0], gv.at[z, r], local_sems.at[1]),
        pltpu.make_async_copy(q_hbm.at[0], q_raw, local_sems.at[2]),
        pltpu.make_async_copy(cot_hbm.at[0], cot_buf, local_sems.at[3]),
        pltpu.make_async_copy(w_hbm, w_buf, local_sems.at[4]),
    ]
    for load in loads:
        load.start()

    barrier = pltpu.get_barrier_semaphore()
    for where in ("+", "-", "y", "c"):
        pl.semaphore_signal(
            barrier, inc=1, device_id=net.dev(where), device_id_type=MESH
        )

    seg_row = seg_ref[...].astype(F32)
    gk[z, r, TOK : TOK + AUX, 0:D] = jnp.broadcast_to(seg_row, (AUX, D)).astype(BF)
    gk[z, r, TOK : TOK + AUX, D : 2 * D] = jnp.zeros((AUX, D), BF)

    keys = Gather(net, "k", gk, True)
    vals = Gather(net, "v", gv, False)
    rows = Gather(net, "r", gr, True)
    cots = Gather(net, "g", gc, False)

    loads[0].wait()
    loads[1].wait()
    pl.semaphore_wait(barrier, 4)
    keys.start()
    vals.start()

    segq_ref[...] = jnp.transpose(jnp.broadcast_to(seg_row, (TOK, D)))
    m_ref[...] = jnp.full(m_ref.shape, NEG, F32)
    acc_ref[...] = jnp.zeros(acc_ref.shape, F32)
    loads[2].wait()
    for h in range(HEADS):
        q_buf[h] = q_raw[:, h * D : (h + 1) * D]

    start = start_ref[0, net.ctx] - net.ctx * TOK
    length = len_ref[0, net.ctx]
    slot_id = lax.broadcasted_iota(jnp.int32, (SLOTS, TOK), 0)
    place = lax.broadcasted_iota(jnp.int32, (SLOTS, TOK), 1)
    packer = jnp.where((place - start == slot_id) & (slot_id < length), 1.0, 0.0).astype(BF)
    loads[3].wait()
    gc[z, r] = jnp.dot(packer, cot_buf[...], preferred_element_type=F32).astype(BF)

    factor = math.log2(math.e) / math.sqrt(D)

    def attend(d):
        zc = net.zmod(d)

        def work():
            segq = segq_ref[...]
            for b in range(4):
                seg_k = gk[zc, b, TOK : TOK + AUX, 0:D].astype(F32)[0:1]
                ok = segq == seg_k
                if d == 0:
                    at = (b - r) * TOK
                    kpos = lax.broadcasted_iota(jnp.int32, (TOK, D), 1) + at
                    qpos = lax.broadcasted_iota(jnp.int32, (TOK, D), 0)
                    ok = ok & (kpos <= qpos)
                bias_ref[:, b * TOK : (b + 1) * TOK] = jnp.where(ok, 0.0, NEG)

            def head(i, carry):
                for kv in range(KV_HEADS):
                    h = i + kv * GROUP
                    kc = gk[zc, :, 0:TOK, kv * D : (kv + 1) * D].reshape(4 * TOK, D)
                    vc = gv[zc, :, :, kv * D : (kv + 1) * D].reshape(4 * TOK, D)
                    vc = jnp.concatenate([vc, jnp.ones((4 * TOK, D), BF)], axis=1)
                    s = lax.dot_general(
                        q_buf[h], kc, (((1,), (1,)), ((), ())), preferred_element_type=F32
                    )
                    s = s * factor + bias_ref[...]
                    m_old = m_ref[h]
                    m_new = jnp.maximum(m_old, jnp.max(s, axis=1, keepdims=True))
                    p = jnp.exp2(s - jnp.concatenate([m_new] * 4, axis=1)).astype(BF)
                    alpha = jnp.exp2(m_old - m_new)
                    m_ref[h] = m_new
                    acc_ref[h] = acc_ref[h] * jnp.concatenate([alpha, alpha], axis=1) + jnp.dot(
                        p, vc, preferred_element_type=F32
                    )
                return carry

            lax.fori_loop(0, GROUP, head, 0)

        if d == 0:
            work()
        else:
            pl.when(zc < z)(work)

    def attend_step(step):
        for d in around(step):
            keys.from_core(d)
            vals.from_core(d)
            attend(d)

    keys.cross(0)
    vals.crosses(0)
    for step in range(1, 5):
        keys.ring(step)
        vals.ring(step)
        if step == 4:
            cots.start()
        attend_step(step - 1)
        vals.crosses(step)
    cots.ring(1)
    cots.crosses(0)
    attend_step(4)

    loads[4].wait()
    for h in range(HEADS):
        acc = acc_ref[h]
        ctx_ref[0, :, h * D : (h + 1) * D] = (acc[:, 0:D] / acc[:, D : 2 * D]).astype(BF)
    packed = jnp.dot(packer, ctx_ref[0], preferred_element_type=F32).astype(BF)
    own = jnp.dot(packed, w_buf[...], preferred_element_type=F32).astype(BF)
    own_ref[...] = own
    own = own.astype(F32)
    scale = lax.rsqrt(jnp.mean(own * own, axis=-1, keepdims=True) + 1e-06)
    gr[z, r] = (own * scale * gain_ref[...]).astype(BF)

    rows.start()
    rows.cross(0)
    cots.ring(2)
    cots.crosses(1)
    for step in range(1, 5):
        rows.ring(step)
        if step < 3:
            cots.ring(step + 2)
            cots.crosses(step + 1)
    cots.crosses(4)
    for step in range(5):
        for d in around(step):
            rows.from_core(d)
            cots.from_core(d)
    outs = [
        pltpu.make_async_copy(gr, rows_out, local_sems.at[5]),
        pltpu.make_async_copy(gc, cot_out, local_sems.at[6]),
    ]
    for out in outs:
        out.start()
    net.drain()
    for out in outs:
        out.wait()


def attend_call(queries, keys, values, segment_ids, turn_start, turn_len, w_proj, gain, cotangent):
    hbm = pl.BlockSpec(memory_space=pl.ANY)
    vmem = pl.BlockSpec(memory_space=pltpu.VMEM)
    smem = pl.BlockSpec(memory_space=pltpu.SMEM)
    wide = (NZ, 4, SLOTS, TD)
    return pl.pallas_call(
        attend_kernel,
        name="attend",
        out_shape=[
            jax.ShapeDtypeStruct((1, TOK, QW), BF),
            jax.ShapeDtypeStruct((SLOTS, TD), BF),
            jax.ShapeDtypeStruct(wide, BF),
            jax.ShapeDtypeStruct(wide, BF),
        ],
        in_specs=[hbm, hbm, hbm, vmem, smem, smem, hbm, vmem, hbm],
        out_specs=[vmem, vmem, hbm, hbm],
        scratch_shapes=[
            pltpu.VMEM((NZ, 4, TOK + AUX, KW), BF),
            pltpu.VMEM((NZ, 4, TOK, KW), BF),
            pltpu.VMEM(wide, BF),
            pltpu.VMEM(wide, BF),
            pltpu.VMEM((TOK, QW), BF),
            pltpu.VMEM((HEADS, TOK, D), BF),
            pltpu.VMEM((QW, TD), BF),
            pltpu.VMEM((TOK, TD), BF),
            pltpu.VMEM((TOK, D), F32),
            pltpu.VMEM((TOK, 4 * TOK), F32),
            pltpu.VMEM((HEADS, TOK, D), F32),
            pltpu.VMEM((HEADS, TOK, 2 * D), F32),
            pltpu.SemaphoreType.DMA((128,)),
            pltpu.SemaphoreType.DMA((128,)),
            pltpu.SemaphoreType.DMA((8,)),
        ],
        compiler_params=pltpu.CompilerParams(
            collective_id=1, has_side_effects=True, vmem_limit_bytes=48 << 20
        ),
    )(queries, keys, values, segment_ids, turn_start, turn_len, w_proj, gain, cotangent)


def shards(
    queries,
    keys,
    values,
    segment_ids,
    turn_start,
    turn_len,
    w_proj,
    gain,
    gate_w,
    up_w,
    down_w,
    cotangent,
):
    context, own_rows, rows_all, cot_all = attend_call(
        queries, keys, values, segment_ids, turn_start, turn_len, w_proj, gain[None], cotangent
    )
    rows_all = rows_all.reshape(NZ * 4 * SLOTS, TD)
    cot_all = cot_all.reshape(NZ * 4 * SLOTS, TD)
    own_rows = own_rows.astype(F32)
    ctx_index = lax.axis_index("ctx")
    start = turn_start[0, ctx_index] - ctx_index * TOK
    slot_id = jnp.arange(SLOTS, dtype=jnp.int32)[:, None]
    place = jnp.arange(TOK, dtype=jnp.int32)[None, :]
    packer = ((place - start == slot_id) & (slot_id < turn_len[0, ctx_index])).astype(BF)
    contract_last = (((1,), (1,)), ((), ()))
    contract_first = (((0,), (0,)), ((), ()))
    gate_pre = lax.dot_general(gate_w, rows_all, contract_last, preferred_element_type=jnp.float32)
    up_pre = lax.dot_general(up_w, rows_all, contract_last, preferred_element_type=jnp.float32)
    sigmoid_gate = jax.nn.sigmoid(gate_pre)
    activated = gate_pre * sigmoid_gate
    hidden_t = (activated * up_pre).astype(jnp.bfloat16)
    ffn_rows = lax.psum_scatter(
        lax.dot_general(
            hidden_t, down_w, contract_first, preferred_element_type=jnp.float32
        ).astype(jnp.bfloat16),
        "ctx",
        scatter_dimension=0,
        tiled=True,
    ).astype(jnp.float32)
    out_rows = (own_rows + ffn_rows).astype(jnp.bfloat16)
    talker_out = lax.dot_general(
        packer, out_rows, contract_first, preferred_element_type=jnp.float32
    ).astype(jnp.bfloat16)
    d_hidden = lax.dot_general(down_w, cot_all, contract_last, preferred_element_type=jnp.float32)
    grad_down = jnp.dot(hidden_t, cot_all, preferred_element_type=jnp.float32)
    d_gate = (d_hidden * up_pre * sigmoid_gate * (1.0 + gate_pre * (1.0 - sigmoid_gate))).astype(
        jnp.bfloat16
    )
    d_up = (d_hidden * activated).astype(jnp.bfloat16)
    grad_gate = jnp.dot(d_gate, rows_all, preferred_element_type=jnp.float32)
    grad_up = jnp.dot(d_up, rows_all, preferred_element_type=jnp.float32)
    grad_gate, grad_up, grad_down = (
        lax.psum(grad_gate.astype(jnp.bfloat16), "grp").astype(jnp.float32),
        lax.psum(grad_up.astype(jnp.bfloat16), "grp").astype(jnp.float32),
        lax.psum(grad_down.astype(jnp.bfloat16), "grp").astype(jnp.float32),
    )
    return (context, talker_out[None], grad_gate, grad_up, grad_down)


def solution(mesh):
    in_specs = (
        P("grp", "ctx", None),
        P("grp", "ctx", None),
        P("grp", "ctx", None),
        P("grp", "ctx"),
        P("grp", None),
        P("grp", None),
        P(),
        P(),
        P("ctx", None),
        P("ctx", None),
        P("ctx", None),
        P("grp", "ctx", None),
    )
    out_specs = (
        P("grp", "ctx", None),
        P("grp", "ctx", None),
        P("ctx", None),
        P("ctx", None),
        P("ctx", None),
    )
    return jax.shard_map(shards, mesh=mesh, in_specs=in_specs, out_specs=out_specs, check_vma=False)
```

```python
import functools
import math

import jax
import jax.numpy as jnp
from jax import lax
from jax.experimental import pallas as pl
from jax.experimental.pallas import tpu as pltpu
from jax.sharding import PartitionSpec as P

HEADS = 14
KV_HEADS = 2
GROUP = HEADS // KV_HEADS
D = 128
TOK = 128
TD = 896
QW = HEADS * D
KW = KV_HEADS * D
SLOTS = 48
NZ = 8
NX = 4
FFD = 296
GROWS = 896
A_ROWS = 512
A_PART = 64
B_PART = 48
B_HALF = (32, 16)
CHUNK = 256
AUX = 16
NEG = -1e30
MESH = pl.DeviceIdType.MESH
BF = jnp.bfloat16
F32 = jnp.float32


class Net:
    def __init__(self, send_sems, recv_sems):
        c = lax.axis_index("ctx")
        g = lax.axis_index("grp")
        self.ctx = c
        self.z = c // 4
        self.r = c % 4
        self.y = self.r // 2
        self.k = self.r % 2
        self.x = g // 2
        self.h = g % 2
        self.send_sems = send_sems
        self.recv_sems = recv_sems
        self.ids = {}
        self.sent = []

    def zmod(self, d):
        return lax.rem(self.z + d + NZ, NZ)

    def xmod(self, d):
        return lax.rem(self.x + d + NX, NX)

    def dev(self, where):
        z, y, k, x, h = self.z, self.y, self.k, self.x, self.h
        if where == "+":
            z = self.zmod(1)
        elif where == "-":
            z = self.zmod(-1)
        elif where == "y":
            y = 1 - y
        elif where == "c":
            k = 1 - k
        elif where == "x+":
            x = self.xmod(1)
        elif where == "x-":
            x = self.xmod(-1)
        elif where == "h":
            h = 1 - h
        return (z * 4 + y * 2 + k, x * 2 + h)

    def greet(self, barrier, places):
        for where in places:
            pl.semaphore_signal(
                barrier, inc=1, device_id=self.dev(where), device_id_type=MESH
            )

    def copy(self, key, src, dst, where):
        n = self.ids.setdefault(key, len(self.ids))
        return pltpu.make_async_remote_copy(
            src_ref=src,
            dst_ref=dst,
            send_sem=self.send_sems.at[n],
            recv_sem=self.recv_sems.at[n],
            device_id=self.dev(where),
            device_id_type=MESH,
        )

    def send(self, key, src, where, dst=None):
        copy = self.copy(key, src, src if dst is None else dst, where)
        copy.start()
        self.sent.append(copy)

    def recv(self, key, ref, where):
        self.copy(key, ref, ref, where).wait_recv()

    def drain(self):
        for copy in self.sent:
            copy.wait_send()
        self.sent = []


class Gather:
    def __init__(self, net, name, buf, early):
        self.net, self.name, self.buf, self.early = net, name, buf, early

    def slot(self, d, lane, other_core=False):
        net = self.net
        y = net.y if lane == "o" else 1 - net.y
        k = 1 - net.k if other_core else net.k
        return self.buf.at[net.zmod(d), y * 2 + k]

    def limit(self, way, lane):
        return 4 if (way == "+") == (lane == "o") else 3

    def to_core(self, d, lane):
        self.net.send((self.name, "c", d, lane), self.slot(d, lane), "c")

    def to_z(self, way, lane, step):
        d = -(step - 1) if way == "+" else step - 1
        self.net.send((self.name, way, lane, step), self.slot(d, lane), way)

    def to_y(self, d):
        self.net.send((self.name, "y", d), self.slot(d, "o"), "y")

    def start(self):
        if self.early:
            self.to_y(0)
        self.to_z("+", "o", 1)
        self.to_z("-", "o", 1)
        if not self.early:
            self.to_y(0)
        self.to_core(0, "o")

    def cross(self, d):
        self.net.recv((self.name, "y", d), self.slot(d, "x"), "y")
        if self.early:
            self.to_z("+", "x", 1)
            self.to_z("-", "x", 1)
        self.to_core(d, "x")

    def arrive(self, way, lane, step):
        top = self.limit(way, lane)
        if step > top:
            return
        d = -step if way == "+" else step
        if d == -4:
            d = 4
        self.net.recv((self.name, way, lane, step), self.slot(d, lane), way)
        if step < top:
            self.to_z(way, lane, step + 1)
        if not self.early:
            self.to_y(d)
        self.to_core(d, lane)

    def ring(self, step):
        for lane in ("o", "x") if self.early else ("o",):
            for way in ("+", "-"):
                self.arrive(way, lane, step)

    def crosses(self, step):
        if not self.early:
            for d in around(step):
                self.cross(d)

    def from_core(self, d):
        for lane in ("o", "x"):
            self.net.recv(
                (self.name, "c", d, lane), self.slot(d, lane, other_core=True), "c"
            )


def around(step):
    if step == 0:
        return (0,)
    if step == 4:
        return (4,)
    return (-step, step)


def attend_kernel(
    q_hbm,
    k_hbm,
    v_hbm,
    seg_ref,
    start_ref,
    len_ref,
    w_hbm,
    gain_ref,
    cot_hbm,
    ctx_ref,
    own_ref,
    rows_out,
    cot_out,
    gk,
    gv,
    gr,
    gc,
    q_raw,
    q_buf,
    w_buf,
    cot_buf,
    segq_ref,
    bias_ref,
    m_ref,
    acc_ref,
    send_sems,
    recv_sems,
    local_sems,
):
    net = Net(send_sems, recv_sems)
    z, r = net.z, net.r

    loads = [
        pltpu.make_async_copy(k_hbm.at[0], gk.at[z, r, pl.ds(0, TOK)], local_sems.at[0]),
        pltpu.make_async_copy(v_hbm.at[0], gv.at[z, r], local_sems.at[1]),
        pltpu.make_async_copy(q_hbm.at[0], q_raw, local_sems.at[2]),
        pltpu.make_async_copy(cot_hbm.at[0], cot_buf, local_sems.at[3]),
        pltpu.make_async_copy(w_hbm, w_buf, local_sems.at[4]),
    ]
    for load in loads:
        load.start()

    barrier = pltpu.get_barrier_semaphore()
    net.greet(barrier, ("+", "-", "y", "c"))

    seg_row = seg_ref[...].astype(F32)
    gk[z, r, TOK : TOK + AUX, 0:D] = jnp.broadcast_to(seg_row, (AUX, D)).astype(BF)
    gk[z, r, TOK : TOK + AUX, D : 2 * D] = jnp.zeros((AUX, D), BF)

    keys = Gather(net, "k", gk, True)
    vals = Gather(net, "v", gv, False)
    rows = Gather(net, "r", gr, True)
    cots = Gather(net, "g", gc, False)

    loads[0].wait()
    loads[1].wait()
    pl.semaphore_wait(barrier, 4)
    keys.start()
    vals.start()

    segq_ref[...] = jnp.transpose(jnp.broadcast_to(seg_row, (TOK, D)))
    m_ref[...] = jnp.full(m_ref.shape, NEG, F32)
    acc_ref[...] = jnp.zeros(acc_ref.shape, F32)
    loads[2].wait()
    for h in range(HEADS):
        q_buf[h] = q_raw[:, h * D : (h + 1) * D]

    start = start_ref[0, net.ctx] - net.ctx * TOK
    length = len_ref[0, net.ctx]
    slot_id = lax.broadcasted_iota(jnp.int32, (SLOTS, TOK), 0)
    place = lax.broadcasted_iota(jnp.int32, (SLOTS, TOK), 1)
    packer = jnp.where((place - start == slot_id) & (slot_id < length), 1.0, 0.0).astype(BF)
    loads[3].wait()
    gc[z, r] = jnp.dot(packer, cot_buf[...], preferred_element_type=F32).astype(BF)

    factor = math.log2(math.e) / math.sqrt(D)

    def attend(d):
        zc = net.zmod(d)

        def work():
            segq = segq_ref[...]
            for b in range(4):
                seg_k = gk[zc, b, TOK : TOK + AUX, 0:D].astype(F32)[0:1]
                ok = segq == seg_k
                if d == 0:
                    at = (b - r) * TOK
                    kpos = lax.broadcasted_iota(jnp.int32, (TOK, D), 1) + at
                    qpos = lax.broadcasted_iota(jnp.int32, (TOK, D), 0)
                    ok = ok & (kpos <= qpos)
                bias_ref[:, b * TOK : (b + 1) * TOK] = jnp.where(ok, 0.0, NEG)

            def head(i, carry):
                for kv in range(KV_HEADS):
                    h = i + kv * GROUP
                    kc = gk[zc, :, 0:TOK, kv * D : (kv + 1) * D].reshape(4 * TOK, D)
                    vc = gv[zc, :, :, kv * D : (kv + 1) * D].reshape(4 * TOK, D)
                    vc = jnp.concatenate([vc, jnp.ones((4 * TOK, D), BF)], axis=1)
                    s = lax.dot_general(
                        q_buf[h], kc, (((1,), (1,)), ((), ())), preferred_element_type=F32
                    )
                    s = s * factor + bias_ref[...]
                    m_old = m_ref[h]
                    m_new = jnp.maximum(m_old, jnp.max(s, axis=1, keepdims=True))
                    p = jnp.exp2(s - jnp.concatenate([m_new] * 4, axis=1)).astype(BF)
                    alpha = jnp.exp2(m_old - m_new)
                    m_ref[h] = m_new
                    acc_ref[h] = acc_ref[h] * jnp.concatenate([alpha, alpha], axis=1) + jnp.dot(
                        p, vc, preferred_element_type=F32
                    )
                return carry

            lax.fori_loop(0, GROUP, head, 0)

        if d == 0:
            work()
        else:
            pl.when(zc < z)(work)

    def attend_step(step):
        for d in around(step):
            keys.from_core(d)
            vals.from_core(d)
            attend(d)

    keys.cross(0)
    vals.crosses(0)
    for step in range(1, 5):
        keys.ring(step)
        vals.ring(step)
        if step == 4:
            cots.start()
        attend_step(step - 1)
        vals.crosses(step)
    cots.ring(1)
    cots.crosses(0)
    attend_step(4)

    loads[4].wait()
    for h in range(HEADS):
        acc = acc_ref[h]
        ctx_ref[0, :, h * D : (h + 1) * D] = (acc[:, 0:D] / acc[:, D : 2 * D]).astype(BF)
    packed = jnp.dot(packer, ctx_ref[0], preferred_element_type=F32).astype(BF)
    own = jnp.dot(packed, w_buf[...], preferred_element_type=F32).astype(BF)
    own_ref[...] = own
    own = own.astype(F32)
    scale = lax.rsqrt(jnp.mean(own * own, axis=-1, keepdims=True) + 1e-06)
    gr[z, r] = (own * scale * gain_ref[...]).astype(BF)

    rows.start()
    rows.cross(0)
    cots.ring(2)
    cots.crosses(1)
    for step in range(1, 5):
        rows.ring(step)
        if step < 3:
            cots.ring(step + 2)
            cots.crosses(step + 1)
    cots.crosses(4)
    for step in range(5):
        for d in around(step):
            rows.from_core(d)
            cots.from_core(d)
    outs = [
        pltpu.make_async_copy(gr, rows_out, local_sems.at[5]),
        pltpu.make_async_copy(gc, cot_out, local_sems.at[6]),
    ]
    for out in outs:
        out.start()
    net.drain()
    for out in outs:
        out.wait()


def attend_call(queries, keys, values, segment_ids, turn_start, turn_len, w_proj, gain, cotangent):
    hbm = pl.BlockSpec(memory_space=pl.ANY)
    vmem = pl.BlockSpec(memory_space=pltpu.VMEM)
    smem = pl.BlockSpec(memory_space=pltpu.SMEM)
    wide = (NZ, 4, SLOTS, TD)
    return pl.pallas_call(
        attend_kernel,
        name="attend",
        out_shape=[
            jax.ShapeDtypeStruct((1, TOK, QW), BF),
            jax.ShapeDtypeStruct((SLOTS, TD), BF),
            jax.ShapeDtypeStruct(wide, BF),
            jax.ShapeDtypeStruct(wide, BF),
        ],
        in_specs=[hbm, hbm, hbm, vmem, smem, smem, hbm, vmem, hbm],
        out_specs=[vmem, vmem, hbm, hbm],
        scratch_shapes=[
            pltpu.VMEM((NZ, 4, TOK + AUX, KW), BF),
            pltpu.VMEM((NZ, 4, TOK, KW), BF),
            pltpu.VMEM(wide, BF),
            pltpu.VMEM(wide, BF),
            pltpu.VMEM((TOK, QW), BF),
            pltpu.VMEM((HEADS, TOK, D), BF),
            pltpu.VMEM((QW, TD), BF),
            pltpu.VMEM((TOK, TD), BF),
            pltpu.VMEM((TOK, D), F32),
            pltpu.VMEM((TOK, 4 * TOK), F32),
            pltpu.VMEM((HEADS, TOK, D), F32),
            pltpu.VMEM((HEADS, TOK, 2 * D), F32),
            pltpu.SemaphoreType.DMA((128,)),
            pltpu.SemaphoreType.DMA((128,)),
            pltpu.SemaphoreType.DMA((8,)),
        ],
        compiler_params=pltpu.CompilerParams(
            collective_id=1, has_side_effects=True, vmem_limit_bytes=48 << 20
        ),
    )(queries, keys, values, segment_ids, turn_start, turn_len, w_proj, gain, cotangent)


class GradSum:
    def __init__(self, net, g32, res, sa, ra, sa3, sah, rah, sb, rb, b32, sbx, rbx, sb3):
        self.net, self.g32, self.res = net, g32, res
        self.sa, self.ra, self.sa3, self.sah, self.rah = sa, ra, sa3, sah, rah
        self.sb, self.rb, self.b32, self.sbx, self.rbx, self.sb3 = sb, rb, b32, sbx, rbx, sb3

    def a_rows(self, x, h, count=1):
        return pl.ds(pl.multiple_of((x * 2 + h) * A_PART, A_PART), count * A_PART)

    def b_rows(self, h, x, half=None):
        at = A_ROWS + (h * NX + x) * B_PART
        size = B_PART
        if half is not None:
            at, size = at + half * B_HALF[0], B_HALF[half]
        return pl.ds(pl.multiple_of(at, 16), size)

    def start(self):
        net = self.net
        self.sb[...] = self.g32[
            pl.ds(pl.multiple_of(A_ROWS + (1 - net.h) * NX * B_PART, 16), NX * B_PART)
        ].astype(BF)
        net.send("b0", self.sb, "h", self.rb)
        for i in range(NX):
            for h in range(2):
                at = (i * 2 + h) * A_PART
                self.sa[i, h] = self.g32[at : at + A_PART].astype(BF)
        far = net.xmod(2)
        net.send("a1+", self.sa.at[far, 0], "x+", self.ra.at[0])
        net.send("a1-", self.sa.at[far, 1], "x-", self.ra.at[1])
        net.send("a2+", self.sa.at[net.xmod(1), 1], "x+", self.ra.at[2])
        net.send("a2-", self.sa.at[net.xmod(-1), 0], "x-", self.ra.at[3])

    def a_pass(self):
        net = self.net
        for n, (way, d, half) in enumerate((("+", 1, 0), ("-", -1, 1))):
            net.recv("a1" + way, self.ra.at[n], "x" + way)
            own = self.g32[self.a_rows(net.xmod(d), half)]
            self.sa3[n] = (own + self.ra[n].astype(F32)).astype(BF)
            net.send("a3" + way, self.sa3.at[n], "x" + way, self.ra.at[4 + n])

    def a_cross(self):
        net = self.net
        net.recv("a2+", self.ra.at[2], "x+")
        net.recv("a2-", self.ra.at[3], "x-")
        net.recv("a3+", self.ra.at[4], "x+")
        net.recv("a3-", self.ra.at[5], "x-")
        for half, (one, two) in enumerate(((3, 4), (2, 5))):
            rows = self.a_rows(net.x, half)
            self.g32[rows] = self.g32[rows] + self.ra[one].astype(F32) + self.ra[two].astype(F32)
        self.sah[...] = self.g32[self.a_rows(net.x, 1 - net.h)].astype(BF)
        net.send("ah", self.sah, "h", self.rah)

    def a_final(self):
        net = self.net
        net.recv("ah", self.rah, "h")
        rows = self.a_rows(net.x, net.h)
        self.res[rows] = (self.g32[rows] + self.rah[...].astype(F32)).astype(BF)
        for key, where in (("e0", "h"), ("e1+", "x+"), ("e1-", "x-")):
            net.send(key, self.res.at[rows], where)

    def a_spread(self):
        net = self.net
        rows = self.res.at[self.a_rows(net.x, 1 - net.h)]
        net.recv("e0", rows, "h")
        net.send("e2+", rows, "x+")
        net.send("e2-", rows, "x-")

    def a_forward(self):
        net = self.net
        for way, d, half in (("+", -1, 0), ("-", 1, 1)):
            x = net.xmod(d)
            net.recv("e1" + way, self.res.at[self.a_rows(x, net.h)], "x" + way)
            net.recv("e2" + way, self.res.at[self.a_rows(x, 1 - net.h)], "x" + way)
            net.send("f" + way, self.res.at[self.a_rows(x, half)], "x" + way)

    def a_end(self):
        net = self.net
        for way, half in (("+", 0), ("-", 1)):
            net.recv("f" + way, self.res.at[self.a_rows(net.xmod(2), half)], "x" + way)

    def b_half(self, half):
        return pl.ds(0 if half == 0 else B_HALF[0], B_HALF[half])

    def b_start(self):
        net = self.net
        net.recv("b0", self.rb, "h")
        for i in range(NX):
            at = slice(i * B_PART, (i + 1) * B_PART)
            own = self.g32[self.b_rows(net.h, i)]
            total = own + self.rb[at].astype(F32)
            self.b32[i] = total
            self.sbx[i] = total.astype(BF)
        for n, (key, way, d, half) in enumerate(
            (("b1+", "+", 2, 0), ("b1-", "-", 2, 1), ("b2+", "+", 1, 1), ("b2-", "-", -1, 0))
        ):
            net.send(
                key,
                self.sbx.at[net.xmod(d), self.b_half(half)],
                "x" + way,
                self.rbx.at[n, pl.ds(0, B_HALF[half])],
            )

    def b_pass(self):
        net = self.net
        for n, (way, d, half) in enumerate((("+", 1, 0), ("-", -1, 1))):
            size = B_HALF[half]
            net.recv("b1" + way, self.rbx.at[n, pl.ds(0, size)], "x" + way)
            own = self.b32[net.xmod(d), self.b_half(half)]
            self.sb3[n, 0:size] = (own + self.rbx[n, 0:size].astype(F32)).astype(BF)
            net.send(
                "b3" + way,
                self.sb3.at[n, pl.ds(0, size)],
                "x" + way,
                self.rbx.at[4 + n, pl.ds(0, size)],
            )

    def b_final(self):
        net = self.net
        net.recv("b2+", self.rbx.at[2, pl.ds(0, B_HALF[1])], "x+")
        net.recv("b2-", self.rbx.at[3, pl.ds(0, B_HALF[0])], "x-")
        net.recv("b3+", self.rbx.at[4, pl.ds(0, B_HALF[0])], "x+")
        net.recv("b3-", self.rbx.at[5, pl.ds(0, B_HALF[1])], "x-")
        for half, (one, two) in enumerate(((3, 4), (2, 5))):
            size = B_HALF[half]
            total = (
                self.b32[net.x, self.b_half(half)]
                + self.rbx[one, 0:size].astype(F32)
                + self.rbx[two, 0:size].astype(F32)
            )
            self.res[self.b_rows(net.h, net.x, half)] = total.astype(BF)
        rows = self.res.at[self.b_rows(net.h, net.x)]
        for key, where in (("q+", "x+"), ("q-", "x-"), ("p0", "h")):
            net.send(key, rows, where)

    def b_forward(self):
        net = self.net
        for n, (way, d, half) in enumerate((("+", -1, 0), ("-", 1, 1))):
            x = net.xmod(d)
            rows = self.res.at[self.b_rows(net.h, x)]
            net.recv("q" + way, rows, "x" + way)
            net.send("s" + way, self.res.at[self.b_rows(net.h, x, half)], "x" + way)
            net.send("p%d" % (n + 1), rows, "h")

    def b_cross(self):
        net = self.net
        x = net.xmod(2)
        for way, half in (("+", 0), ("-", 1)):
            net.recv("s" + way, self.res.at[self.b_rows(net.h, x, half)], "x" + way)
        net.send("p3", self.res.at[self.b_rows(net.h, x)], "h")

    def b_end(self):
        net = self.net
        for n, d in enumerate((0, -1, 1, 2)):
            net.recv("p%d" % n, self.res.at[self.b_rows(1 - net.h, net.xmod(d))], "h")


class RowSum:
    def __init__(self, net, part, from_core, stage, land, ys, yr):
        self.net, self.part, self.from_core = net, part, from_core
        self.stage, self.land, self.ys, self.yr = stage, land, ys, yr
        self.at = {}
        for way in ("+", "-"):
            for lane in ("o", "x"):
                for step in range(1, self.limit(way, lane) + 1):
                    self.at[way, lane, step] = len(self.at)

    def limit(self, way, lane):
        return 4 if (way == "+") == (lane == "o") else 3

    def swap(self, d):
        net = self.net
        z = net.zmod(d)
        net.send(("c", d), self.part.at[1 - net.k, z], "c", self.from_core.at[z])

    def swapped(self, d):
        self.net.recv(("c", d), self.from_core.at[self.net.zmod(d)], "c")

    def own(self, d, lane):
        net = self.net
        z = net.zmod(d)
        y = net.y if lane == "o" else 1 - net.y
        return self.part[net.k, z, y].astype(F32) + self.from_core[z, y].astype(F32)

    def landed(self, way, lane, step):
        n = self.at[way, lane, step]
        self.net.recv(("z", way, lane, step), self.land.at[n], way)
        return self.land[n].astype(F32)

    def step(self, step):
        for lane in ("o", "x"):
            for way in ("+", "-"):
                top = self.limit(way, lane)
                if step > top:
                    continue
                left = top - step + 1
                d = left if way == "+" or left == 4 else -left
                total = self.own(d, lane)
                if step > 1:
                    total = total + self.landed(way, lane, step - 1)
                n = self.at[way, lane, step]
                self.stage[n] = total.astype(BF)
                self.net.send(("z", way, lane, step), self.stage.at[n], way, self.land.at[n])

    def across(self):
        total = self.own(0, "x")
        for way in ("+", "-"):
            total = total + self.landed(way, "x", self.limit(way, "x"))
        self.ys[...] = total.astype(BF)
        self.net.send("y", self.ys, "y", self.yr)

    def result(self):
        total = self.own(0, "o")
        for way in ("+", "-"):
            total = total + self.landed(way, "o", self.limit(way, "o"))
        self.net.recv("y", self.yr, "y")
        return total + self.yr[...].astype(F32)


def talk_kernel(
    rows_hbm,
    cot_hbm,
    own_ref,
    start_ref,
    len_ref,
    gate_ref,
    up_ref,
    down_ref,
    out_ref,
    grads_out,
    rows,
    cots,
    hid,
    d_gate,
    d_up,
    hid_rows,
    g32,
    res,
    sa,
    ra,
    sa3,
    sah,
    rah,
    sb,
    rb,
    b32,
    sbx,
    rbx,
    sb3,
    part,
    from_core,
    stage,
    land,
    ys,
    yr,
    send_sems,
    recv_sems,
    local_sems,
):
    net = Net(send_sems, recv_sems)
    loads = [
        pltpu.make_async_copy(rows_hbm, rows, local_sems.at[0]),
        pltpu.make_async_copy(cot_hbm, cots, local_sems.at[1]),
    ]
    for load in loads:
        load.start()
    barrier = pltpu.get_barrier_semaphore()
    places = ("+", "-", "y", "c", "x+", "x-", "h")
    net.greet(barrier, places)
    for load in loads:
        load.wait()

    nt = (((1,), (1,)), ((), ()))

    def chunk(i, carry):
        at = pl.ds(pl.multiple_of(i * CHUNK, CHUNK), CHUNK)
        row = rows[at]
        cot = cots[at]
        gate = lax.dot_general(gate_ref[...], row, nt, preferred_element_type=F32)
        up = lax.dot_general(up_ref[...], row, nt, preferred_element_type=F32)
        d_hidden = lax.dot_general(down_ref[...], cot, nt, preferred_element_type=F32)
        sig = jax.nn.sigmoid(gate)
        act = gate * sig
        hidden = act * up
        hid[:, at] = hidden.astype(BF)
        hid_rows[at] = jnp.transpose(hidden).astype(BF)
        d_gate[:, at] = (d_hidden * up * sig * (1.0 + gate * (1.0 - sig))).astype(BF)
        d_up[:, at] = (d_hidden * act).astype(BF)
        return carry

    lax.fori_loop(0, rows.shape[0] // CHUNK, chunk, 0)

    for n, (left, right) in enumerate(((hid, cots), (d_gate, rows), (d_up, rows))):
        g32[n * FFD : (n + 1) * FFD] = jnp.dot(
            left[...], right[...], preferred_element_type=F32
        )
    g32[3 * FFD :] = jnp.zeros((GROWS - 3 * FFD, TD), F32)

    grads = GradSum(net, g32, res, sa, ra, sa3, sah, rah, sb, rb, b32, sbx, rbx, sb3)
    sums = RowSum(net, part, from_core, stage, land, ys, yr)
    pl.semaphore_wait(barrier, len(places))
    grads.start()

    def ffn(d):
        z = net.zmod(d)
        at = pl.ds(pl.multiple_of(z * 4 * SLOTS, 4 * SLOTS), 4 * SLOTS)
        total = jnp.dot(hid_rows[at], down_ref[...], preferred_element_type=F32).astype(BF)
        for b in range(4):
            part[b % 2, z, b // 2] = total[b * SLOTS : (b + 1) * SLOTS]
        sums.swap(d)

    for d in (4, 3, -3):
        ffn(d)
    grads.a_pass()
    for d in (2, -2):
        ffn(d)
    for d in (4, 3, -3):
        sums.swapped(d)
    sums.step(1)
    for d in (1, -1, 0):
        ffn(d)
    grads.b_start()
    for d in (2, -2):
        sums.swapped(d)
    sums.step(2)
    grads.a_cross()
    for d in (1, -1, 0):
        sums.swapped(d)
    sums.step(3)
    grads.b_pass()
    grads.a_final()
    sums.step(4)
    grads.b_final()
    grads.a_spread()
    sums.across()
    grads.b_forward()
    grads.a_forward()
    grads.b_cross()

    start = start_ref[0, net.ctx] - net.ctx * TOK
    length = len_ref[0, net.ctx]
    place = lax.broadcasted_iota(jnp.int32, (TOK, SLOTS), 0)
    slot_id = lax.broadcasted_iota(jnp.int32, (TOK, SLOTS), 1)
    spread = jnp.where((place - start == slot_id) & (slot_id < length), 1.0, 0.0).astype(BF)
    out_rows = (own_ref[...].astype(F32) + sums.result()).astype(BF)
    out_ref[0] = jnp.dot(spread, out_rows, preferred_element_type=F32).astype(BF)

    grads.a_end()
    grads.b_end()
    save = pltpu.make_async_copy(res, grads_out, local_sems.at[2])
    save.start()
    net.drain()
    save.wait()


def talk_call(rows, cots, own, turn_start, turn_len, gate_w, up_w, down_w):
    hbm = pl.BlockSpec(memory_space=pl.ANY)
    vmem = pl.BlockSpec(memory_space=pltpu.VMEM)
    smem = pl.BlockSpec(memory_space=pltpu.SMEM)
    total = NZ * 4 * SLOTS
    return pl.pallas_call(
        talk_kernel,
        name="talk",
        out_shape=[
            jax.ShapeDtypeStruct((1, TOK, TD), BF),
            jax.ShapeDtypeStruct((GROWS, TD), BF),
        ],
        in_specs=[hbm, hbm, vmem, smem, smem, vmem, vmem, vmem],
        out_specs=[vmem, hbm],
        scratch_shapes=[
            pltpu.VMEM((total, TD), BF),
            pltpu.VMEM((total, TD), BF),
            pltpu.VMEM((FFD, total), BF),
            pltpu.VMEM((FFD, total), BF),
            pltpu.VMEM((FFD, total), BF),
            pltpu.VMEM((total, FFD), BF),
            pltpu.VMEM((GROWS, TD), F32),
            pltpu.VMEM((GROWS, TD), BF),
            pltpu.VMEM((NX, 2, A_PART, TD), BF),
            pltpu.VMEM((6, A_PART, TD), BF),
            pltpu.VMEM((2, A_PART, TD), BF),
            pltpu.VMEM((A_PART, TD), BF),
            pltpu.VMEM((A_PART, TD), BF),
            pltpu.VMEM((NX * B_PART, TD), BF),
            pltpu.VMEM((NX * B_PART, TD), BF),
            pltpu.VMEM((NX, B_PART, TD), F32),
            pltpu.VMEM((NX, B_PART, TD), BF),
            pltpu.VMEM((6, B_HALF[0], TD), BF),
            pltpu.VMEM((2, B_HALF[0], TD), BF),
            pltpu.VMEM((2, NZ, 2, SLOTS, TD), BF),
            pltpu.VMEM((NZ, 2, SLOTS, TD), BF),
            pltpu.VMEM((14, SLOTS, TD), BF),
            pltpu.VMEM((14, SLOTS, TD), BF),
            pltpu.VMEM((SLOTS, TD), BF),
            pltpu.VMEM((SLOTS, TD), BF),
            pltpu.SemaphoreType.DMA((64,)),
            pltpu.SemaphoreType.DMA((64,)),
            pltpu.SemaphoreType.DMA((4,)),
        ],
        compiler_params=pltpu.CompilerParams(
            collective_id=2, has_side_effects=True, vmem_limit_bytes=48 << 20
        ),
    )(rows, cots, own, turn_start, turn_len, gate_w, up_w, down_w)


def shards(
    queries,
    keys,
    values,
    segment_ids,
    turn_start,
    turn_len,
    w_proj,
    gain,
    gate_w,
    up_w,
    down_w,
    cotangent,
):
    context, own_rows, rows_all, cot_all = attend_call(
        queries, keys, values, segment_ids, turn_start, turn_len, w_proj, gain[None], cotangent
    )
    rows_all = rows_all.reshape(NZ * 4 * SLOTS, TD)
    cot_all = cot_all.reshape(NZ * 4 * SLOTS, TD)
    talker_out, grads = talk_call(
        rows_all, cot_all, own_rows, turn_start, turn_len, gate_w, up_w, down_w
    )
    grad_down, grad_gate, grad_up = (
        grads[n * FFD : (n + 1) * FFD].astype(F32) for n in range(3)
    )
    return (context, talker_out, grad_gate, grad_up, grad_down)


def solution(mesh):
    in_specs = (
        P("grp", "ctx", None),
        P("grp", "ctx", None),
        P("grp", "ctx", None),
        P("grp", "ctx"),
        P("grp", None),
        P("grp", None),
        P(),
        P(),
        P("ctx", None),
        P("ctx", None),
        P("ctx", None),
        P("grp", "ctx", None),
    )
    out_specs = (
        P("grp", "ctx", None),
        P("grp", "ctx", None),
        P("ctx", None),
        P("ctx", None),
        P("ctx", None),
    )
    return jax.shard_map(shards, mesh=mesh, in_specs=in_specs, out_specs=out_specs, check_vma=False)
```

```python
import math

import jax
import jax.numpy as jnp
from jax import lax
from jax.experimental import pallas as pl
from jax.experimental.pallas import tpu as pltpu
from jax.sharding import PartitionSpec as P

HEADS = 14
KV_HEADS = 2
GROUP = HEADS // KV_HEADS
D = 128
TOK = 128
TD = 896
QW = HEADS * D
KW = KV_HEADS * D
SLOTS = 48
NZ = 8
NX = 4
FFD = 296
GROWS = 896
A_ROWS = 512
A_PART = 64
B_PART = 48
B_HALF = (32, 16)
AUX = 16
CHUNK = 256
KROWS = TOK + AUX
NEG = -1e30
MESH = pl.DeviceIdType.MESH
BF = jnp.bfloat16
F32 = jnp.float32
NT = (((1,), (1,)), ((), ()))
VMEM_LIMIT = 63 << 20


class Net:
    def __init__(self, send_sems, recv_sems):
        c = lax.axis_index("ctx")
        g = lax.axis_index("grp")
        self.ctx = c
        self.z = c // 4
        self.r = c % 4
        self.y = self.r // 2
        self.k = self.r % 2
        self.x = g // 2
        self.h = g % 2
        self.send_sems = send_sems
        self.recv_sems = recv_sems
        self.ids = {}
        self.sent = []

    def zmod(self, d):
        return lax.rem(self.z + d + NZ, NZ)

    def xmod(self, d):
        return lax.rem(self.x + d + NX, NX)

    def dev(self, where):
        z, y, k, x, h = self.z, self.y, self.k, self.x, self.h
        if where == "+":
            z = self.zmod(1)
        elif where == "-":
            z = self.zmod(-1)
        elif where == "y":
            y = 1 - y
        elif where == "c":
            k = 1 - k
        elif where == "x+":
            x = self.xmod(1)
        elif where == "x-":
            x = self.xmod(-1)
        elif where == "h":
            h = 1 - h
        return (z * 4 + y * 2 + k, x * 2 + h)

    def greet(self, barrier, places):
        for where in places:
            pl.semaphore_signal(
                barrier, inc=1, device_id=self.dev(where), device_id_type=MESH
            )

    def copy(self, key, src, dst, where):
        n = self.ids.setdefault(key, len(self.ids))
        return pltpu.make_async_remote_copy(
            src_ref=src,
            dst_ref=dst,
            send_sem=self.send_sems.at[n],
            recv_sem=self.recv_sems.at[n],
            device_id=self.dev(where),
            device_id_type=MESH,
        )

    def send(self, key, src, where, dst=None):
        copy = self.copy(key, src, src if dst is None else dst, where)
        copy.start()
        self.sent.append(copy)

    def recv(self, key, ref, where):
        self.copy(key, ref, ref, where).wait_recv()

    def drain(self):
        for copy in self.sent:
            copy.wait_send()
        self.sent = []


class Gather:
    def __init__(self, net, name, buf, early, size):
        self.net, self.name, self.buf, self.early, self.size = net, name, buf, early, size

    def slot(self, d, lane, other_core=False):
        net = self.net
        y = net.y if lane == "o" else 1 - net.y
        k = 1 - net.k if other_core else net.k
        return self.buf.at[net.zmod(d), pl.ds(pl.multiple_of((y * 2 + k) * self.size, 16), self.size)]

    def limit(self, way, lane):
        return 4 if (way == "+") == (lane == "o") else 3

    def to_core(self, d, lane):
        self.net.send((self.name, "c", d, lane), self.slot(d, lane), "c")

    def to_z(self, way, lane, step):
        d = -(step - 1) if way == "+" else step - 1
        self.net.send((self.name, way, lane, step), self.slot(d, lane), way)

    def to_y(self, d):
        self.net.send((self.name, "y", d), self.slot(d, "o"), "y")

    def start(self):
        if self.early:
            self.to_y(0)
        self.to_z("+", "o", 1)
        self.to_z("-", "o", 1)
        if not self.early:
            self.to_y(0)
        self.to_core(0, "o")

    def cross(self, d):
        self.net.recv((self.name, "y", d), self.slot(d, "x"), "y")
        if self.early:
            self.to_z("+", "x", 1)
            self.to_z("-", "x", 1)
        self.to_core(d, "x")

    def arrive(self, way, lane, step):
        top = self.limit(way, lane)
        if step > top:
            return
        d = -step if way == "+" else step
        if d == -4:
            d = 4
        self.net.recv((self.name, way, lane, step), self.slot(d, lane), way)
        if step < top:
            self.to_z(way, lane, step + 1)
        if not self.early:
            self.to_y(d)
        self.to_core(d, lane)

    def ring(self, step, lanes):
        for lane in lanes:
            for way in ("+", "-"):
                self.arrive(way, lane, step)

    def crosses(self, step):
        if not self.early:
            for d in around(step):
                self.cross(d)

    def from_core(self, d):
        for lane in ("o", "x"):
            self.net.recv(
                (self.name, "c", d, lane), self.slot(d, lane, other_core=True), "c"
            )


def around(step):
    if step == 0:
        return (0,)
    if step == 4:
        return (4,)
    return (-step, step)


class GradSum:
    def __init__(self, net, g32, res, sa, ra, sa3, sah, rah, sb, rb, b32, sbx, rbx, sb3):
        self.net, self.g32, self.res = net, g32, res
        self.sa, self.ra, self.sa3, self.sah, self.rah = sa, ra, sa3, sah, rah
        self.sb, self.rb, self.b32, self.sbx, self.rbx, self.sb3 = sb, rb, b32, sbx, rbx, sb3

    def a_rows(self, x, h, count=1):
        return pl.ds(pl.multiple_of((x * 2 + h) * A_PART, A_PART), count * A_PART)

    def b_rows(self, h, x, half=None):
        at = A_ROWS + (h * NX + x) * B_PART
        size = B_PART
        if half is not None:
            at, size = at + half * B_HALF[0], B_HALF[half]
        return pl.ds(pl.multiple_of(at, 16), size)

    def b_send(self):
        net = self.net
        self.sb[...] = self.g32[
            pl.ds(pl.multiple_of(A_ROWS + (1 - net.h) * NX * B_PART, 16), NX * B_PART)
        ].astype(BF)
        net.send("b0", self.sb, "h", self.rb)

    def a_start(self):
        net = self.net
        for i in range(NX):
            for h in range(2):
                at = (i * 2 + h) * A_PART
                self.sa[i, h] = self.g32[at : at + A_PART].astype(BF)
        far = net.xmod(2)
        net.send("a1+", self.sa.at[far, 0], "x+", self.ra.at[0])
        net.send("a1-", self.sa.at[far, 1], "x-", self.ra.at[1])
        net.send("a2+", self.sa.at[net.xmod(1), 1], "x+", self.ra.at[2])
        net.send("a2-", self.sa.at[net.xmod(-1), 0], "x-", self.ra.at[3])

    def a_pass(self):
        net = self.net
        for n, (way, d, half) in enumerate((("+", 1, 0), ("-", -1, 1))):
            net.recv("a1" + way, self.ra.at[n], "x" + way)
            own = self.g32[self.a_rows(net.xmod(d), half)]
            self.sa3[n] = (own + self.ra[n].astype(F32)).astype(BF)
            net.send("a3" + way, self.sa3.at[n], "x" + way, self.ra.at[4 + n])

    def a_cross(self):
        net = self.net
        net.recv("a2+", self.ra.at[2], "x+")
        net.recv("a2-", self.ra.at[3], "x-")
        net.recv("a3+", self.ra.at[4], "x+")
        net.recv("a3-", self.ra.at[5], "x-")
        for half, (one, two) in enumerate(((3, 4), (2, 5))):
            rows = self.a_rows(net.x, half)
            self.g32[rows] = self.g32[rows] + self.ra[one].astype(F32) + self.ra[two].astype(F32)
        self.sah[...] = self.g32[self.a_rows(net.x, 1 - net.h)].astype(BF)
        net.send("ah", self.sah, "h", self.rah)

    def a_final(self):
        net = self.net
        net.recv("ah", self.rah, "h")
        rows = self.a_rows(net.x, net.h)
        self.res[rows] = (self.g32[rows] + self.rah[...].astype(F32)).astype(BF)
        for key, where in (("e0", "h"), ("e1+", "x+"), ("e1-", "x-")):
            net.send(key, self.res.at[rows], where)

    def a_spread(self):
        net = self.net
        rows = self.res.at[self.a_rows(net.x, 1 - net.h)]
        net.recv("e0", rows, "h")
        net.send("e2+", rows, "x+")
        net.send("e2-", rows, "x-")

    def a_forward(self):
        net = self.net
        for way, d, half in (("+", -1, 0), ("-", 1, 1)):
            x = net.xmod(d)
            net.recv("e1" + way, self.res.at[self.a_rows(x, net.h)], "x" + way)
            net.recv("e2" + way, self.res.at[self.a_rows(x, 1 - net.h)], "x" + way)
            net.send("f" + way, self.res.at[self.a_rows(x, half)], "x" + way)

    def a_end(self):
        net = self.net
        for way, half in (("+", 0), ("-", 1)):
            net.recv("f" + way, self.res.at[self.a_rows(net.xmod(2), half)], "x" + way)

    def b_half(self, half):
        return pl.ds(0 if half == 0 else B_HALF[0], B_HALF[half])

    def b_start(self):
        net = self.net
        net.recv("b0", self.rb, "h")
        for i in range(NX):
            at = slice(i * B_PART, (i + 1) * B_PART)
            own = self.g32[self.b_rows(net.h, i)]
            total = own + self.rb[at].astype(F32)
            self.b32[i] = total
            self.sbx[i] = total.astype(BF)
        for n, (key, way, d, half) in enumerate(
            (("b1+", "+", 2, 0), ("b1-", "-", 2, 1), ("b2+", "+", 1, 1), ("b2-", "-", -1, 0))
        ):
            net.send(
                key,
                self.sbx.at[net.xmod(d), self.b_half(half)],
                "x" + way,
                self.rbx.at[n, pl.ds(0, B_HALF[half])],
            )

    def b_pass(self):
        net = self.net
        for n, (way, d, half) in enumerate((("+", 1, 0), ("-", -1, 1))):
            size = B_HALF[half]
            net.recv("b1" + way, self.rbx.at[n, pl.ds(0, size)], "x" + way)
            own = self.b32[net.xmod(d), self.b_half(half)]
            self.sb3[n, 0:size] = (own + self.rbx[n, 0:size].astype(F32)).astype(BF)
            net.send(
                "b3" + way,
                self.sb3.at[n, pl.ds(0, size)],
                "x" + way,
                self.rbx.at[4 + n, pl.ds(0, size)],
            )

    def b_final(self):
        net = self.net
        net.recv("b2+", self.rbx.at[2, pl.ds(0, B_HALF[1])], "x+")
        net.recv("b2-", self.rbx.at[3, pl.ds(0, B_HALF[0])], "x-")
        net.recv("b3+", self.rbx.at[4, pl.ds(0, B_HALF[0])], "x+")
        net.recv("b3-", self.rbx.at[5, pl.ds(0, B_HALF[1])], "x-")
        for half, (one, two) in enumerate(((3, 4), (2, 5))):
            size = B_HALF[half]
            total = (
                self.b32[net.x, self.b_half(half)]
                + self.rbx[one, 0:size].astype(F32)
                + self.rbx[two, 0:size].astype(F32)
            )
            self.res[self.b_rows(net.h, net.x, half)] = total.astype(BF)
        rows = self.res.at[self.b_rows(net.h, net.x)]
        for key, where in (("q+", "x+"), ("q-", "x-"), ("p0", "h")):
            net.send(key, rows, where)

    def b_forward(self):
        net = self.net
        for n, (way, d, half) in enumerate((("+", -1, 0), ("-", 1, 1))):
            x = net.xmod(d)
            rows = self.res.at[self.b_rows(net.h, x)]
            net.recv("q" + way, rows, "x" + way)
            net.send("s" + way, self.res.at[self.b_rows(net.h, x, half)], "x" + way)
            net.send("p%d" % (n + 1), rows, "h")

    def b_cross(self):
        net = self.net
        x = net.xmod(2)
        for way, half in (("+", 0), ("-", 1)):
            net.recv("s" + way, self.res.at[self.b_rows(net.h, x, half)], "x" + way)
        net.send("p3", self.res.at[self.b_rows(net.h, x)], "h")

    def b_end(self):
        net = self.net
        for n, d in enumerate((0, -1, 1, 2)):
            net.recv("p%d" % n, self.res.at[self.b_rows(1 - net.h, net.xmod(d))], "h")


class RowSum:
    def __init__(self, net, part, from_core, stage, land, ys, yr):
        self.net, self.part, self.from_core = net, part, from_core
        self.stage, self.land, self.ys, self.yr = stage, land, ys, yr
        self.at = {}
        for way in ("+", "-"):
            for lane in ("o", "x"):
                for step in range(1, self.limit(way, lane) + 1):
                    self.at[way, lane, step] = len(self.at)

    def limit(self, way, lane):
        return 4 if (way == "+") == (lane == "o") else 3

    def swap(self, d):
        net = self.net
        z = net.zmod(d)
        net.send(("c", d), self.part.at[1 - net.k, z], "c", self.from_core.at[z])

    def swapped(self, d):
        self.net.recv(("c", d), self.from_core.at[self.net.zmod(d)], "c")

    def own(self, d, lane):
        net = self.net
        z = net.zmod(d)
        y = net.y if lane == "o" else 1 - net.y
        return self.part[net.k, z, y].astype(F32) + self.from_core[z, y].astype(F32)

    def landed(self, way, lane, step):
        n = self.at[way, lane, step]
        self.net.recv(("z", way, lane, step), self.land.at[n], way)
        return self.land[n].astype(F32)

    def step(self, step):
        for lane in ("o", "x"):
            for way in ("+", "-"):
                top = self.limit(way, lane)
                if step > top:
                    continue
                left = top - step + 1
                d = left if way == "+" or left == 4 else -left
                total = self.own(d, lane)
                if step > 1:
                    total = total + self.landed(way, lane, step - 1)
                n = self.at[way, lane, step]
                self.stage[n] = total.astype(BF)
                self.net.send(("z", way, lane, step), self.stage.at[n], way, self.land.at[n])

    def across(self):
        total = self.own(0, "x")
        for way in ("+", "-"):
            total = total + self.landed(way, "x", self.limit(way, "x"))
        self.ys[...] = total.astype(BF)
        self.net.send("y", self.ys, "y", self.yr)

    def result(self):
        total = self.own(0, "o")
        for way in ("+", "-"):
            total = total + self.landed(way, "o", self.limit(way, "o"))
        self.net.recv("y", self.yr, "y")
        return total + self.yr[...].astype(F32)


def kernel(
    q_hbm,
    k_hbm,
    v_hbm,
    seg_hbm,
    start_hbm,
    len_hbm,
    w_hbm,
    gain_hbm,
    gate_hbm,
    up_hbm,
    down_hbm,
    cot_hbm,
    ctx_out,
    talker_out,
    grads_out,
    gk,
    gv,
    gr,
    gc,
    q_raw,
    q_buf,
    ctx_buf,
    w_buf,
    cot_buf,
    seg_buf,
    start_buf,
    len_buf,
    gain_buf,
    gate_w,
    up_w,
    down_w,
    segq,
    bias,
    m_buf,
    acc_buf,
    own_buf,
    out_buf,
    hid,
    d_gate,
    d_up,
    hid_rows,
    g32,
    res,
    sa,
    ra,
    sa3,
    sah,
    rah,
    sb,
    rb,
    b32,
    sbx,
    rbx,
    sb3,
    part,
    from_core,
    stage,
    land,
    ys,
    yr,
    send_sems,
    recv_sems,
    local_sems,
):
    net = Net(send_sems, recv_sems)
    z, r = net.z, net.r

    def load(n, src, dst):
        copy = pltpu.make_async_copy(src, dst, local_sems.at[n])
        copy.start()
        return copy

    at_k = pl.ds(pl.multiple_of(r * KROWS, 16), TOK)
    at_aux = pl.ds(pl.multiple_of(r * KROWS + TOK, 16), AUX)
    at_v = pl.ds(pl.multiple_of(r * TOK, 16), TOK)
    at_row = pl.ds(pl.multiple_of(r * SLOTS, 16), SLOTS)
    load_seg = load(0, seg_hbm, seg_buf)
    load_k = load(1, k_hbm.at[0], gk.at[z, at_k])
    load_v = load(2, v_hbm.at[0], gv.at[z, at_v])
    load_q = load(3, q_hbm.at[0], q_raw)
    load_start = load(4, start_hbm, start_buf)
    load_len = load(5, len_hbm, len_buf)
    load_cot = load(6, cot_hbm.at[0], cot_buf)
    load_w = load(7, w_hbm, w_buf)
    load_gain = load(8, gain_hbm, gain_buf)
    load_ffn = [
        load(9, gate_hbm, gate_w),
        load(10, up_hbm, up_w),
        load(11, down_hbm, down_w),
    ]

    barrier = pltpu.get_barrier_semaphore()
    places = ("+", "-", "y", "c", "x+", "x-", "h")
    net.greet(barrier, places)

    load_seg.wait()
    seg_row = seg_buf[...].astype(F32)
    gk[z, at_aux, 0:D] = jnp.broadcast_to(seg_row, (AUX, D)).astype(BF)
    gk[z, at_aux, D : 2 * D] = jnp.zeros((AUX, D), BF)

    keys = Gather(net, "k", gk, True, KROWS)
    vals = Gather(net, "v", gv, False, TOK)
    rows = Gather(net, "r", gr, True, SLOTS)
    cots = Gather(net, "g", gc, False, SLOTS)

    load_k.wait()
    load_v.wait()
    pl.semaphore_wait(barrier, len(places))
    keys.start()
    vals.start()

    segq[...] = jnp.transpose(jnp.broadcast_to(seg_row, (TOK, D)))
    m_buf[...] = jnp.full(m_buf.shape, NEG, F32)
    acc_buf[...] = jnp.zeros(acc_buf.shape, F32)
    load_q.wait()
    for h in range(HEADS):
        q_buf[h] = q_raw[:, h * D : (h + 1) * D]

    load_start.wait()
    load_len.wait()
    start = start_buf[0, net.ctx] - net.ctx * TOK
    length = len_buf[0, net.ctx]
    slot_id = lax.broadcasted_iota(jnp.int32, (SLOTS, TOK), 0)
    place = lax.broadcasted_iota(jnp.int32, (SLOTS, TOK), 1)
    packer = jnp.where((place - start == slot_id) & (slot_id < length), 1.0, 0.0).astype(BF)
    load_cot.wait()
    gc[z, at_row] = jnp.dot(packer, cot_buf[...], preferred_element_type=F32).astype(BF)
    for i in range(NZ):
        for buf in (gr, gc):
            buf[i, 4 * SLOTS :] = jnp.zeros((CHUNK - 4 * SLOTS, TD), BF)

    factor = math.log2(math.e) / math.sqrt(D)

    def attend(d):
        zc = net.zmod(d)

        def work():
            for b in range(4):
                aux = b * KROWS + TOK
                ok = segq[...] == gk[zc, aux : aux + AUX, 0:D].astype(F32)[0:1]
                if d == 0:
                    kpos = lax.broadcasted_iota(jnp.int32, (TOK, D), 1) + (b - r) * TOK
                    qpos = lax.broadcasted_iota(jnp.int32, (TOK, D), 0)
                    ok = ok & (kpos <= qpos)
                bias[:, b * TOK : (b + 1) * TOK] = jnp.where(ok, 0.0, NEG)

            def head(i, carry):
                for kv in range(KV_HEADS):
                    h = i + kv * GROUP
                    lanes = slice(kv * D, (kv + 1) * D)
                    kc = jnp.concatenate(
                        [gk[zc, b * KROWS : b * KROWS + TOK, lanes] for b in range(4)], axis=0
                    )
                    vc = jnp.concatenate([gv[zc, :, lanes], jnp.ones((4 * TOK, D), BF)], axis=1)
                    s = lax.dot_general(q_buf[h], kc, NT, preferred_element_type=F32)
                    s = s * factor + bias[...]
                    m_old = m_buf[h]
                    m_new = jnp.maximum(m_old, jnp.max(s, axis=1, keepdims=True))
                    p = jnp.exp2(s - jnp.concatenate([m_new] * 4, axis=1)).astype(BF)
                    alpha = jnp.exp2(m_old - m_new)
                    m_buf[h] = m_new
                    acc_buf[h] = acc_buf[h] * jnp.concatenate([alpha, alpha], axis=1) + jnp.dot(
                        p, vc, preferred_element_type=F32
                    )
                return carry

            lax.fori_loop(0, GROUP, head, 0)

        if d == 0:
            work()
        else:
            pl.when(zc < z)(work)

    def attend_step(step):
        for d in around(step):
            keys.from_core(d)
            vals.from_core(d)
            attend(d)

    vals.crosses(0)
    keys.cross(0)
    for step in range(1, 5):
        keys.ring(step, "o")
        vals.ring(step, "o")
        keys.ring(step, "x")
        if step == 3:
            cots.start()
        if step == 4:
            cots.ring(1, "o")
            cots.crosses(0)
        attend_step(step - 1)
        vals.crosses(step)
    cots.ring(2, "o")
    cots.crosses(1)
    attend_step(4)

    for h in range(HEADS):
        acc = acc_buf[h]
        ctx_buf[:, h * D : (h + 1) * D] = (acc[:, 0:D] / acc[:, D : 2 * D]).astype(BF)
    load_w.wait()
    load_gain.wait()
    packed = jnp.dot(packer, ctx_buf[...], preferred_element_type=F32).astype(BF)
    own = jnp.dot(packed, w_buf[...], preferred_element_type=F32).astype(BF)
    own_buf[...] = own
    own = own.astype(F32)
    scale = lax.rsqrt(jnp.mean(own * own, axis=-1, keepdims=True) + 1e-06)
    gr[z, at_row] = (own * scale * gain_buf[...]).astype(BF)

    rows.start()
    save_ctx = load(12, ctx_buf, ctx_out.at[0])
    for wait in load_ffn:
        wait.wait()

    def ffn_in(d):
        rows.from_core(d)
        cots.from_core(d)
        zc = net.zmod(d)
        at = pl.ds(pl.multiple_of(zc * CHUNK, CHUNK), CHUNK)
        row = gr[zc]
        gate = lax.dot_general(gate_w[...], row, NT, preferred_element_type=F32)
        up = lax.dot_general(up_w[...], row, NT, preferred_element_type=F32)
        d_hidden = lax.dot_general(down_w[...], gc[zc], NT, preferred_element_type=F32)
        sig = jax.nn.sigmoid(gate)
        act = gate * sig
        hidden = act * up
        hid[:, at] = hidden.astype(BF)
        hid_rows[zc] = jnp.transpose(hidden).astype(BF)
        d_gate[:, at] = (d_hidden * up * sig * (1.0 + gate * (1.0 - sig))).astype(BF)
        d_up[:, at] = (d_hidden * act).astype(BF)

    cots.ring(3, "o")
    cots.crosses(2)
    rows.cross(0)
    cots.ring(4, "o")
    cots.crosses(3)
    rows.ring(1, "ox")
    ffn_in(0)
    rows.ring(2, "ox")
    cots.crosses(4)
    for step in (1, 2, 3):
        if step < 3:
            rows.ring(step + 2, "ox")
        for d in around(step):
            ffn_in(d)
    ffn_in(4)

    grads = GradSum(net, g32, res, sa, ra, sa3, sah, rah, sb, rb, b32, sbx, rbx, sb3)
    sums = RowSum(net, part, from_core, stage, land, ys, yr)

    def grad(n, left, right):
        g32[n * FFD : (n + 1) * FFD] = jnp.dot(
            left[...], right[...].reshape(NZ * CHUNK, TD), preferred_element_type=F32
        )

    g32[3 * FFD :] = jnp.zeros((GROWS - 3 * FFD, TD), F32)
    grad(0, hid, gc)
    grad(1, d_gate, gr)
    grads.a_start()
    grad(2, d_up, gr)
    grads.b_send()

    def ffn_out(d):
        zc = net.zmod(d)
        total = jnp.dot(
            hid_rows[zc, 0 : 4 * SLOTS], down_w[...], preferred_element_type=F32
        ).astype(BF)
        for b in range(4):
            part[b % 2, zc, b // 2] = total[b * SLOTS : (b + 1) * SLOTS]
        sums.swap(d)

    for d in (4, 3, -3):
        ffn_out(d)
    grads.a_pass()
    for d in (2, -2):
        ffn_out(d)
    for d in (4, 3, -3):
        sums.swapped(d)
    sums.step(1)
    for d in (1, -1, 0):
        ffn_out(d)
    grads.b_start()
    for d in (2, -2):
        sums.swapped(d)
    sums.step(2)
    grads.a_cross()
    for d in (1, -1, 0):
        sums.swapped(d)
    sums.step(3)
    grads.b_pass()
    grads.a_final()
    sums.step(4)
    grads.b_final()
    grads.a_spread()
    sums.across()
    grads.b_forward()
    grads.a_forward()
    grads.b_cross()

    place = lax.broadcasted_iota(jnp.int32, (TOK, SLOTS), 0)
    slot_id = lax.broadcasted_iota(jnp.int32, (TOK, SLOTS), 1)
    spread = jnp.where((place - start == slot_id) & (slot_id < length), 1.0, 0.0).astype(BF)
    out_rows = (own_buf[...].astype(F32) + sums.result()).astype(BF)
    out_buf[...] = jnp.dot(spread, out_rows, preferred_element_type=F32).astype(BF)
    save_out = load(13, out_buf, talker_out.at[0])

    grads.a_end()
    grads.b_end()
    save_grads = load(14, res, grads_out)
    net.drain()
    for save in (save_ctx, save_out, save_grads):
        save.wait()


def fused(*args):
    hbm = pl.BlockSpec(memory_space=pl.ANY)
    scratch = (
        ((NZ, 4 * KROWS, KW), BF),
        ((NZ, 4 * TOK, KW), BF),
        ((NZ, CHUNK, TD), BF),
        ((NZ, CHUNK, TD), BF),
        ((TOK, QW), BF),
        ((HEADS, TOK, D), BF),
        ((TOK, QW), BF),
        ((QW, TD), BF),
        ((TOK, TD), BF),
        ((1, TOK), jnp.int32),
        pltpu.SMEM((1, 32), jnp.int32),
        pltpu.SMEM((1, 32), jnp.int32),
        ((TD,), F32),
        ((FFD, TD), BF),
        ((FFD, TD), BF),
        ((FFD, TD), BF),
        ((TOK, D), F32),
        ((TOK, 4 * TOK), F32),
        ((HEADS, TOK, D), F32),
        ((HEADS, TOK, 2 * D), F32),
        ((SLOTS, TD), BF),
        ((TOK, TD), BF),
        ((FFD, NZ * CHUNK), BF),
        ((FFD, NZ * CHUNK), BF),
        ((FFD, NZ * CHUNK), BF),
        ((NZ, CHUNK, FFD), BF),
        ((GROWS, TD), F32),
        ((GROWS, TD), BF),
        ((NX, 2, A_PART, TD), BF),
        ((6, A_PART, TD), BF),
        ((2, A_PART, TD), BF),
        ((A_PART, TD), BF),
        ((A_PART, TD), BF),
        ((NX * B_PART, TD), BF),
        ((NX * B_PART, TD), BF),
        ((NX, B_PART, TD), F32),
        ((NX, B_PART, TD), BF),
        ((6, B_HALF[0], TD), BF),
        ((2, B_HALF[0], TD), BF),
        ((2, NZ, 2, SLOTS, TD), BF),
        ((NZ, 2, SLOTS, TD), BF),
        ((14, SLOTS, TD), BF),
        ((14, SLOTS, TD), BF),
        ((SLOTS, TD), BF),
        ((SLOTS, TD), BF),
        pltpu.SemaphoreType.DMA((192,)),
        pltpu.SemaphoreType.DMA((192,)),
        pltpu.SemaphoreType.DMA((16,)),
    )
    return pl.pallas_call(
        kernel,
        name="mega",
        out_shape=[
            jax.ShapeDtypeStruct((1, TOK, QW), BF),
            jax.ShapeDtypeStruct((1, TOK, TD), BF),
            jax.ShapeDtypeStruct((GROWS, TD), BF),
        ],
        in_specs=[hbm] * len(args),
        out_specs=[hbm] * 3,
        scratch_shapes=[pltpu.VMEM(*s) if isinstance(s, tuple) else s for s in scratch],
        compiler_params=pltpu.CompilerParams(
            collective_id=1, has_side_effects=True, vmem_limit_bytes=VMEM_LIMIT
        ),
    )(*args)


def shards(*args):
    context, talker_out, grads = fused(*args)
    grad_down, grad_gate, grad_up = (
        grads[n * FFD : (n + 1) * FFD].astype(F32) for n in range(3)
    )
    return (context, talker_out, grad_gate, grad_up, grad_down)


def solution(mesh):
    in_specs = (
        P("grp", "ctx", None),
        P("grp", "ctx", None),
        P("grp", "ctx", None),
        P("grp", "ctx"),
        P("grp", None),
        P("grp", None),
        P(),
        P(),
        P("ctx", None),
        P("ctx", None),
        P("ctx", None),
        P("grp", "ctx", None),
    )
    out_specs = (
        P("grp", "ctx", None),
        P("grp", "ctx", None),
        P("ctx", None),
        P("ctx", None),
        P("ctx", None),
    )
    return jax.shard_map(shards, mesh=mesh, in_specs=in_specs, out_specs=out_specs, check_vma=False)
```

```python
import math

import jax
import jax.numpy as jnp
from jax import lax
from jax.experimental import pallas as pl
from jax.experimental.pallas import tpu as pltpu
from jax.sharding import PartitionSpec as P

HEADS = 14
KV_HEADS = 2
GROUP = HEADS // KV_HEADS
D = 128
TOK = 128
TD = 896
QW = HEADS * D
KW = KV_HEADS * D
SLOTS = 48
NZ = 8
NX = 4
FFD = 296
GROWS = 896
AUX = 16
CHUNK = 256
KROWS = TOK + AUX
NEG = -1e30
MESH = pl.DeviceIdType.MESH
BF = jnp.bfloat16
F32 = jnp.float32
NT = (((1,), (1,)), ((), ()))
VMEM_LIMIT = 63 << 20


class Net:
    def __init__(self, send_sems, recv_sems):
        c = lax.axis_index("ctx")
        g = lax.axis_index("grp")
        self.ctx = c
        self.z = c // 4
        self.r = c % 4
        self.y = self.r // 2
        self.k = self.r % 2
        self.x = g // 2
        self.h = g % 2
        self.send_sems = send_sems
        self.recv_sems = recv_sems
        self.ids = {}
        self.sent = []

    def zmod(self, d):
        return lax.rem(self.z + d + NZ, NZ)

    def xmod(self, d):
        return lax.rem(self.x + d + NX, NX)

    def dev(self, where):
        z, y, k, x, h = self.z, self.y, self.k, self.x, self.h
        if where == "+":
            z = self.zmod(1)
        elif where == "-":
            z = self.zmod(-1)
        elif where == "y":
            y = 1 - y
        elif where == "c":
            k = 1 - k
        elif where == "x+":
            x = self.xmod(1)
        elif where == "x-":
            x = self.xmod(-1)
        elif where == "h":
            h = 1 - h
        return (z * 4 + y * 2 + k, x * 2 + h)

    def greet(self, barrier, places):
        for where in places:
            pl.semaphore_signal(
                barrier, inc=1, device_id=self.dev(where), device_id_type=MESH
            )

    def copy(self, key, src, dst, where):
        n = self.ids.setdefault(key, len(self.ids))
        return pltpu.make_async_remote_copy(
            src_ref=src,
            dst_ref=dst,
            send_sem=self.send_sems.at[n],
            recv_sem=self.recv_sems.at[n],
            device_id=self.dev(where),
            device_id_type=MESH,
        )

    def send(self, key, src, where, dst=None):
        copy = self.copy(key, src, src if dst is None else dst, where)
        copy.start()
        self.sent.append(copy)

    def recv(self, key, ref, where):
        self.copy(key, ref, ref, where).wait_recv()

    def drain(self):
        for copy in self.sent:
            copy.wait_send()
        self.sent = []


class Gather:
    def __init__(self, net, name, buf, early, size):
        self.net, self.name, self.buf, self.early, self.size = net, name, buf, early, size

    def slot(self, d, lane, other_core=False):
        net = self.net
        y = net.y if lane == "o" else 1 - net.y
        k = 1 - net.k if other_core else net.k
        return self.buf.at[net.zmod(d), pl.ds(pl.multiple_of((y * 2 + k) * self.size, 16), self.size)]

    def limit(self, way, lane):
        return 4 if (way == "+") == (lane == "o") else 3

    def to_core(self, d, lane):
        self.net.send((self.name, "c", d, lane), self.slot(d, lane), "c")

    def to_z(self, way, lane, step):
        d = -(step - 1) if way == "+" else step - 1
        self.net.send((self.name, way, lane, step), self.slot(d, lane), way)

    def to_y(self, d):
        self.net.send((self.name, "y", d), self.slot(d, "o"), "y")

    def start(self):
        if self.early:
            self.to_y(0)
        self.to_z("+", "o", 1)
        self.to_z("-", "o", 1)
        if not self.early:
            self.to_y(0)
        self.to_core(0, "o")

    def cross(self, d):
        self.net.recv((self.name, "y", d), self.slot(d, "x"), "y")
        if self.early:
            self.to_z("+", "x", 1)
            self.to_z("-", "x", 1)
        self.to_core(d, "x")

    def arrive(self, way, lane, step):
        top = self.limit(way, lane)
        if step > top:
            return
        d = -step if way == "+" else step
        if d == -4:
            d = 4
        self.net.recv((self.name, way, lane, step), self.slot(d, lane), way)
        if step < top:
            self.to_z(way, lane, step + 1)
        if not self.early:
            self.to_y(d)
        self.to_core(d, lane)

    def ring(self, step, lanes):
        for lane in lanes:
            for way in ("+", "-"):
                self.arrive(way, lane, step)

    def crosses(self, step):
        if not self.early:
            for d in around(step):
                self.cross(d)

    def from_core(self, d):
        for lane in ("o", "x"):
            self.net.recv(
                (self.name, "c", d, lane), self.slot(d, lane, other_core=True), "c"
            )


def around(step):
    if step == 0:
        return (0,)
    if step == 4:
        return (4,)
    return (-step, step)


class GradSum:
    def __init__(self, net, name, g32, res, base, size, refs):
        self.net, self.name, self.g32, self.res = net, name, g32, res
        self.base, self.size = base, size
        self.refs = refs

    def send(self, key, src, where, dst=None):
        self.net.send((self.name, key), src, where, dst)

    def recv(self, key, ref, where):
        self.net.recv((self.name, key), ref, where)


class XFirst(GradSum):
    def rows(self, x, h):
        return pl.ds(pl.multiple_of(self.base + (x * 2 + h) * self.size, 16), self.size)

    def start(self):
        net = self.net
        first, land = self.refs[:2]
        for i in range(NX):
            for h in range(2):
                at = self.base + (i * 2 + h) * self.size
                first[i, h] = self.g32[at : at + self.size].astype(BF)
        far = net.xmod(2)
        self.send("1+", first.at[far, 0], "x+", land.at[0])
        self.send("1-", first.at[far, 1], "x-", land.at[1])
        self.send("2+", first.at[net.xmod(1), 1], "x+", land.at[2])
        self.send("2-", first.at[net.xmod(-1), 0], "x-", land.at[3])

    def relay(self):
        net = self.net
        land, second = self.refs[1:3]
        for n, (way, d, half) in enumerate((("+", 1, 0), ("-", -1, 1))):
            self.recv("1" + way, land.at[n], "x" + way)
            own = self.g32[self.rows(net.xmod(d), half)]
            second[n] = (own + land[n].astype(F32)).astype(BF)
            self.send("3" + way, second.at[n], "x" + way, land.at[4 + n])

    def cross(self):
        net = self.net
        land, _, over, back = self.refs[1:]
        self.recv("2+", land.at[2], "x+")
        self.recv("2-", land.at[3], "x-")
        self.recv("3+", land.at[4], "x+")
        self.recv("3-", land.at[5], "x-")
        for half, (one, two) in enumerate(((3, 4), (2, 5))):
            rows = self.rows(net.x, half)
            self.g32[rows] = self.g32[rows] + land[one].astype(F32) + land[two].astype(F32)
        over[...] = self.g32[self.rows(net.x, 1 - net.h)].astype(BF)
        self.send("h", over, "h", back)

    def final(self):
        net = self.net
        back = self.refs[4]
        self.recv("h", back, "h")
        rows = self.rows(net.x, net.h)
        self.res[rows] = (self.g32[rows] + back[...].astype(F32)).astype(BF)
        for key, where in (("e0", "h"), ("e1+", "x+"), ("e1-", "x-")):
            self.send(key, self.res.at[rows], where)

    def spread(self):
        net = self.net
        rows = self.res.at[self.rows(net.x, 1 - net.h)]
        self.recv("e0", rows, "h")
        self.send("e2+", rows, "x+")
        self.send("e2-", rows, "x-")

    def forward(self):
        net = self.net
        for way, d, half in (("+", -1, 0), ("-", 1, 1)):
            x = net.xmod(d)
            self.recv("e1" + way, self.res.at[self.rows(x, net.h)], "x" + way)
            self.recv("e2" + way, self.res.at[self.rows(x, 1 - net.h)], "x" + way)
            self.send("f" + way, self.res.at[self.rows(x, half)], "x" + way)

    def end(self):
        net = self.net
        for way, half in (("+", 0), ("-", 1)):
            self.recv("f" + way, self.res.at[self.rows(net.xmod(2), half)], "x" + way)


class HFirst(GradSum):
    def part(self, half):
        low = self.size // 32 * 16 or self.size
        return (0, low) if half == 0 else (low, self.size - low)

    def rows(self, h, x, half=None):
        at, size = (0, self.size) if half is None else self.part(half)
        return pl.ds(pl.multiple_of(self.base + (h * NX + x) * self.size + at, 16), size)

    def ways(self, plan):
        return [m for m in plan if self.part(m[-1])[1]]

    def start(self):
        net = self.net
        first, land = self.refs[:2]
        at = self.base + (1 - net.h) * NX * self.size
        first[...] = self.g32[pl.ds(pl.multiple_of(at, 16), NX * self.size)].astype(BF)
        self.send("0", first, "h", land)

    def cross(self):
        net = self.net
        back, total, second, ring = self.refs[1:5]
        self.recv("0", back, "h")
        for i in range(NX):
            rows = slice(i * self.size, (i + 1) * self.size)
            value = self.g32[self.rows(net.h, i)] + back[rows].astype(F32)
            total[i] = value
            second[i] = value.astype(BF)
        plan = ((0, "1+", "+", 2, 0), (1, "1-", "-", 2, 1), (2, "2+", "+", 1, 1), (3, "2-", "-", -1, 0))
        for n, key, way, d, half in self.ways(plan):
            at = pl.ds(*self.part(half))
            self.send(key, second.at[net.xmod(d), at], "x" + way, ring.at[n, at])

    def relay(self):
        net = self.net
        total, _, ring, third = self.refs[2:]
        for n, way, d, half in self.ways(((0, "+", 1, 0), (1, "-", -1, 1))):
            at = pl.ds(*self.part(half))
            self.recv("1" + way, ring.at[n, at], "x" + way)
            third[n, at] = (total[net.xmod(d), at] + ring[n, at].astype(F32)).astype(BF)
            self.send("3" + way, third.at[n, at], "x" + way, ring.at[4 + n, at])

    def final(self):
        net = self.net
        total, _, ring = self.refs[2:5]
        plan = ((2, "2+", "+", 1), (3, "2-", "-", 0), (4, "3+", "+", 0), (5, "3-", "-", 1))
        for n, key, way, half in self.ways(plan):
            self.recv(key, ring.at[n, pl.ds(*self.part(half))], "x" + way)
        for one, two, half in self.ways(((3, 4, 0), (2, 5, 1))):
            at = pl.ds(*self.part(half))
            value = total[net.x, at] + ring[one, at].astype(F32) + ring[two, at].astype(F32)
            self.res[self.rows(net.h, net.x, half)] = value.astype(BF)
        rows = self.res.at[self.rows(net.h, net.x)]
        for key, where in (("q+", "x+"), ("q-", "x-"), ("p0", "h")):
            self.send(key, rows, where)

    def forward(self):
        net = self.net
        for n, (way, d, half) in enumerate((("+", -1, 0), ("-", 1, 1))):
            x = net.xmod(d)
            rows = self.res.at[self.rows(net.h, x)]
            self.recv("q" + way, rows, "x" + way)
            if self.part(half)[1]:
                self.send("s" + way, self.res.at[self.rows(net.h, x, half)], "x" + way)
            self.send("p%d" % (n + 1), rows, "h")

    def spread(self):
        net = self.net
        x = net.xmod(2)
        for way, half in self.ways((("+", 0), ("-", 1))):
            self.recv("s" + way, self.res.at[self.rows(net.h, x, half)], "x" + way)
        self.send("p3", self.res.at[self.rows(net.h, x)], "h")

    def end(self):
        net = self.net
        for n, d in enumerate((0, -1, 1, 2)):
            self.recv("p%d" % n, self.res.at[self.rows(1 - net.h, net.xmod(d))], "h")


class RowSum:
    def __init__(self, net, part, from_core, stage, land, ys, yr):
        self.net, self.part, self.from_core = net, part, from_core
        self.stage, self.land, self.ys, self.yr = stage, land, ys, yr
        self.at = {}
        for way in ("+", "-"):
            for lane in ("o", "x"):
                for step in range(1, self.limit(way, lane) + 1):
                    self.at[way, lane, step] = len(self.at)

    def limit(self, way, lane):
        return 4 if (way == "+") == (lane == "o") else 3

    def swap(self, d):
        net = self.net
        z = net.zmod(d)
        net.send(("c", d), self.part.at[1 - net.k, z], "c", self.from_core.at[z])

    def swapped(self, d):
        self.net.recv(("c", d), self.from_core.at[self.net.zmod(d)], "c")

    def own(self, d, lane):
        net = self.net
        z = net.zmod(d)
        y = net.y if lane == "o" else 1 - net.y
        return self.part[net.k, z, y].astype(F32) + self.from_core[z, y].astype(F32)

    def landed(self, way, lane, step):
        n = self.at[way, lane, step]
        self.net.recv(("z", way, lane, step), self.land.at[n], way)
        return self.land[n].astype(F32)

    def step(self, step):
        for lane in ("o", "x"):
            for way in ("+", "-"):
                top = self.limit(way, lane)
                if step > top:
                    continue
                left = top - step + 1
                d = left if way == "+" or left == 4 else -left
                total = self.own(d, lane)
                if step > 1:
                    total = total + self.landed(way, lane, step - 1)
                n = self.at[way, lane, step]
                self.stage[n] = total.astype(BF)
                self.net.send(("z", way, lane, step), self.stage.at[n], way, self.land.at[n])

    def across(self):
        total = self.own(0, "x")
        for way in ("+", "-"):
            total = total + self.landed(way, "x", self.limit(way, "x"))
        self.ys[...] = total.astype(BF)
        self.net.send("y", self.ys, "y", self.yr)

    def result(self):
        total = self.own(0, "o")
        for way in ("+", "-"):
            total = total + self.landed(way, "o", self.limit(way, "o"))
        self.net.recv("y", self.yr, "y")
        return total + self.yr[...].astype(F32)


def kernel(
    q_hbm,
    k_hbm,
    v_hbm,
    seg_hbm,
    start_hbm,
    len_hbm,
    w_hbm,
    gain_hbm,
    gate_hbm,
    up_hbm,
    down_hbm,
    cot_hbm,
    ctx_out,
    talker_out,
    grads_out,
    gk,
    gv,
    gr,
    gc,
    q_raw,
    q_buf,
    ctx_buf,
    w_buf,
    cot_buf,
    seg_buf,
    start_buf,
    len_buf,
    gain_buf,
    gate_w,
    up_w,
    down_w,
    segq,
    bias,
    m_buf,
    acc_buf,
    own_buf,
    out_buf,
    hid,
    d_gate,
    d_up,
    hid_rows,
    g32,
    res,
    a1_refs,
    a2_refs,
    b1_refs,
    b2_refs,
    part,
    from_core,
    stage,
    land,
    ys,
    yr,
    send_sems,
    recv_sems,
    local_sems,
):
    net = Net(send_sems, recv_sems)
    z, r = net.z, net.r

    def load(n, src, dst):
        copy = pltpu.make_async_copy(src, dst, local_sems.at[n])
        copy.start()
        return copy

    at_k = pl.ds(pl.multiple_of(r * KROWS, 16), TOK)
    at_aux = pl.ds(pl.multiple_of(r * KROWS + TOK, 16), AUX)
    at_v = pl.ds(pl.multiple_of(r * TOK, 16), TOK)
    at_row = pl.ds(pl.multiple_of(r * SLOTS, 16), SLOTS)
    load_seg = load(0, seg_hbm, seg_buf)
    load_k = load(1, k_hbm.at[0], gk.at[z, at_k])
    load_v = load(2, v_hbm.at[0], gv.at[z, at_v])
    load_q = load(3, q_hbm.at[0], q_raw)
    load_start = load(4, start_hbm, start_buf)
    load_len = load(5, len_hbm, len_buf)
    load_cot = load(6, cot_hbm.at[0], cot_buf)
    load_w = load(7, w_hbm, w_buf)
    load_gain = load(8, gain_hbm, gain_buf)
    load_ffn = [
        load(9, gate_hbm, gate_w),
        load(10, up_hbm, up_w),
        load(11, down_hbm, down_w),
    ]

    barrier = pltpu.get_barrier_semaphore()
    places = ("+", "-", "y", "c", "x+", "x-", "h")
    net.greet(barrier, places)

    load_seg.wait()
    seg_row = seg_buf[...].astype(F32)
    gk[z, at_aux, 0:D] = jnp.broadcast_to(seg_row, (AUX, D)).astype(BF)
    gk[z, at_aux, D : 2 * D] = jnp.zeros((AUX, D), BF)

    keys = Gather(net, "k", gk, True, KROWS)
    vals = Gather(net, "v", gv, False, TOK)
    rows = Gather(net, "r", gr, True, SLOTS)
    cots = Gather(net, "g", gc, False, SLOTS)

    load_k.wait()
    load_v.wait()
    pl.semaphore_wait(barrier, len(places))
    keys.start()
    vals.start()

    segq[...] = jnp.transpose(jnp.broadcast_to(seg_row, (TOK, D)))
    m_buf[...] = jnp.full(m_buf.shape, NEG, F32)
    acc_buf[...] = jnp.zeros(acc_buf.shape, F32)
    load_q.wait()
    for h in range(HEADS):
        q_buf[h] = q_raw[:, h * D : (h + 1) * D]

    load_start.wait()
    load_len.wait()
    start = start_buf[0, net.ctx] - net.ctx * TOK
    length = len_buf[0, net.ctx]
    slot_id = lax.broadcasted_iota(jnp.int32, (SLOTS, TOK), 0)
    place = lax.broadcasted_iota(jnp.int32, (SLOTS, TOK), 1)
    packer = jnp.where((place - start == slot_id) & (slot_id < length), 1.0, 0.0).astype(BF)
    load_cot.wait()
    gc[z, at_row] = jnp.dot(packer, cot_buf[...], preferred_element_type=F32).astype(BF)
    for i in range(NZ):
        for buf in (gr, gc):
            buf[i, 4 * SLOTS :] = jnp.zeros((CHUNK - 4 * SLOTS, TD), BF)

    factor = math.log2(math.e) / math.sqrt(D)

    def attend(d):
        zc = net.zmod(d)

        def work():
            for b in range(4):
                aux = b * KROWS + TOK
                ok = segq[...] == gk[zc, aux : aux + AUX, 0:D].astype(F32)[0:1]
                if d == 0:
                    kpos = lax.broadcasted_iota(jnp.int32, (TOK, D), 1) + (b - r) * TOK
                    qpos = lax.broadcasted_iota(jnp.int32, (TOK, D), 0)
                    ok = ok & (kpos <= qpos)
                bias[:, b * TOK : (b + 1) * TOK] = jnp.where(ok, 0.0, NEG)

            def head(i, carry):
                for kv in range(KV_HEADS):
                    h = i + kv * GROUP
                    lanes = slice(kv * D, (kv + 1) * D)
                    kc = jnp.concatenate(
                        [gk[zc, b * KROWS : b * KROWS + TOK, lanes] for b in range(4)], axis=0
                    )
                    vc = jnp.concatenate([gv[zc, :, lanes], jnp.ones((4 * TOK, D), BF)], axis=1)
                    s = lax.dot_general(q_buf[h], kc, NT, preferred_element_type=F32)
                    s = s * factor + bias[...]
                    m_old = m_buf[h]
                    m_new = jnp.maximum(m_old, jnp.max(s, axis=1, keepdims=True))
                    p = jnp.exp2(s - jnp.concatenate([m_new] * 4, axis=1)).astype(BF)
                    alpha = jnp.exp2(m_old - m_new)
                    m_buf[h] = m_new
                    acc_buf[h] = acc_buf[h] * jnp.concatenate([alpha, alpha], axis=1) + jnp.dot(
                        p, vc, preferred_element_type=F32
                    )
                return carry

            lax.fori_loop(0, GROUP, head, 0, unroll=True)

        if d == 0:
            work()
        else:
            pl.when(zc < z)(work)

    def attend_one(d):
        keys.from_core(d)
        vals.from_core(d)
        attend(d)

    def attend_step(step):
        for d in around(step):
            attend_one(d)

    vals.crosses(0)
    keys.cross(0)
    for step in range(1, 5):
        vals.ring(step, "o")
        keys.ring(step, "ox")
        if step == 3:
            cots.start()
        if step == 4:
            cots.ring(1, "o")
            cots.crosses(0)
            attend_one(-3)
            vals.crosses(4)
            attend_one(3)
        else:
            attend_step(step - 1)
            vals.crosses(step)
    cots.ring(2, "o")
    cots.crosses(1)
    attend_step(4)

    for h in range(HEADS):
        acc = acc_buf[h]
        ctx_buf[:, h * D : (h + 1) * D] = (acc[:, 0:D] / acc[:, D : 2 * D]).astype(BF)
    load_w.wait()
    load_gain.wait()
    packed = jnp.dot(packer, ctx_buf[...], preferred_element_type=F32).astype(BF)
    own = jnp.dot(packed, w_buf[...], preferred_element_type=F32).astype(BF)
    own_buf[...] = own
    own = own.astype(F32)
    scale = lax.rsqrt(jnp.mean(own * own, axis=-1, keepdims=True) + 1e-06)
    gr[z, at_row] = (own * scale * gain_buf[...]).astype(BF)

    rows.start()
    save_ctx = load(12, ctx_buf, ctx_out.at[0])
    for wait in load_ffn:
        wait.wait()

    def ffn_in(d):
        rows.from_core(d)
        cots.from_core(d)
        zc = net.zmod(d)
        at = pl.ds(pl.multiple_of(zc * CHUNK, CHUNK), CHUNK)
        row = gr[zc]
        gate = lax.dot_general(gate_w[...], row, NT, preferred_element_type=F32)
        up = lax.dot_general(up_w[...], row, NT, preferred_element_type=F32)
        d_hidden = lax.dot_general(down_w[...], gc[zc], NT, preferred_element_type=F32)
        sig = jax.nn.sigmoid(gate)
        act = gate * sig
        hidden = act * up
        hid[:, at] = hidden.astype(BF)
        hid_rows[zc] = jnp.transpose(hidden).astype(BF)
        d_gate[:, at] = (d_hidden * up * sig * (1.0 + gate * (1.0 - sig))).astype(BF)
        d_up[:, at] = (d_hidden * act).astype(BF)

    cots.ring(3, "o")
    cots.crosses(2)
    rows.cross(0)
    cots.ring(4, "o")
    cots.crosses(3)
    rows.ring(1, "ox")
    ffn_in(0)
    rows.ring(2, "ox")
    cots.crosses(4)
    for step in (1, 2, 3):
        for d in around(step):
            ffn_in(d)
        if step < 3:
            rows.ring(step + 2, "ox")
    ffn_in(4)

    a1 = XFirst(net, "a1", g32, res, 0, 32, a1_refs)
    b1 = HFirst(net, "b1", g32, res, 256, 32, b1_refs)
    a2 = XFirst(net, "a2", g32, res, 512, 32, a2_refs)
    b2 = HFirst(net, "b2", g32, res, 768, 16, b2_refs)
    sums = RowSum(net, part, from_core, stage, land, ys, yr)

    def grad(n, left, right):
        g32[n * FFD : (n + 1) * FFD] = jnp.dot(
            left[...], right[...].reshape(NZ * CHUNK, TD), preferred_element_type=F32
        )

    def ffn_out(*shifts):
        for d in shifts:
            zc = net.zmod(d)
            total = jnp.dot(
                hid_rows[zc, 0 : 4 * SLOTS], down_w[...], preferred_element_type=F32
            ).astype(BF)
            for b in range(4):
                part[b % 2, zc, b // 2] = total[b * SLOTS : (b + 1) * SLOTS]
            sums.swap(d)

    def swapped(*shifts):
        for d in shifts:
            sums.swapped(d)

    grad(0, hid, gc)
    a1.start()
    grad(1, d_gate, gr)
    b1.start()
    g32[3 * FFD :] = jnp.zeros((GROWS - 3 * FFD, TD), F32)
    grad(2, d_up, gr)
    a2.start()
    b2.start()
    ffn_out(4, 3, -3)
    a1.relay()
    ffn_out(2, -2)
    a2.relay()
    swapped(4, 3, -3)
    sums.step(1)
    a1.cross()
    ffn_out(1, -1, 0)
    a2.cross()
    b1.cross()
    swapped(2, -2)
    sums.step(2)
    a1.final()
    b2.cross()
    b1.relay()
    a2.final()
    b2.relay()
    swapped(1, -1, 0)
    sums.step(3)
    a1.spread()
    b1.final()
    a2.spread()
    b2.final()
    sums.step(4)
    a1.forward()
    b1.forward()
    a2.forward()
    b2.forward()
    b1.spread()
    b2.spread()
    sums.across()

    place = lax.broadcasted_iota(jnp.int32, (TOK, SLOTS), 0)
    slot_id = lax.broadcasted_iota(jnp.int32, (TOK, SLOTS), 1)
    spread = jnp.where((place - start == slot_id) & (slot_id < length), 1.0, 0.0).astype(BF)
    out_rows = (own_buf[...].astype(F32) + sums.result()).astype(BF)
    out_buf[...] = jnp.dot(spread, out_rows, preferred_element_type=F32).astype(BF)
    save_out = load(13, out_buf, talker_out.at[0])

    for grads in (a1, a2, b1, b2):
        grads.end()
    save_grads = load(14, res, grads_out)
    net.drain()
    for save in (save_ctx, save_out, save_grads):
        save.wait()


def x_first(size):
    shapes = ((NX, 2, size, TD), (6, size, TD), (2, size, TD), (size, TD), (size, TD))
    return [pltpu.VMEM(shape, BF) for shape in shapes]


def h_first(size):
    wide = pltpu.VMEM((NX * size, TD), BF)
    return [
        wide,
        wide,
        pltpu.VMEM((NX, size, TD), F32),
        pltpu.VMEM((NX, size, TD), BF),
        pltpu.VMEM((6, size, TD), BF),
        pltpu.VMEM((2, size, TD), BF),
    ]


def fused(*args):
    hbm = pl.BlockSpec(memory_space=pl.ANY)
    scratch = (
        ((NZ, 4 * KROWS, KW), BF),
        ((NZ, 4 * TOK, KW), BF),
        ((NZ, CHUNK, TD), BF),
        ((NZ, CHUNK, TD), BF),
        ((TOK, QW), BF),
        ((HEADS, TOK, D), BF),
        ((TOK, QW), BF),
        ((QW, TD), BF),
        ((TOK, TD), BF),
        ((1, TOK), jnp.int32),
        pltpu.SMEM((1, 32), jnp.int32),
        pltpu.SMEM((1, 32), jnp.int32),
        ((TD,), F32),
        ((FFD, TD), BF),
        ((FFD, TD), BF),
        ((FFD, TD), BF),
        ((TOK, D), F32),
        ((TOK, 4 * TOK), F32),
        ((HEADS, TOK, D), F32),
        ((HEADS, TOK, 2 * D), F32),
        ((SLOTS, TD), BF),
        ((TOK, TD), BF),
        ((FFD, NZ * CHUNK), BF),
        ((FFD, NZ * CHUNK), BF),
        ((FFD, NZ * CHUNK), BF),
        ((NZ, CHUNK, FFD), BF),
        ((GROWS, TD), F32),
        ((GROWS, TD), BF),
        x_first(32),
        x_first(32),
        h_first(32),
        h_first(16),
        ((2, NZ, 2, SLOTS, TD), BF),
        ((NZ, 2, SLOTS, TD), BF),
        ((14, SLOTS, TD), BF),
        ((14, SLOTS, TD), BF),
        ((SLOTS, TD), BF),
        ((SLOTS, TD), BF),
        pltpu.SemaphoreType.DMA((256,)),
        pltpu.SemaphoreType.DMA((256,)),
        pltpu.SemaphoreType.DMA((16,)),
    )
    return pl.pallas_call(
        kernel,
        name="mega",
        out_shape=[
            jax.ShapeDtypeStruct((1, TOK, QW), BF),
            jax.ShapeDtypeStruct((1, TOK, TD), BF),
            jax.ShapeDtypeStruct((GROWS, TD), BF),
        ],
        in_specs=[hbm] * len(args),
        out_specs=[hbm] * 3,
        scratch_shapes=[pltpu.VMEM(*s) if isinstance(s, tuple) else s for s in scratch],
        compiler_params=pltpu.CompilerParams(
            collective_id=1, has_side_effects=True, vmem_limit_bytes=VMEM_LIMIT
        ),
    )(*args)


def shards(*args):
    context, talker_out, grads = fused(*args)
    grad_down, grad_gate, grad_up = (
        grads[n * FFD : (n + 1) * FFD].astype(F32) for n in range(3)
    )
    return (context, talker_out, grad_gate, grad_up, grad_down)


def solution(mesh):
    in_specs = (
        P("grp", "ctx", None),
        P("grp", "ctx", None),
        P("grp", "ctx", None),
        P("grp", "ctx"),
        P("grp", None),
        P("grp", None),
        P(),
        P(),
        P("ctx", None),
        P("ctx", None),
        P("ctx", None),
        P("grp", "ctx", None),
    )
    out_specs = (
        P("grp", "ctx", None),
        P("grp", "ctx", None),
        P("ctx", None),
        P("ctx", None),
        P("ctx", None),
    )
    return jax.shard_map(shards, mesh=mesh, in_specs=in_specs, out_specs=out_specs, check_vma=False)
```

```python
import math

import jax
import jax.numpy as jnp
from jax import lax
from jax.experimental import pallas as pl
from jax.experimental.pallas import tpu as pltpu
from jax.sharding import PartitionSpec as P

HEADS = 14
KV_HEADS = 2
GROUP = HEADS // KV_HEADS
D = 128
TOK = 128
TD = 896
QW = HEADS * D
KW = KV_HEADS * D
SLOTS = 48
NZ = 8
NX = 4
FFD = 296
GROWS = 896
SPLIT = 512
AUX = 16
CHUNK = 256
KROWS = TOK + AUX
NEG = -1e30
MESH = pl.DeviceIdType.MESH
BF = jnp.bfloat16
F32 = jnp.float32
NT = (((1,), (1,)), ((), ()))
VMEM_LIMIT = 63 << 20


class Net:
    def __init__(self, send_sems, recv_sems):
        c = lax.axis_index("ctx")
        g = lax.axis_index("grp")
        self.ctx = c
        self.z = c // 4
        self.r = c % 4
        self.y = self.r // 2
        self.k = self.r % 2
        self.x = g // 2
        self.h = g % 2
        self.send_sems = send_sems
        self.recv_sems = recv_sems
        self.ids = {}
        self.sent = []

    def zmod(self, d):
        return lax.rem(self.z + d + NZ, NZ)

    def xmod(self, d):
        return lax.rem(self.x + d + NX, NX)

    def dev(self, where):
        z, y, k, x, h = self.z, self.y, self.k, self.x, self.h
        if where == "+":
            z = self.zmod(1)
        elif where == "-":
            z = self.zmod(-1)
        elif where == "y":
            y = 1 - y
        elif where == "c":
            k = 1 - k
        elif where == "x+":
            x = self.xmod(1)
        elif where == "x-":
            x = self.xmod(-1)
        elif where == "h":
            h = 1 - h
        return (z * 4 + y * 2 + k, x * 2 + h)

    def greet(self, barrier, places):
        for where in places:
            pl.semaphore_signal(
                barrier, inc=1, device_id=self.dev(where), device_id_type=MESH
            )

    def copy(self, key, src, dst, where):
        n = self.ids.setdefault(key, len(self.ids))
        return pltpu.make_async_remote_copy(
            src_ref=src,
            dst_ref=dst,
            send_sem=self.send_sems.at[n],
            recv_sem=self.recv_sems.at[n],
            device_id=self.dev(where),
            device_id_type=MESH,
        )

    def send(self, key, src, where, dst=None):
        copy = self.copy(key, src, src if dst is None else dst, where)
        copy.start()
        self.sent.append(copy)

    def recv(self, key, ref, where):
        self.copy(key, ref, ref, where).wait_recv()

    def drain(self):
        for copy in self.sent:
            copy.wait_send()
        self.sent = []


class Gather:
    def __init__(self, net, name, buf, early, size, lanes=None):
        self.net, self.name, self.buf, self.early, self.size = net, name, buf, early, size
        self.lanes = lanes

    def slot(self, d, lane, other_core=False):
        net = self.net
        y = net.y if lane == "o" else 1 - net.y
        k = 1 - net.k if other_core else net.k
        rows = pl.ds(pl.multiple_of((y * 2 + k) * self.size, 16), self.size)
        if self.lanes is None:
            return self.buf.at[net.zmod(d), rows]
        return self.buf.at[net.zmod(d), rows, pl.ds(*self.lanes)]

    def limit(self, way, lane):
        return 4 if (way == "+") == (lane == "o") else 3

    def to_core(self, d, lane):
        self.net.send((self.name, "c", d, lane), self.slot(d, lane), "c")

    def to_z(self, way, lane, step):
        d = -(step - 1) if way == "+" else step - 1
        self.net.send((self.name, way, lane, step), self.slot(d, lane), way)

    def to_y(self, d):
        self.net.send((self.name, "y", d), self.slot(d, "o"), "y")

    def start(self):
        if self.early:
            self.to_y(0)
        self.to_z("+", "o", 1)
        self.to_z("-", "o", 1)
        if not self.early:
            self.to_y(0)
        self.to_core(0, "o")

    def cross(self, d):
        self.net.recv((self.name, "y", d), self.slot(d, "x"), "y")
        if self.early:
            self.to_z("+", "x", 1)
            self.to_z("-", "x", 1)
        self.to_core(d, "x")

    def arrive(self, way, lane, step):
        top = self.limit(way, lane)
        if step > top:
            return
        d = -step if way == "+" else step
        if d == -4:
            d = 4
        self.net.recv((self.name, way, lane, step), self.slot(d, lane), way)
        if step < top:
            self.to_z(way, lane, step + 1)
        if not self.early:
            self.to_y(d)
        self.to_core(d, lane)

    def ring(self, step, lanes):
        for lane in lanes:
            for way in ("+", "-"):
                self.arrive(way, lane, step)

    def crosses(self, step):
        if not self.early:
            for d in around(step):
                self.cross(d)

    def from_core(self, d):
        for lane in ("o", "x"):
            self.net.recv(
                (self.name, "c", d, lane), self.slot(d, lane, other_core=True), "c"
            )


def around(step):
    if step == 0:
        return (0,)
    if step == 4:
        return (4,)
    return (-step, step)


class GradSum:
    def __init__(self, net, name, g32, res, base, size, refs):
        self.net, self.name, self.g32, self.res = net, name, g32, res
        self.base, self.size = base, size
        self.refs = refs

    def send(self, key, src, where, dst=None):
        self.net.send((self.name, key), src, where, dst)

    def recv(self, key, ref, where):
        self.net.recv((self.name, key), ref, where)


class XFirst(GradSum):
    def rows(self, x, h):
        return pl.ds(pl.multiple_of(self.base + (x * 2 + h) * self.size, 16), self.size)

    def start(self):
        net = self.net
        first, land = self.refs[:2]
        for i in range(NX):
            for h in range(2):
                at = self.base + (i * 2 + h) * self.size
                first[i, h] = self.g32[at : at + self.size].astype(BF)
        far = net.xmod(2)
        self.send("1+", first.at[far, 0], "x+", land.at[0])
        self.send("1-", first.at[far, 1], "x-", land.at[1])
        self.send("2+", first.at[net.xmod(1), 1], "x+", land.at[2])
        self.send("2-", first.at[net.xmod(-1), 0], "x-", land.at[3])

    def relay(self):
        net = self.net
        land, second = self.refs[1:3]
        for n, (way, d, half) in enumerate((("+", 1, 0), ("-", -1, 1))):
            self.recv("1" + way, land.at[n], "x" + way)
            own = self.g32[self.rows(net.xmod(d), half)]
            second[n] = (own + land[n].astype(F32)).astype(BF)
            self.send("3" + way, second.at[n], "x" + way, land.at[4 + n])

    def cross(self):
        net = self.net
        land, _, over, back = self.refs[1:]
        self.recv("2+", land.at[2], "x+")
        self.recv("2-", land.at[3], "x-")
        self.recv("3+", land.at[4], "x+")
        self.recv("3-", land.at[5], "x-")
        for half, (one, two) in enumerate(((3, 4), (2, 5))):
            rows = self.rows(net.x, half)
            self.g32[rows] = self.g32[rows] + land[one].astype(F32) + land[two].astype(F32)
        over[...] = self.g32[self.rows(net.x, 1 - net.h)].astype(BF)
        self.send("h", over, "h", back)

    def final(self):
        net = self.net
        back = self.refs[4]
        self.recv("h", back, "h")
        rows = self.rows(net.x, net.h)
        self.res[rows] = (self.g32[rows] + back[...].astype(F32)).astype(BF)
        for key, where in (("e0", "h"), ("e1+", "x+"), ("e1-", "x-")):
            self.send(key, self.res.at[rows], where)

    def spread(self):
        net = self.net
        rows = self.res.at[self.rows(net.x, 1 - net.h)]
        self.recv("e0", rows, "h")
        self.send("e2+", rows, "x+")
        self.send("e2-", rows, "x-")

    def forward(self):
        net = self.net
        for way, d, half in (("+", -1, 0), ("-", 1, 1)):
            x = net.xmod(d)
            self.recv("e1" + way, self.res.at[self.rows(x, net.h)], "x" + way)
            self.recv("e2" + way, self.res.at[self.rows(x, 1 - net.h)], "x" + way)
            self.send("f" + way, self.res.at[self.rows(x, half)], "x" + way)

    def end(self):
        net = self.net
        for way, half in (("+", 0), ("-", 1)):
            self.recv("f" + way, self.res.at[self.rows(net.xmod(2), half)], "x" + way)


class HFirst(GradSum):
    def part(self, half):
        low = self.size // 32 * 16 or self.size
        return (0, low) if half == 0 else (low, self.size - low)

    def rows(self, h, x, half=None):
        at, size = (0, self.size) if half is None else self.part(half)
        return pl.ds(pl.multiple_of(self.base + (h * NX + x) * self.size + at, 16), size)

    def ways(self, plan):
        return [m for m in plan if self.part(m[-1])[1]]

    def start(self):
        net = self.net
        first, land = self.refs[:2]
        at = self.base + (1 - net.h) * NX * self.size
        first[...] = self.g32[pl.ds(pl.multiple_of(at, 16), NX * self.size)].astype(BF)
        self.send("0", first, "h", land)

    def cross(self):
        net = self.net
        back, total, second, ring = self.refs[1:5]
        self.recv("0", back, "h")
        for i in range(NX):
            rows = slice(i * self.size, (i + 1) * self.size)
            value = self.g32[self.rows(net.h, i)] + back[rows].astype(F32)
            total[i] = value
            second[i] = value.astype(BF)
        plan = ((0, "1+", "+", 2, 0), (1, "1-", "-", 2, 1), (2, "2+", "+", 1, 1), (3, "2-", "-", -1, 0))
        for n, key, way, d, half in self.ways(plan):
            at = pl.ds(*self.part(half))
            self.send(key, second.at[net.xmod(d), at], "x" + way, ring.at[n, at])

    def relay(self):
        net = self.net
        total, _, ring, third = self.refs[2:]
        for n, way, d, half in self.ways(((0, "+", 1, 0), (1, "-", -1, 1))):
            at = pl.ds(*self.part(half))
            self.recv("1" + way, ring.at[n, at], "x" + way)
            third[n, at] = (total[net.xmod(d), at] + ring[n, at].astype(F32)).astype(BF)
            self.send("3" + way, third.at[n, at], "x" + way, ring.at[4 + n, at])

    def final(self):
        net = self.net
        total, _, ring = self.refs[2:5]
        plan = ((2, "2+", "+", 1), (3, "2-", "-", 0), (4, "3+", "+", 0), (5, "3-", "-", 1))
        for n, key, way, half in self.ways(plan):
            self.recv(key, ring.at[n, pl.ds(*self.part(half))], "x" + way)
        for one, two, half in self.ways(((3, 4, 0), (2, 5, 1))):
            at = pl.ds(*self.part(half))
            value = total[net.x, at] + ring[one, at].astype(F32) + ring[two, at].astype(F32)
            self.res[self.rows(net.h, net.x, half)] = value.astype(BF)
        rows = self.res.at[self.rows(net.h, net.x)]
        for key, where in (("q+", "x+"), ("q-", "x-"), ("p0", "h")):
            self.send(key, rows, where)

    def forward(self):
        net = self.net
        for n, (way, d, half) in enumerate((("+", -1, 0), ("-", 1, 1))):
            x = net.xmod(d)
            rows = self.res.at[self.rows(net.h, x)]
            self.recv("q" + way, rows, "x" + way)
            if self.part(half)[1]:
                self.send("s" + way, self.res.at[self.rows(net.h, x, half)], "x" + way)
            self.send("p%d" % (n + 1), rows, "h")

    def spread(self):
        net = self.net
        x = net.xmod(2)
        for way, half in self.ways((("+", 0), ("-", 1))):
            self.recv("s" + way, self.res.at[self.rows(net.h, x, half)], "x" + way)
        self.send("p3", self.res.at[self.rows(net.h, x)], "h")

    def end(self):
        net = self.net
        for n, d in enumerate((0, -1, 1, 2)):
            self.recv("p%d" % n, self.res.at[self.rows(1 - net.h, net.xmod(d))], "h")


class RowSum:
    def __init__(self, net, part, from_core, stage, land, ys, yr):
        self.net, self.part, self.from_core = net, part, from_core
        self.stage, self.land, self.ys, self.yr = stage, land, ys, yr
        self.at = {}
        for way in ("+", "-"):
            for lane in ("o", "x"):
                for step in range(1, self.limit(way, lane) + 1):
                    self.at[way, lane, step] = len(self.at)

    def limit(self, way, lane):
        return 4 if (way == "+") == (lane == "o") else 3

    def swap(self, d):
        net = self.net
        z = net.zmod(d)
        net.send(("c", d), self.part.at[1 - net.k, z], "c", self.from_core.at[z])

    def swapped(self, d):
        self.net.recv(("c", d), self.from_core.at[self.net.zmod(d)], "c")

    def own(self, d, lane):
        net = self.net
        z = net.zmod(d)
        y = net.y if lane == "o" else 1 - net.y
        return self.part[net.k, z, y].astype(F32) + self.from_core[z, y].astype(F32)

    def landed(self, way, lane, step):
        n = self.at[way, lane, step]
        self.net.recv(("z", way, lane, step), self.land.at[n], way)
        return self.land[n].astype(F32)

    def step(self, step):
        for lane in ("o", "x"):
            for way in ("+", "-"):
                top = self.limit(way, lane)
                if step > top:
                    continue
                left = top - step + 1
                d = left if way == "+" or left == 4 else -left
                total = self.own(d, lane)
                if step > 1:
                    total = total + self.landed(way, lane, step - 1)
                n = self.at[way, lane, step]
                self.stage[n] = total.astype(BF)
                self.net.send(("z", way, lane, step), self.stage.at[n], way, self.land.at[n])

    def across(self):
        total = self.own(0, "x")
        for way in ("+", "-"):
            total = total + self.landed(way, "x", self.limit(way, "x"))
        self.ys[...] = total.astype(BF)
        self.net.send("y", self.ys, "y", self.yr)

    def result(self):
        total = self.own(0, "o")
        for way in ("+", "-"):
            total = total + self.landed(way, "o", self.limit(way, "o"))
        self.net.recv("y", self.yr, "y")
        return total + self.yr[...].astype(F32)


def kernel(
    q_hbm,
    k_hbm,
    v_hbm,
    seg_hbm,
    start_hbm,
    len_hbm,
    w_hbm,
    gain_hbm,
    gate_hbm,
    up_hbm,
    down_hbm,
    cot_hbm,
    ctx_out,
    talker_out,
    grads_out,
    gk,
    gv,
    gr,
    gc,
    q_raw,
    q_buf,
    ctx_buf,
    w_buf,
    cot_buf,
    seg_buf,
    start_buf,
    len_buf,
    gain_buf,
    gate_w,
    up_w,
    down_w,
    segq,
    bias,
    m_buf,
    acc_buf,
    own_buf,
    out_buf,
    hid,
    d_gate,
    d_up,
    hid_rows,
    g32,
    res,
    a1_refs,
    b1_refs,
    b2_refs,
    a2_refs,
    a3_refs,
    part,
    from_core,
    stage,
    land,
    ys,
    yr,
    send_sems,
    recv_sems,
    local_sems,
):
    net = Net(send_sems, recv_sems)
    z, r = net.z, net.r

    def load(n, src, dst):
        copy = pltpu.make_async_copy(src, dst, local_sems.at[n])
        copy.start()
        return copy

    at_k = pl.ds(pl.multiple_of(r * KROWS, 16), TOK)
    at_aux = pl.ds(pl.multiple_of(r * KROWS + TOK, 16), AUX)
    at_v = pl.ds(pl.multiple_of(r * TOK, 16), TOK)
    at_row = pl.ds(pl.multiple_of(r * SLOTS, 16), SLOTS)
    load_seg = load(0, seg_hbm, seg_buf)
    load_k = load(1, k_hbm.at[0], gk.at[z, at_k])
    load_v = load(2, v_hbm.at[0], gv.at[z, at_v])
    load_q = load(3, q_hbm.at[0], q_raw)
    load_start = load(4, start_hbm, start_buf)
    load_len = load(5, len_hbm, len_buf)
    load_cot = load(6, cot_hbm.at[0], cot_buf)
    load_w = load(7, w_hbm, w_buf)
    load_gain = load(8, gain_hbm, gain_buf)
    load_ffn = [
        load(9, gate_hbm, gate_w),
        load(10, up_hbm, up_w),
        load(11, down_hbm, down_w),
    ]

    barrier = pltpu.get_barrier_semaphore()
    places = ("+", "-", "y", "c", "x+", "x-", "h")
    net.greet(barrier, places)

    load_seg.wait()
    seg_row = seg_buf[...].astype(F32)
    gk[z, at_aux, 0:D] = jnp.broadcast_to(seg_row, (AUX, D)).astype(BF)
    gk[z, at_aux, D : 2 * D] = jnp.zeros((AUX, D), BF)

    keys = Gather(net, "k", gk, True, KROWS)
    vals = Gather(net, "v", gv, False, TOK)
    rows_a = Gather(net, "ra", gr, True, SLOTS, (0, SPLIT))
    rows_b = Gather(net, "rb", gr, False, SLOTS, (SPLIT, TD - SPLIT))
    cots = Gather(net, "g", gc, False, SLOTS)

    load_k.wait()
    load_v.wait()
    pl.semaphore_wait(barrier, len(places))
    keys.start()
    vals.start()

    segq[...] = jnp.transpose(jnp.broadcast_to(seg_row, (TOK, D)))
    m_buf[...] = jnp.full(m_buf.shape, NEG, F32)
    acc_buf[...] = jnp.zeros(acc_buf.shape, F32)
    load_q.wait()
    for h in range(HEADS):
        q_buf[h] = q_raw[:, h * D : (h + 1) * D]

    load_start.wait()
    load_len.wait()
    start = start_buf[0, net.ctx] - net.ctx * TOK
    length = len_buf[0, net.ctx]
    slot_id = lax.broadcasted_iota(jnp.int32, (SLOTS, TOK), 0)
    place = lax.broadcasted_iota(jnp.int32, (SLOTS, TOK), 1)
    packer = jnp.where((place - start == slot_id) & (slot_id < length), 1.0, 0.0).astype(BF)
    load_cot.wait()
    gc[z, at_row] = jnp.dot(packer, cot_buf[...], preferred_element_type=F32).astype(BF)
    for i in range(NZ):
        for buf in (gr, gc):
            buf[i, 4 * SLOTS :] = jnp.zeros((CHUNK - 4 * SLOTS, TD), BF)

    factor = math.log2(math.e) / math.sqrt(D)

    def attend(d):
        zc = net.zmod(d)

        def work():
            for b in range(4):
                aux = b * KROWS + TOK
                ok = segq[...] == gk[zc, aux : aux + AUX, 0:D].astype(F32)[0:1]
                if d == 0:
                    kpos = lax.broadcasted_iota(jnp.int32, (TOK, D), 1) + (b - r) * TOK
                    qpos = lax.broadcasted_iota(jnp.int32, (TOK, D), 0)
                    ok = ok & (kpos <= qpos)
                bias[:, b * TOK : (b + 1) * TOK] = jnp.where(ok, 0.0, NEG)

            def head(i, carry):
                for kv in range(KV_HEADS):
                    h = i + kv * GROUP
                    lanes = slice(kv * D, (kv + 1) * D)
                    kc = jnp.concatenate(
                        [gk[zc, b * KROWS : b * KROWS + TOK, lanes] for b in range(4)], axis=0
                    )
                    vc = jnp.concatenate([gv[zc, :, lanes], jnp.ones((4 * TOK, D), BF)], axis=1)
                    s = lax.dot_general(q_buf[h], kc, NT, preferred_element_type=F32)
                    s = s * factor + bias[...]
                    m_old = m_buf[h]
                    m_new = jnp.maximum(m_old, jnp.max(s, axis=1, keepdims=True))
                    p = jnp.exp2(s - jnp.concatenate([m_new] * 4, axis=1)).astype(BF)
                    alpha = jnp.exp2(m_old - m_new)
                    m_buf[h] = m_new
                    acc_buf[h] = acc_buf[h] * jnp.concatenate([alpha, alpha], axis=1) + jnp.dot(
                        p, vc, preferred_element_type=F32
                    )
                return carry

            lax.fori_loop(0, GROUP, head, 0, unroll=True)

        if d == 0:
            work()
        else:
            pl.when(zc < z)(work)

    def attend_one(d):
        keys.from_core(d)
        vals.from_core(d)
        attend(d)

    def attend_step(step):
        for d in around(step):
            attend_one(d)

    vals.crosses(0)
    keys.cross(0)
    for step in range(1, 5):
        vals.ring(step, "o")
        keys.ring(step, "ox")
        if step == 3:
            cots.start()
        if step == 4:
            cots.ring(1, "o")
            cots.crosses(0)
            attend_one(-3)
            vals.crosses(4)
            attend_one(3)
        else:
            attend_step(step - 1)
            vals.crosses(step)
    cots.ring(2, "o")
    cots.crosses(1)
    attend_step(4)

    for h in range(HEADS):
        acc = acc_buf[h]
        ctx_buf[:, h * D : (h + 1) * D] = (acc[:, 0:D] / acc[:, D : 2 * D]).astype(BF)
    load_w.wait()
    load_gain.wait()
    packed = jnp.dot(packer, ctx_buf[...], preferred_element_type=F32).astype(BF)
    own = jnp.dot(packed, w_buf[...], preferred_element_type=F32).astype(BF)
    own_buf[...] = own
    own = own.astype(F32)
    scale = lax.rsqrt(jnp.mean(own * own, axis=-1, keepdims=True) + 1e-06)
    gr[z, at_row] = (own * scale * gain_buf[...]).astype(BF)

    rows_a.start()
    rows_b.start()
    save_ctx = load(12, ctx_buf, ctx_out)
    for wait in load_ffn:
        wait.wait()
    sums = RowSum(net, part, from_core, stage, land, ys, yr)

    def ffn(d):
        rows_a.from_core(d)
        rows_b.from_core(d)
        cots.from_core(d)
        zc = net.zmod(d)
        at = pl.ds(pl.multiple_of(zc * CHUNK, CHUNK), CHUNK)
        row = gr[zc]
        gate = lax.dot_general(gate_w[...], row, NT, preferred_element_type=F32)
        up = lax.dot_general(up_w[...], row, NT, preferred_element_type=F32)
        d_hidden = lax.dot_general(down_w[...], gc[zc], NT, preferred_element_type=F32)
        sig = jax.nn.sigmoid(gate)
        act = gate * sig
        hidden = act * up
        hid[:, at] = hidden.astype(BF)
        hid_rows[zc] = jnp.transpose(hidden).astype(BF)
        total = jnp.dot(
            hid_rows[zc, 0 : 4 * SLOTS], down_w[...], preferred_element_type=F32
        ).astype(BF)
        for b in range(4):
            part[b % 2, zc, b // 2] = total[b * SLOTS : (b + 1) * SLOTS]
        sums.swap(d)
        d_gate[:, at] = (d_hidden * up * sig * (1.0 + gate * (1.0 - sig))).astype(BF)
        d_up[:, at] = (d_hidden * act).astype(BF)

    cots.ring(3, "o")
    cots.crosses(2)
    rows_a.cross(0)
    rows_b.crosses(0)
    cots.ring(4, "o")
    cots.crosses(3)
    for step in range(1, 5):
        rows_a.ring(step, "o")
        rows_b.ring(step, "o")
        if step > 1:
            rows_b.crosses(step - 1)
        rows_a.ring(step, "x")
        if step == 2:
            cots.crosses(4)
        for d in around(step - 1):
            ffn(d)
    rows_b.crosses(4)
    ffn(4)

    def grad(n, left, right):
        g32[n * FFD : (n + 1) * FFD] = jnp.dot(
            left[...], right[...].reshape(NZ * CHUNK, TD), preferred_element_type=F32
        )

    def swapped(*shifts):
        for d in shifts:
            sums.swapped(d)

    a1 = XFirst(net, "a1", g32, res, 0, 16, a1_refs)
    b1 = HFirst(net, "b1", g32, res, 128, 16, b1_refs)
    b2 = HFirst(net, "b2", g32, res, 256, 32, b2_refs)
    a2 = XFirst(net, "a2", g32, res, 512, 32, a2_refs)
    a3 = XFirst(net, "a3", g32, res, 768, 16, a3_refs)

    grad(0, hid, gc)
    a1.start()
    b1.start()
    swapped(4, 3, -3)
    sums.step(1)
    grad(1, d_gate, gr)
    b2.start()
    g32[3 * FFD :] = jnp.zeros((GROWS - 3 * FFD, TD), F32)
    grad(2, d_up, gr)
    a2.start()
    a3.start()
    a1.relay()
    swapped(2, -2)
    sums.step(2)
    b1.cross()
    a1.cross()
    a2.relay()
    a3.relay()
    b1.relay()
    a3.cross()
    a2.cross()
    swapped(1, -1, 0)
    sums.step(3)
    a1.final()
    b2.cross()
    b1.final()
    a3.final()
    a2.final()
    b2.relay()
    sums.step(4)
    a1.spread()
    b1.forward()
    a1.forward()
    b2.final()
    b1.spread()
    a3.spread()
    a2.spread()
    sums.across()
    a3.forward()
    b2.forward()
    a2.forward()
    b2.spread()

    place = lax.broadcasted_iota(jnp.int32, (TOK, SLOTS), 0)
    slot_id = lax.broadcasted_iota(jnp.int32, (TOK, SLOTS), 1)
    spread = jnp.where((place - start == slot_id) & (slot_id < length), 1.0, 0.0).astype(BF)
    out_rows = (own_buf[...].astype(F32) + sums.result()).astype(BF)
    out_buf[...] = jnp.dot(spread, out_rows, preferred_element_type=F32).astype(BF)
    save_out = load(13, out_buf, talker_out)

    for grads in (a1, b1, a3, a2, b2):
        grads.end()
    save_grads = load(14, res, grads_out)
    net.drain()
    for save in (save_ctx, save_out, save_grads):
        save.wait()


def x_first(size):
    shapes = ((NX, 2, size, TD), (6, size, TD), (2, size, TD), (size, TD), (size, TD))
    return [pltpu.VMEM(shape, BF) for shape in shapes]


def h_first(size):
    wide = pltpu.VMEM((NX * size, TD), BF)
    return [
        wide,
        wide,
        pltpu.VMEM((NX, size, TD), F32),
        pltpu.VMEM((NX, size, TD), BF),
        pltpu.VMEM((6, size, TD), BF),
        pltpu.VMEM((2, size, TD), BF),
    ]


def fused(*args):
    hbm = pl.BlockSpec(memory_space=pl.ANY)
    scratch = (
        ((NZ, 4 * KROWS, KW), BF),
        ((NZ, 4 * TOK, KW), BF),
        ((NZ, CHUNK, TD), BF),
        ((NZ, CHUNK, TD), BF),
        ((TOK, QW), BF),
        ((HEADS, TOK, D), BF),
        ((TOK, QW), BF),
        ((QW, TD), BF),
        ((TOK, TD), BF),
        ((1, TOK), jnp.int32),
        pltpu.SMEM((1, 32), jnp.int32),
        pltpu.SMEM((1, 32), jnp.int32),
        ((TD,), F32),
        ((FFD, TD), BF),
        ((FFD, TD), BF),
        ((FFD, TD), BF),
        ((TOK, D), F32),
        ((TOK, 4 * TOK), F32),
        ((HEADS, TOK, D), F32),
        ((HEADS, TOK, 2 * D), F32),
        ((SLOTS, TD), BF),
        ((TOK, TD), BF),
        ((FFD, NZ * CHUNK), BF),
        ((FFD, NZ * CHUNK), BF),
        ((FFD, NZ * CHUNK), BF),
        ((NZ, CHUNK, FFD), BF),
        ((GROWS, TD), F32),
        ((GROWS, TD), BF),
        x_first(16),
        h_first(16),
        h_first(32),
        x_first(32),
        x_first(16),
        ((2, NZ, 2, SLOTS, TD), BF),
        ((NZ, 2, SLOTS, TD), BF),
        ((14, SLOTS, TD), BF),
        ((14, SLOTS, TD), BF),
        ((SLOTS, TD), BF),
        ((SLOTS, TD), BF),
        pltpu.SemaphoreType.DMA((288,)),
        pltpu.SemaphoreType.DMA((288,)),
        pltpu.SemaphoreType.DMA((16,)),
    )
    return pl.pallas_call(
        kernel,
        name="mega",
        out_shape=[
            jax.ShapeDtypeStruct((TOK, QW), BF),
            jax.ShapeDtypeStruct((TOK, TD), BF),
            jax.ShapeDtypeStruct((GROWS, TD), BF),
        ],
        in_specs=[hbm] * len(args),
        out_specs=[hbm] * 3,
        scratch_shapes=[pltpu.VMEM(*s) if isinstance(s, tuple) else s for s in scratch],
        compiler_params=pltpu.CompilerParams(
            collective_id=1, has_side_effects=True, vmem_limit_bytes=VMEM_LIMIT
        ),
    )(*args)


def finish_kernel(ctx_in, talker_in, grads_in, ctx_out, talker_out, down_out, gate_out, up_out, low, wide, sems):
    def move(n, src, dst):
        copy = pltpu.make_async_copy(src, dst, sems.at[n])
        copy.start()
        return copy

    step = 128
    loads = [
        move(n, grads_in.at[pl.ds(n * step, step)], low.at[pl.ds(n * step, step)])
        for n in range(GROWS // step)
    ]
    moves = [move(7, ctx_in, ctx_out.at[0]), move(8, talker_in, talker_out.at[0])]
    outs = [down_out, gate_out, up_out]
    for n, load in enumerate(loads):
        load.wait()
        wide[n * step : (n + 1) * step] = low[n * step : (n + 1) * step].astype(F32)
        done = 3 - len(outs)
        if outs and (n + 1) * step >= (done + 1) * FFD:
            moves.append(move(9 + done, wide.at[pl.ds(done * FFD, FFD)], outs.pop(0)))
    for copy in moves:
        copy.wait()


def finish(context, talker, grads):
    hbm = pl.BlockSpec(memory_space=pl.ANY)
    grad = jax.ShapeDtypeStruct((FFD, TD), F32)
    return pl.pallas_call(
        finish_kernel,
        name="finish",
        out_shape=[
            jax.ShapeDtypeStruct((1, TOK, QW), BF),
            jax.ShapeDtypeStruct((1, TOK, TD), BF),
            grad,
            grad,
            grad,
        ],
        in_specs=[hbm] * 3,
        out_specs=[hbm] * 5,
        scratch_shapes=[
            pltpu.VMEM((GROWS, TD), BF),
            pltpu.VMEM((GROWS, TD), F32),
            pltpu.SemaphoreType.DMA((12,)),
        ],
        compiler_params=pltpu.CompilerParams(vmem_limit_bytes=VMEM_LIMIT),
    )(context, talker, grads)


def shards(*args):
    context, talker, grad_down, grad_gate, grad_up = finish(*fused(*args))
    return (context, talker, grad_gate, grad_up, grad_down)


def solution(mesh):
    in_specs = (
        P("grp", "ctx", None),
        P("grp", "ctx", None),
        P("grp", "ctx", None),
        P("grp", "ctx"),
        P("grp", None),
        P("grp", None),
        P(),
        P(),
        P("ctx", None),
        P("ctx", None),
        P("ctx", None),
        P("grp", "ctx", None),
    )
    out_specs = (
        P("grp", "ctx", None),
        P("grp", "ctx", None),
        P("ctx", None),
        P("ctx", None),
        P("ctx", None),
    )
    return jax.shard_map(shards, mesh=mesh, in_specs=in_specs, out_specs=out_specs, check_vma=False)
```

```python
import math

import jax
import jax.numpy as jnp
from jax import lax
from jax.experimental import pallas as pl
from jax.experimental.pallas import tpu as pltpu
from jax.sharding import PartitionSpec as P

HEADS = 14
KV_HEADS = 2
GROUP = HEADS // KV_HEADS
D = 128
TOK = 128
TD = 896
QW = HEADS * D
KW = KV_HEADS * D
SLOTS = 48
NZ = 8
NX = 4
FFD = 296
GROWS = 896
AUX = 16
CHUNK = 256
KROWS = TOK + AUX
NEG = -1e30
MESH = pl.DeviceIdType.MESH
BF = jnp.bfloat16
F32 = jnp.float32
NT = (((1,), (1,)), ((), ()))
VMEM_LIMIT = 63 << 20


class Net:
    def __init__(self, send_sems, recv_sems):
        c = lax.axis_index("ctx")
        g = lax.axis_index("grp")
        self.ctx = c
        self.z = c // 4
        self.r = c % 4
        self.y = self.r // 2
        self.k = self.r % 2
        self.x = g // 2
        self.h = g % 2
        self.send_sems = send_sems
        self.recv_sems = recv_sems
        self.ids = {}
        self.sent = []
        self.older = []

    def zmod(self, d):
        return lax.rem(self.z + d + NZ, NZ)

    def xmod(self, d):
        return lax.rem(self.x + d + NX, NX)

    def dev(self, where):
        z, y, k, x, h = self.z, self.y, self.k, self.x, self.h
        if where == "+":
            z = self.zmod(1)
        elif where == "-":
            z = self.zmod(-1)
        elif where == "y":
            y = 1 - y
        elif where == "c":
            k = 1 - k
        elif where == "x+":
            x = self.xmod(1)
        elif where == "x-":
            x = self.xmod(-1)
        elif where == "h":
            h = 1 - h
        return (z * 4 + y * 2 + k, x * 2 + h)

    def greet(self, barrier, places):
        for where in places:
            pl.semaphore_signal(
                barrier, inc=1, device_id=self.dev(where), device_id_type=MESH
            )

    def copy(self, key, src, dst, where):
        n = self.ids.setdefault(key, len(self.ids))
        return pltpu.make_async_remote_copy(
            src_ref=src,
            dst_ref=dst,
            send_sem=self.send_sems.at[n],
            recv_sem=self.recv_sems.at[n],
            device_id=self.dev(where),
            device_id_type=MESH,
        )

    def send(self, key, src, where, dst=None):
        copy = self.copy(key, src, src if dst is None else dst, where)
        copy.start()
        self.sent.append(copy)

    def recv(self, key, ref, where):
        self.copy(key, ref, ref, where).wait_recv()

    def settle(self):
        for copy in self.older:
            copy.wait_send()
        self.older, self.sent = self.sent, []

    def drain(self):
        self.settle()
        self.settle()


class Gather:
    def __init__(self, net, name, buf, early, size):
        self.net, self.name, self.buf, self.early, self.size = net, name, buf, early, size

    def slot(self, d, lane, other_core=False):
        net = self.net
        y = net.y if lane == "o" else 1 - net.y
        k = 1 - net.k if other_core else net.k
        return self.buf.at[net.zmod(d), pl.ds(pl.multiple_of((y * 2 + k) * self.size, 16), self.size)]

    def limit(self, way, lane):
        return 4 if (way == "+") == (lane == "o") else 3

    def to_core(self, d, lane):
        self.net.send((self.name, "c", d, lane), self.slot(d, lane), "c")

    def to_z(self, way, lane, step):
        d = -(step - 1) if way == "+" else step - 1
        self.net.send((self.name, way, lane, step), self.slot(d, lane), way)

    def to_y(self, d):
        self.net.send((self.name, "y", d), self.slot(d, "o"), "y")

    def start(self):
        if self.early:
            self.to_y(0)
        self.to_z("+", "o", 1)
        self.to_z("-", "o", 1)
        if not self.early:
            self.to_y(0)
        self.to_core(0, "o")

    def cross(self, d):
        self.net.recv((self.name, "y", d), self.slot(d, "x"), "y")
        if self.early:
            self.to_z("+", "x", 1)
            self.to_z("-", "x", 1)
        self.to_core(d, "x")

    def arrive(self, way, lane, step):
        top = self.limit(way, lane)
        if step > top:
            return
        d = -step if way == "+" else step
        if d == -4:
            d = 4
        self.net.recv((self.name, way, lane, step), self.slot(d, lane), way)
        if step < top:
            self.to_z(way, lane, step + 1)
        if not self.early:
            self.to_y(d)
        self.to_core(d, lane)

    def ring(self, step, lanes):
        for lane in lanes:
            for way in ("+", "-"):
                self.arrive(way, lane, step)

    def crosses(self, step):
        if not self.early:
            for d in around(step):
                self.cross(d)

    def from_core(self, d):
        for lane in ("o", "x"):
            self.net.recv(
                (self.name, "c", d, lane), self.slot(d, lane, other_core=True), "c"
            )


def around(step):
    if step == 0:
        return (0,)
    if step == 4:
        return (4,)
    return (-step, step)


class GradSum:
    def __init__(self, net, name, g32, res, base, size, refs):
        self.net, self.name, self.g32, self.res = net, name, g32, res
        self.base, self.size = base, size
        self.refs = refs

    def send(self, key, src, where, dst=None):
        self.net.send((self.name, key), src, where, dst)

    def recv(self, key, ref, where):
        self.net.recv((self.name, key), ref, where)


class XFirst(GradSum):
    def rows(self, x, h):
        return pl.ds(pl.multiple_of(self.base + (x * 2 + h) * self.size, 16), self.size)

    def start(self):
        net = self.net
        first, land = self.refs[:2]
        for i in range(NX):
            for h in range(2):
                at = self.base + (i * 2 + h) * self.size
                first[i, h] = self.g32[at : at + self.size].astype(BF)
        far = net.xmod(2)
        self.send("1+", first.at[far, 0], "x+", land.at[0])
        self.send("1-", first.at[far, 1], "x-", land.at[1])
        self.send("2+", first.at[net.xmod(1), 1], "x+", land.at[2])
        self.send("2-", first.at[net.xmod(-1), 0], "x-", land.at[3])

    def relay(self):
        net = self.net
        land, second = self.refs[1:3]
        for n, (way, d, half) in enumerate((("+", 1, 0), ("-", -1, 1))):
            self.recv("1" + way, land.at[n], "x" + way)
            own = self.g32[self.rows(net.xmod(d), half)]
            second[n] = (own + land[n].astype(F32)).astype(BF)
            self.send("3" + way, second.at[n], "x" + way, land.at[4 + n])

    def cross(self):
        net = self.net
        land, _, over, back = self.refs[1:]
        self.recv("2+", land.at[2], "x+")
        self.recv("2-", land.at[3], "x-")
        self.recv("3+", land.at[4], "x+")
        self.recv("3-", land.at[5], "x-")
        for half, (one, two) in enumerate(((3, 4), (2, 5))):
            rows = self.rows(net.x, half)
            self.g32[rows] = self.g32[rows] + land[one].astype(F32) + land[two].astype(F32)
        over[...] = self.g32[self.rows(net.x, 1 - net.h)].astype(BF)
        self.send("h", over, "h", back)

    def final(self):
        net = self.net
        back = self.refs[4]
        self.recv("h", back, "h")
        rows = self.rows(net.x, net.h)
        self.res[rows] = (self.g32[rows] + back[...].astype(F32)).astype(BF)
        for key, where in (("e0", "h"), ("e1+", "x+"), ("e1-", "x-")):
            self.send(key, self.res.at[rows], where)

    def spread(self):
        net = self.net
        rows = self.res.at[self.rows(net.x, 1 - net.h)]
        self.recv("e0", rows, "h")
        self.send("e2+", rows, "x+")
        self.send("e2-", rows, "x-")

    def forward(self):
        net = self.net
        for way, d, half in (("+", -1, 0), ("-", 1, 1)):
            x = net.xmod(d)
            self.recv("e1" + way, self.res.at[self.rows(x, net.h)], "x" + way)
            self.recv("e2" + way, self.res.at[self.rows(x, 1 - net.h)], "x" + way)
            self.send("f" + way, self.res.at[self.rows(x, half)], "x" + way)

    def end(self):
        net = self.net
        for way, half in (("+", 0), ("-", 1)):
            self.recv("f" + way, self.res.at[self.rows(net.xmod(2), half)], "x" + way)


class HFirst(GradSum):
    def part(self, half):
        low = self.size // 32 * 16 or self.size
        return (0, low) if half == 0 else (low, self.size - low)

    def rows(self, h, x, half=None):
        at, size = (0, self.size) if half is None else self.part(half)
        return pl.ds(pl.multiple_of(self.base + (h * NX + x) * self.size + at, 16), size)

    def ways(self, plan):
        return [m for m in plan if self.part(m[-1])[1]]

    def start(self):
        net = self.net
        first, land = self.refs[:2]
        for i in range(NX):
            first[i] = self.g32[self.rows(1 - net.h, i)].astype(BF)
        for d in (2, 1, -1, 0):
            x = net.xmod(d)
            self.send(("0", d), first.at[x], "h", land.at[x])

    def pair(self, d):
        net = self.net
        back, total, second = self.refs[1:4]
        x = net.xmod(d)
        self.recv(("0", d), back.at[x], "h")
        value = self.g32[self.rows(net.h, x)] + back[x].astype(F32)
        total[x] = value
        second[x] = value.astype(BF)

    def pass_on(self, n, key, way, d, half):
        second, ring = self.refs[3:5]
        if self.part(half)[1]:
            at = pl.ds(*self.part(half))
            self.send(key, second.at[self.net.xmod(d), at], "x" + way, ring.at[n, at])

    def cross_far(self):
        self.pair(2)
        self.pass_on(0, "1+", "+", 2, 0)
        self.pass_on(1, "1-", "-", 2, 1)

    def cross(self):
        self.pair(1)
        self.pass_on(2, "2+", "+", 1, 1)
        self.pair(-1)
        self.pass_on(3, "2-", "-", -1, 0)
        self.pair(0)

    def relay(self):
        net = self.net
        total, _, ring, third = self.refs[2:]
        for n, way, d, half in self.ways(((0, "+", 1, 0), (1, "-", -1, 1))):
            at = pl.ds(*self.part(half))
            self.recv("1" + way, ring.at[n, at], "x" + way)
            third[n, at] = (total[net.xmod(d), at] + ring[n, at].astype(F32)).astype(BF)
            self.send("3" + way, third.at[n, at], "x" + way, ring.at[4 + n, at])

    def final(self):
        net = self.net
        total, _, ring = self.refs[2:5]
        plan = ((2, "2+", "+", 1), (3, "2-", "-", 0), (4, "3+", "+", 0), (5, "3-", "-", 1))
        for n, key, way, half in self.ways(plan):
            self.recv(key, ring.at[n, pl.ds(*self.part(half))], "x" + way)
        for one, two, half in self.ways(((3, 4, 0), (2, 5, 1))):
            at = pl.ds(*self.part(half))
            value = total[net.x, at] + ring[one, at].astype(F32) + ring[two, at].astype(F32)
            self.res[self.rows(net.h, net.x, half)] = value.astype(BF)
        rows = self.res.at[self.rows(net.h, net.x)]
        for key, where in (("q+", "x+"), ("q-", "x-"), ("p0", "h")):
            self.send(key, rows, where)

    def forward(self):
        net = self.net
        for n, (way, d, half) in enumerate((("+", -1, 0), ("-", 1, 1))):
            x = net.xmod(d)
            rows = self.res.at[self.rows(net.h, x)]
            self.recv("q" + way, rows, "x" + way)
            if self.part(half)[1]:
                self.send("s" + way, self.res.at[self.rows(net.h, x, half)], "x" + way)
            self.send("p%d" % (n + 1), rows, "h")

    def spread(self):
        net = self.net
        x = net.xmod(2)
        for way, half in self.ways((("+", 0), ("-", 1))):
            self.recv("s" + way, self.res.at[self.rows(net.h, x, half)], "x" + way)
        self.send("p3", self.res.at[self.rows(net.h, x)], "h")

    def end(self):
        net = self.net
        for n, d in enumerate((0, -1, 1, 2)):
            self.recv("p%d" % n, self.res.at[self.rows(1 - net.h, net.xmod(d))], "h")


class RowSum:
    def __init__(self, net, part, from_core, stage, land, ys, yr):
        self.net, self.part, self.from_core = net, part, from_core
        self.stage, self.land, self.ys, self.yr = stage, land, ys, yr
        self.at = {}
        for way in ("+", "-"):
            for lane in ("o", "x"):
                for step in range(1, self.limit(way, lane) + 1):
                    self.at[way, lane, step] = len(self.at)

    def limit(self, way, lane):
        return 4 if (way == "+") == (lane == "o") else 3

    def swap(self, d):
        net = self.net
        z = net.zmod(d)
        net.send(("c", d), self.part.at[1 - net.k, z], "c", self.from_core.at[z])

    def swapped(self, d):
        self.net.recv(("c", d), self.from_core.at[self.net.zmod(d)], "c")

    def own(self, d, lane):
        net = self.net
        z = net.zmod(d)
        y = net.y if lane == "o" else 1 - net.y
        return self.part[net.k, z, y].astype(F32) + self.from_core[z, y].astype(F32)

    def landed(self, way, lane, step):
        n = self.at[way, lane, step]
        self.net.recv(("z", way, lane, step), self.land.at[n], way)
        return self.land[n].astype(F32)

    def step(self, step):
        for lane in ("o", "x"):
            for way in ("+", "-"):
                top = self.limit(way, lane)
                if step > top:
                    continue
                left = top - step + 1
                d = left if way == "+" or left == 4 else -left
                total = self.own(d, lane)
                if step > 1:
                    total = total + self.landed(way, lane, step - 1)
                n = self.at[way, lane, step]
                self.stage[n] = total.astype(BF)
                self.net.send(("z", way, lane, step), self.stage.at[n], way, self.land.at[n])

    def across(self):
        total = self.own(0, "x")
        for way in ("+", "-"):
            total = total + self.landed(way, "x", self.limit(way, "x"))
        self.ys[...] = total.astype(BF)
        self.net.send("y", self.ys, "y", self.yr)

    def result(self):
        total = self.own(0, "o")
        for way in ("+", "-"):
            total = total + self.landed(way, "o", self.limit(way, "o"))
        self.net.recv("y", self.yr, "y")
        return total + self.yr[...].astype(F32)


def kernel(
    q_hbm,
    k_hbm,
    v_hbm,
    seg_hbm,
    start_hbm,
    len_hbm,
    w_hbm,
    gain_hbm,
    gate_hbm,
    up_hbm,
    down_hbm,
    cot_hbm,
    ctx_out,
    talker_out,
    grads_out,
    gk,
    gv,
    gr,
    gc,
    q_raw,
    q_buf,
    ctx_buf,
    w_buf,
    cot_buf,
    seg_buf,
    start_buf,
    len_buf,
    gain_buf,
    gate_w,
    up_w,
    down_w,
    segq,
    bias,
    m_buf,
    acc_buf,
    own_buf,
    out_buf,
    hid,
    d_gate,
    d_up,
    hid_rows,
    g32,
    res,
    a1_refs,
    a2_refs,
    b1_refs,
    b2_refs,
    part,
    from_core,
    stage,
    land,
    ys,
    yr,
    send_sems,
    recv_sems,
    local_sems,
):
    net = Net(send_sems, recv_sems)
    z, r = net.z, net.r

    def load(n, src, dst):
        copy = pltpu.make_async_copy(src, dst, local_sems.at[n])
        copy.start()
        return copy

    at_k = pl.ds(pl.multiple_of(r * KROWS, 16), TOK)
    at_aux = pl.ds(pl.multiple_of(r * KROWS + TOK, 16), AUX)
    at_v = pl.ds(pl.multiple_of(r * TOK, 16), TOK)
    at_row = pl.ds(pl.multiple_of(r * SLOTS, 16), SLOTS)
    load_seg = load(0, seg_hbm, seg_buf)
    load_k = load(1, k_hbm.at[0], gk.at[z, at_k])
    load_v = load(2, v_hbm.at[0], gv.at[z, at_v])
    load_q = load(3, q_hbm.at[0], q_raw)
    load_start = load(4, start_hbm, start_buf)
    load_len = load(5, len_hbm, len_buf)
    load_cot = load(6, cot_hbm.at[0], cot_buf)
    load_w = load(7, w_hbm, w_buf)
    load_gain = load(8, gain_hbm, gain_buf)
    load_ffn = [
        load(9, gate_hbm, gate_w),
        load(10, up_hbm, up_w),
        load(11, down_hbm, down_w),
    ]

    barrier = pltpu.get_barrier_semaphore()
    places = ("+", "-", "y", "c", "x+", "x-", "h")
    net.greet(barrier, places)

    load_seg.wait()
    seg_row = seg_buf[...].astype(F32)
    gk[z, at_aux, 0:D] = jnp.broadcast_to(seg_row, (AUX, D)).astype(BF)
    gk[z, at_aux, D : 2 * D] = jnp.zeros((AUX, D), BF)

    keys = Gather(net, "k", gk, True, KROWS)
    vals = Gather(net, "v", gv, False, TOK)
    rows = Gather(net, "r", gr, True, SLOTS)
    cots = Gather(net, "g", gc, False, SLOTS)

    load_k.wait()
    load_v.wait()
    pl.semaphore_wait(barrier, len(places))
    keys.start()
    vals.start()

    segq[...] = jnp.transpose(jnp.broadcast_to(seg_row, (TOK, D)))
    m_buf[...] = jnp.full(m_buf.shape, NEG, F32)
    acc_buf[...] = jnp.zeros(acc_buf.shape, F32)
    load_q.wait()
    for h in range(HEADS):
        q_buf[h] = q_raw[:, h * D : (h + 1) * D]

    load_start.wait()
    load_len.wait()
    start = start_buf[0, net.ctx] - net.ctx * TOK
    length = len_buf[0, net.ctx]
    slot_id = lax.broadcasted_iota(jnp.int32, (SLOTS, TOK), 0)
    place = lax.broadcasted_iota(jnp.int32, (SLOTS, TOK), 1)
    packer = jnp.where((place - start == slot_id) & (slot_id < length), 1.0, 0.0).astype(BF)
    load_cot.wait()
    gc[z, at_row] = jnp.dot(packer, cot_buf[...], preferred_element_type=F32).astype(BF)
    for i in range(NZ):
        for buf in (gr, gc):
            buf[i, 4 * SLOTS :] = jnp.zeros((CHUNK - 4 * SLOTS, TD), BF)

    factor = math.log2(math.e) / math.sqrt(D)

    def attend(d):
        zc = net.zmod(d)

        def work():
            for b in range(4):
                aux = b * KROWS + TOK
                ok = segq[...] == gk[zc, aux : aux + AUX, 0:D].astype(F32)[0:1]
                if d == 0:
                    kpos = lax.broadcasted_iota(jnp.int32, (TOK, D), 1) + (b - r) * TOK
                    qpos = lax.broadcasted_iota(jnp.int32, (TOK, D), 0)
                    ok = ok & (kpos <= qpos)
                bias[:, b * TOK : (b + 1) * TOK] = jnp.where(ok, 0.0, NEG)

            def head(i, carry):
                for kv in range(KV_HEADS):
                    h = i + kv * GROUP
                    lanes = slice(kv * D, (kv + 1) * D)
                    kc = jnp.concatenate(
                        [gk[zc, b * KROWS : b * KROWS + TOK, lanes] for b in range(4)], axis=0
                    )
                    vc = jnp.concatenate([gv[zc, :, lanes], jnp.ones((4 * TOK, D), BF)], axis=1)
                    s = lax.dot_general(q_buf[h], kc, NT, preferred_element_type=F32)
                    s = s * factor + bias[...]
                    m_old = m_buf[h]
                    m_new = jnp.maximum(m_old, jnp.max(s, axis=1, keepdims=True))
                    p = jnp.exp2(s - jnp.concatenate([m_new] * 4, axis=1)).astype(BF)
                    alpha = jnp.exp2(m_old - m_new)
                    m_buf[h] = m_new
                    acc_buf[h] = acc_buf[h] * jnp.concatenate([alpha, alpha], axis=1) + jnp.dot(
                        p, vc, preferred_element_type=F32
                    )
                return carry

            lax.fori_loop(0, GROUP, head, 0, unroll=True)

        if d == 0:
            work()
        else:
            pl.when(zc < z)(work)

    def attend_one(d):
        keys.from_core(d)
        vals.from_core(d)
        attend(d)

    def attend_step(step):
        for d in around(step):
            attend_one(d)

    vals.crosses(0)
    keys.cross(0)
    for step in range(1, 5):
        vals.ring(step, "o")
        keys.ring(step, "ox")
        if step == 3:
            cots.start()
        if step == 4:
            cots.ring(1, "o")
            cots.crosses(0)
            attend_one(-3)
            vals.crosses(4)
            attend_one(3)
        else:
            attend_step(step - 1)
            vals.crosses(step)
        net.settle()
    cots.ring(2, "o")
    cots.crosses(1)
    attend_step(4)

    for h in range(HEADS):
        acc = acc_buf[h]
        ctx_buf[:, h * D : (h + 1) * D] = (acc[:, 0:D] / acc[:, D : 2 * D]).astype(BF)
    load_w.wait()
    load_gain.wait()
    packed = jnp.dot(packer, ctx_buf[...], preferred_element_type=F32).astype(BF)
    own = jnp.dot(packed, w_buf[...], preferred_element_type=F32).astype(BF)
    own_buf[...] = own
    own = own.astype(F32)
    scale = lax.rsqrt(jnp.mean(own * own, axis=-1, keepdims=True) + 1e-06)
    gr[z, at_row] = (own * scale * gain_buf[...]).astype(BF)

    rows.start()
    save_ctx = load(12, ctx_buf, ctx_out)
    for wait in load_ffn:
        wait.wait()

    def ffn_in(d):
        rows.from_core(d)
        cots.from_core(d)
        zc = net.zmod(d)
        at = pl.ds(pl.multiple_of(zc * CHUNK, CHUNK), CHUNK)
        row = gr[zc]
        gate = lax.dot_general(gate_w[...], row, NT, preferred_element_type=F32)
        up = lax.dot_general(up_w[...], row, NT, preferred_element_type=F32)
        d_hidden = lax.dot_general(down_w[...], gc[zc], NT, preferred_element_type=F32)
        sig = jax.nn.sigmoid(gate)
        act = gate * sig
        hidden = act * up
        hid[:, at] = hidden.astype(BF)
        hid_rows[zc] = jnp.transpose(hidden).astype(BF)
        d_gate[:, at] = (d_hidden * up * sig * (1.0 + gate * (1.0 - sig))).astype(BF)
        d_up[:, at] = (d_hidden * act).astype(BF)

    cots.ring(3, "o")
    cots.crosses(2)
    rows.cross(0)
    cots.ring(4, "o")
    cots.crosses(3)
    sums = RowSum(net, part, from_core, stage, land, ys, yr)

    def ffn_out(*shifts):
        for d in shifts:
            zc = net.zmod(d)
            total = jnp.dot(
                hid_rows[zc, 0 : 4 * SLOTS], down_w[...], preferred_element_type=F32
            ).astype(BF)
            for b in range(4):
                part[b % 2, zc, b // 2] = total[b * SLOTS : (b + 1) * SLOTS]
            sums.swap(d)

    rows.ring(1, "ox")
    ffn_in(0)
    ffn_out(0)
    net.settle()
    rows.ring(2, "ox")
    cots.crosses(4)
    ffn_in(-1)
    ffn_in(1)
    ffn_out(-1, 1)
    net.settle()
    rows.ring(3, "ox")
    ffn_in(-2)
    ffn_in(2)
    net.settle()
    rows.ring(4, "ox")
    ffn_in(-3)
    ffn_in(3)
    ffn_in(4)

    b1 = HFirst(net, "b1", g32, res, 0, 32, b1_refs)
    a1 = XFirst(net, "a1", g32, res, 256, 32, a1_refs)
    a2 = XFirst(net, "a2", g32, res, 512, 32, a2_refs)
    b2 = HFirst(net, "b2", g32, res, 768, 16, b2_refs)

    def grad(n, left, right):
        g32[n * FFD : (n + 1) * FFD] = jnp.dot(
            left[...], right[...].reshape(NZ * CHUNK, TD), preferred_element_type=F32
        )

    def swapped(*shifts):
        for d in shifts:
            sums.swapped(d)

    grad(0, hid, gc)
    b1.start()
    grad(1, d_gate, gr)
    a1.start()
    g32[3 * FFD :] = jnp.zeros((GROWS - 3 * FFD, TD), F32)
    grad(2, d_up, gr)
    a2.start()
    b2.start()
    ffn_out(4, 3, -3)
    b1.cross_far()
    a1.relay()
    ffn_out(2, -2)
    a2.relay()
    swapped(4, 3, -3)
    sums.step(1)
    b1.cross()
    b2.cross_far()
    a1.cross()
    b1.relay()
    b2.cross()
    a2.cross()
    swapped(2, -2)
    sums.step(2)
    net.settle()
    b2.relay()
    b1.final()
    a1.final()
    swapped(1, -1, 0)
    sums.step(3)
    b1.forward()
    a2.final()
    b2.final()
    net.settle()
    a1.spread()
    b1.spread()
    b2.forward()
    sums.step(4)
    a2.spread()
    a1.forward()
    b2.spread()
    a2.forward()
    sums.across()
    net.settle()

    place = lax.broadcasted_iota(jnp.int32, (TOK, SLOTS), 0)
    slot_id = lax.broadcasted_iota(jnp.int32, (TOK, SLOTS), 1)
    spread = jnp.where((place - start == slot_id) & (slot_id < length), 1.0, 0.0).astype(BF)
    out_rows = (own_buf[...].astype(F32) + sums.result()).astype(BF)
    out_buf[...] = jnp.dot(spread, out_rows, preferred_element_type=F32).astype(BF)
    save_out = load(13, out_buf, talker_out)

    for grads in (b1, a1, b2, a2):
        grads.end()
    save_grads = load(14, res, grads_out)
    net.drain()
    for save in (save_ctx, save_out, save_grads):
        save.wait()


def x_first(size):
    shapes = ((NX, 2, size, TD), (6, size, TD), (2, size, TD), (size, TD), (size, TD))
    return [pltpu.VMEM(shape, BF) for shape in shapes]


def h_first(size):
    piece = pltpu.VMEM((NX, size, TD), BF)
    return [
        piece,
        piece,
        pltpu.VMEM((NX, size, TD), F32),
        piece,
        pltpu.VMEM((6, size, TD), BF),
        pltpu.VMEM((2, size, TD), BF),
    ]


def fused(*args):
    hbm = pl.BlockSpec(memory_space=pl.ANY)
    scratch = (
        ((NZ, 4 * KROWS, KW), BF),
        ((NZ, 4 * TOK, KW), BF),
        ((NZ, CHUNK, TD), BF),
        ((NZ, CHUNK, TD), BF),
        ((TOK, QW), BF),
        ((HEADS, TOK, D), BF),
        ((TOK, QW), BF),
        ((QW, TD), BF),
        ((TOK, TD), BF),
        ((1, TOK), jnp.int32),
        pltpu.SMEM((1, 32), jnp.int32),
        pltpu.SMEM((1, 32), jnp.int32),
        ((TD,), F32),
        ((FFD, TD), BF),
        ((FFD, TD), BF),
        ((FFD, TD), BF),
        ((TOK, D), F32),
        ((TOK, 4 * TOK), F32),
        ((HEADS, TOK, D), F32),
        ((HEADS, TOK, 2 * D), F32),
        ((SLOTS, TD), BF),
        ((TOK, TD), BF),
        ((FFD, NZ * CHUNK), BF),
        ((FFD, NZ * CHUNK), BF),
        ((FFD, NZ * CHUNK), BF),
        ((NZ, CHUNK, FFD), BF),
        ((GROWS, TD), F32),
        ((GROWS, TD), BF),
        x_first(32),
        x_first(32),
        h_first(32),
        h_first(16),
        ((2, NZ, 2, SLOTS, TD), BF),
        ((NZ, 2, SLOTS, TD), BF),
        ((14, SLOTS, TD), BF),
        ((14, SLOTS, TD), BF),
        ((SLOTS, TD), BF),
        ((SLOTS, TD), BF),
        pltpu.SemaphoreType.DMA((256,)),
        pltpu.SemaphoreType.DMA((256,)),
        pltpu.SemaphoreType.DMA((16,)),
    )
    return pl.pallas_call(
        kernel,
        name="mega",
        out_shape=[
            jax.ShapeDtypeStruct((TOK, QW), BF),
            jax.ShapeDtypeStruct((TOK, TD), BF),
            jax.ShapeDtypeStruct((GROWS, TD), BF),
        ],
        in_specs=[hbm] * len(args),
        out_specs=[hbm] * 3,
        scratch_shapes=[pltpu.VMEM(*s) if isinstance(s, tuple) else s for s in scratch],
        compiler_params=pltpu.CompilerParams(
            collective_id=1, has_side_effects=True, vmem_limit_bytes=VMEM_LIMIT
        ),
    )(*args)


def finish_kernel(ctx_in, talker_in, grads_in, ctx_out, talker_out, down_out, gate_out, up_out, low, wide, ctx_buf, talker_buf, sems):
    def move(n, src, dst):
        copy = pltpu.make_async_copy(src, dst, sems.at[n])
        copy.start()
        return copy

    step = 128
    loads = [
        move(n, grads_in.at[pl.ds(n * step, step)], low.at[pl.ds(n * step, step)])
        for n in range(GROWS // step)
    ]
    hops = [
        (move(7, ctx_in, ctx_buf), 12, ctx_buf, ctx_out.at[0]),
        (move(8, talker_in, talker_buf), 13, talker_buf, talker_out.at[0]),
    ]
    moves = []
    for hop, n, src, dst in hops:
        hop.wait()
        moves.append(move(n, src, dst))
    outs = [down_out, gate_out, up_out]
    for n, load in enumerate(loads):
        load.wait()
        wide[n * step : (n + 1) * step] = low[n * step : (n + 1) * step].astype(F32)
        done = 3 - len(outs)
        if outs and (n + 1) * step >= (done + 1) * FFD:
            moves.append(move(9 + done, wide.at[pl.ds(done * FFD, FFD)], outs.pop(0)))
    for copy in moves:
        copy.wait()


def finish(context, talker, grads):
    hbm = pl.BlockSpec(memory_space=pl.ANY)
    grad = jax.ShapeDtypeStruct((FFD, TD), F32)
    return pl.pallas_call(
        finish_kernel,
        name="finish",
        out_shape=[
            jax.ShapeDtypeStruct((1, TOK, QW), BF),
            jax.ShapeDtypeStruct((1, TOK, TD), BF),
            grad,
            grad,
            grad,
        ],
        in_specs=[hbm] * 3,
        out_specs=[hbm] * 5,
        scratch_shapes=[
            pltpu.VMEM((GROWS, TD), BF),
            pltpu.VMEM((GROWS, TD), F32),
            pltpu.VMEM((TOK, QW), BF),
            pltpu.VMEM((TOK, TD), BF),
            pltpu.SemaphoreType.DMA((16,)),
        ],
        compiler_params=pltpu.CompilerParams(vmem_limit_bytes=VMEM_LIMIT),
    )(context, talker, grads)


def shards(*args):
    context, talker, grad_down, grad_gate, grad_up = finish(*fused(*args))
    return (context, talker, grad_gate, grad_up, grad_down)


def solution(mesh):
    in_specs = (
        P("grp", "ctx", None),
        P("grp", "ctx", None),
        P("grp", "ctx", None),
        P("grp", "ctx"),
        P("grp", None),
        P("grp", None),
        P(),
        P(),
        P("ctx", None),
        P("ctx", None),
        P("ctx", None),
        P("grp", "ctx", None),
    )
    out_specs = (
        P("grp", "ctx", None),
        P("grp", "ctx", None),
        P("ctx", None),
        P("ctx", None),
        P("ctx", None),
    )
    return jax.shard_map(shards, mesh=mesh, in_specs=in_specs, out_specs=out_specs, check_vma=False)
```

```python
import math

import jax
import jax.numpy as jnp
from jax import lax
from jax.experimental import pallas as pl
from jax.experimental.pallas import tpu as pltpu
from jax.sharding import PartitionSpec as P

HEADS = 14
KV_HEADS = 2
GROUP = HEADS // KV_HEADS
D = 128
TOK = 128
TD = 896
QW = HEADS * D
KW = KV_HEADS * D
SLOTS = 48
NZ = 8
NX = 4
FFD = 296
GROWS = 896
AUX = 16
CHUNK = 256
KROWS = TOK + AUX
NEG = -1e30
MESH = pl.DeviceIdType.MESH
BF = jnp.bfloat16
F32 = jnp.float32
NT = (((1,), (1,)), ((), ()))
VMEM_LIMIT = 63 << 20


class Net:
    def __init__(self, send_sems, recv_sems):
        c = lax.axis_index("ctx")
        g = lax.axis_index("grp")
        self.ctx = c
        self.z = c // 4
        self.r = c % 4
        self.y = self.r // 2
        self.k = self.r % 2
        self.x = g // 2
        self.h = g % 2
        self.send_sems = send_sems
        self.recv_sems = recv_sems
        self.ids = {}
        self.sent = []
        self.older = []

    def zmod(self, d):
        return lax.rem(self.z + d + NZ, NZ)

    def xmod(self, d):
        return lax.rem(self.x + d + NX, NX)

    def dev(self, where):
        z, y, k, x, h = self.z, self.y, self.k, self.x, self.h
        if where == "+":
            z = self.zmod(1)
        elif where == "-":
            z = self.zmod(-1)
        elif where == "y":
            y = 1 - y
        elif where == "c":
            k = 1 - k
        elif where == "x+":
            x = self.xmod(1)
        elif where == "x-":
            x = self.xmod(-1)
        elif where == "h":
            h = 1 - h
        return (z * 4 + y * 2 + k, x * 2 + h)

    def greet(self, barrier, places):
        for where in places:
            pl.semaphore_signal(
                barrier, inc=1, device_id=self.dev(where), device_id_type=MESH
            )

    def copy(self, key, src, dst, where):
        n = self.ids.setdefault(key, len(self.ids))
        return pltpu.make_async_remote_copy(
            src_ref=src,
            dst_ref=dst,
            send_sem=self.send_sems.at[n],
            recv_sem=self.recv_sems.at[n],
            device_id=self.dev(where),
            device_id_type=MESH,
        )

    def send(self, key, src, where, dst=None):
        copy = self.copy(key, src, src if dst is None else dst, where)
        copy.start()
        self.sent.append(copy)

    def recv(self, key, ref, where):
        self.copy(key, ref, ref, where).wait_recv()

    def settle(self):
        for copy in self.older:
            copy.wait_send()
        self.older, self.sent = self.sent, []

    def drain(self):
        self.settle()
        self.settle()


class Gather:
    def __init__(self, net, name, buf, early, size):
        self.net, self.name, self.buf, self.early, self.size = net, name, buf, early, size

    def slot(self, d, lane, other_core=False):
        net = self.net
        y = net.y if lane == "o" else 1 - net.y
        k = 1 - net.k if other_core else net.k
        return self.buf.at[net.zmod(d), pl.ds(pl.multiple_of((y * 2 + k) * self.size, 16), self.size)]

    def limit(self, way, lane):
        return 4 if (way == "+") == (lane == "o") else 3

    def to_core(self, d, lane):
        self.net.send((self.name, "c", d, lane), self.slot(d, lane), "c")

    def to_z(self, way, lane, step):
        d = -(step - 1) if way == "+" else step - 1
        self.net.send((self.name, way, lane, step), self.slot(d, lane), way)

    def to_y(self, d):
        self.net.send((self.name, "y", d), self.slot(d, "o"), "y")

    def start(self):
        if self.early:
            self.to_y(0)
        self.to_z("+", "o", 1)
        self.to_z("-", "o", 1)
        if not self.early:
            self.to_y(0)
        self.to_core(0, "o")

    def cross(self, d):
        self.net.recv((self.name, "y", d), self.slot(d, "x"), "y")
        if self.early:
            self.to_z("+", "x", 1)
            self.to_z("-", "x", 1)
        self.to_core(d, "x")

    def arrive(self, way, lane, step):
        top = self.limit(way, lane)
        if step > top:
            return
        d = -step if way == "+" else step
        if d == -4:
            d = 4
        self.net.recv((self.name, way, lane, step), self.slot(d, lane), way)
        if step < top:
            self.to_z(way, lane, step + 1)
        if not self.early:
            self.to_y(d)
        self.to_core(d, lane)

    def ring(self, step, lanes):
        for lane in lanes:
            for way in ("+", "-"):
                self.arrive(way, lane, step)

    def crosses(self, step):
        if not self.early:
            for d in around(step):
                self.cross(d)

    def from_core(self, d):
        for lane in ("o", "x"):
            self.net.recv(
                (self.name, "c", d, lane), self.slot(d, lane, other_core=True), "c"
            )


def around(step):
    if step == 0:
        return (0,)
    if step == 4:
        return (4,)
    return (-step, step)


class GradSum:
    def __init__(self, net, name, g32, res, base, size, refs):
        self.net, self.name, self.g32, self.res = net, name, g32, res
        self.base, self.size = base, size
        self.refs = refs

    def send(self, key, src, where, dst=None):
        self.net.send((self.name, key), src, where, dst)

    def recv(self, key, ref, where):
        self.net.recv((self.name, key), ref, where)


class XFirst(GradSum):
    def rows(self, x, h):
        return pl.ds(pl.multiple_of(self.base + (x * 2 + h) * self.size, 16), self.size)

    def start(self):
        net = self.net
        first, land = self.refs[:2]
        for i in range(NX):
            for h in range(2):
                at = self.base + (i * 2 + h) * self.size
                first[i, h] = self.g32[at : at + self.size].astype(BF)
        far = net.xmod(2)
        self.send("1+", first.at[far, 0], "x+", land.at[0])
        self.send("1-", first.at[far, 1], "x-", land.at[1])
        self.send("2+", first.at[net.xmod(1), 1], "x+", land.at[2])
        self.send("2-", first.at[net.xmod(-1), 0], "x-", land.at[3])

    def relay(self):
        net = self.net
        land, second = self.refs[1:3]
        for n, (way, d, half) in enumerate((("+", 1, 0), ("-", -1, 1))):
            self.recv("1" + way, land.at[n], "x" + way)
            own = self.g32[self.rows(net.xmod(d), half)]
            second[n] = (own + land[n].astype(F32)).astype(BF)
            self.send("3" + way, second.at[n], "x" + way, land.at[4 + n])

    def cross(self):
        net = self.net
        land, _, over, back = self.refs[1:]
        self.recv("2+", land.at[2], "x+")
        self.recv("2-", land.at[3], "x-")
        self.recv("3+", land.at[4], "x+")
        self.recv("3-", land.at[5], "x-")
        for half, (one, two) in enumerate(((3, 4), (2, 5))):
            rows = self.rows(net.x, half)
            self.g32[rows] = self.g32[rows] + land[one].astype(F32) + land[two].astype(F32)
        over[...] = self.g32[self.rows(net.x, 1 - net.h)].astype(BF)
        self.send("h", over, "h", back)

    def final(self):
        net = self.net
        back = self.refs[4]
        self.recv("h", back, "h")
        rows = self.rows(net.x, net.h)
        self.res[rows] = (self.g32[rows] + back[...].astype(F32)).astype(BF)
        for key, where in (("e0", "h"), ("e1+", "x+"), ("e1-", "x-")):
            self.send(key, self.res.at[rows], where)

    def spread(self):
        net = self.net
        rows = self.res.at[self.rows(net.x, 1 - net.h)]
        self.recv("e0", rows, "h")
        self.send("e2+", rows, "x+")
        self.send("e2-", rows, "x-")

    def forward(self):
        net = self.net
        for way, d, half in (("+", -1, 0), ("-", 1, 1)):
            x = net.xmod(d)
            self.recv("e1" + way, self.res.at[self.rows(x, net.h)], "x" + way)
            self.recv("e2" + way, self.res.at[self.rows(x, 1 - net.h)], "x" + way)
            self.send("f" + way, self.res.at[self.rows(x, half)], "x" + way)

    def end(self):
        net = self.net
        for way, half in (("+", 0), ("-", 1)):
            self.recv("f" + way, self.res.at[self.rows(net.xmod(2), half)], "x" + way)


class HFirst(GradSum):
    def part(self, half):
        low = self.size // 32 * 16 or self.size
        return (0, low) if half == 0 else (low, self.size - low)

    def rows(self, h, x, half=None):
        at, size = (0, self.size) if half is None else self.part(half)
        return pl.ds(pl.multiple_of(self.base + (h * NX + x) * self.size + at, 16), size)

    def ways(self, plan):
        return [m for m in plan if self.part(m[-1])[1]]

    def start(self):
        net = self.net
        first, land = self.refs[:2]
        for i in range(NX):
            first[i] = self.g32[self.rows(1 - net.h, i)].astype(BF)
        for d in (2, 1, -1, 0):
            x = net.xmod(d)
            self.send(("0", d), first.at[x], "h", land.at[x])

    def pair(self, d):
        net = self.net
        back, total, second = self.refs[1:4]
        x = net.xmod(d)
        self.recv(("0", d), back.at[x], "h")
        value = self.g32[self.rows(net.h, x)] + back[x].astype(F32)
        total[x] = value
        second[x] = value.astype(BF)

    def pass_on(self, n, key, way, d, half):
        second, ring = self.refs[3:5]
        if self.part(half)[1]:
            at = pl.ds(*self.part(half))
            self.send(key, second.at[self.net.xmod(d), at], "x" + way, ring.at[n, at])

    def cross_far(self):
        self.pair(2)
        self.pass_on(0, "1+", "+", 2, 0)
        self.pass_on(1, "1-", "-", 2, 1)

    def cross(self):
        self.pair(1)
        self.pass_on(2, "2+", "+", 1, 1)
        self.pair(-1)
        self.pass_on(3, "2-", "-", -1, 0)
        self.pair(0)

    def relay(self):
        net = self.net
        total, _, ring, third = self.refs[2:]
        for n, way, d, half in self.ways(((0, "+", 1, 0), (1, "-", -1, 1))):
            at = pl.ds(*self.part(half))
            self.recv("1" + way, ring.at[n, at], "x" + way)
            third[n, at] = (total[net.xmod(d), at] + ring[n, at].astype(F32)).astype(BF)
            self.send("3" + way, third.at[n, at], "x" + way, ring.at[4 + n, at])

    def final(self):
        net = self.net
        total, _, ring = self.refs[2:5]
        plan = ((2, "2+", "+", 1), (3, "2-", "-", 0), (4, "3+", "+", 0), (5, "3-", "-", 1))
        for n, key, way, half in self.ways(plan):
            self.recv(key, ring.at[n, pl.ds(*self.part(half))], "x" + way)
        for one, two, half in self.ways(((3, 4, 0), (2, 5, 1))):
            at = pl.ds(*self.part(half))
            value = total[net.x, at] + ring[one, at].astype(F32) + ring[two, at].astype(F32)
            self.res[self.rows(net.h, net.x, half)] = value.astype(BF)
        rows = self.res.at[self.rows(net.h, net.x)]
        for key, where in (("q+", "x+"), ("q-", "x-"), ("p0", "h")):
            self.send(key, rows, where)

    def forward(self):
        net = self.net
        for n, (way, d, half) in enumerate((("+", -1, 0), ("-", 1, 1))):
            x = net.xmod(d)
            rows = self.res.at[self.rows(net.h, x)]
            self.recv("q" + way, rows, "x" + way)
            if self.part(half)[1]:
                self.send("s" + way, self.res.at[self.rows(net.h, x, half)], "x" + way)
            self.send("p%d" % (n + 1), rows, "h")

    def spread(self):
        net = self.net
        x = net.xmod(2)
        for way, half in self.ways((("+", 0), ("-", 1))):
            self.recv("s" + way, self.res.at[self.rows(net.h, x, half)], "x" + way)
        self.send("p3", self.res.at[self.rows(net.h, x)], "h")

    def end(self):
        net = self.net
        for n, d in enumerate((0, -1, 1, 2)):
            self.recv("p%d" % n, self.res.at[self.rows(1 - net.h, net.xmod(d))], "h")


class RowSum:
    def __init__(self, net, part, from_core, stage, land, ys, yr):
        self.net, self.part, self.from_core = net, part, from_core
        self.stage, self.land, self.ys, self.yr = stage, land, ys, yr
        self.at = {}
        for way in ("+", "-"):
            for lane in ("o", "x"):
                for step in range(1, self.limit(way, lane) + 1):
                    self.at[way, lane, step] = len(self.at)

    def limit(self, way, lane):
        return 4 if (way == "+") == (lane == "o") else 3

    def swap(self, d):
        net = self.net
        z = net.zmod(d)
        net.send(("c", d), self.part.at[1 - net.k, z], "c", self.from_core.at[z])

    def swapped(self, d):
        self.net.recv(("c", d), self.from_core.at[self.net.zmod(d)], "c")

    def own(self, d, lane):
        net = self.net
        z = net.zmod(d)
        y = net.y if lane == "o" else 1 - net.y
        return self.part[net.k, z, y].astype(F32) + self.from_core[z, y].astype(F32)

    def landed(self, way, lane, step):
        n = self.at[way, lane, step]
        self.net.recv(("z", way, lane, step), self.land.at[n], way)
        return self.land[n].astype(F32)

    def step(self, step):
        for lane in ("o", "x"):
            for way in ("+", "-"):
                top = self.limit(way, lane)
                if step > top:
                    continue
                left = top - step + 1
                d = left if way == "+" or left == 4 else -left
                total = self.own(d, lane)
                if step > 1:
                    total = total + self.landed(way, lane, step - 1)
                n = self.at[way, lane, step]
                self.stage[n] = total.astype(BF)
                self.net.send(("z", way, lane, step), self.stage.at[n], way, self.land.at[n])

    def across(self):
        total = self.own(0, "x")
        for way in ("+", "-"):
            total = total + self.landed(way, "x", self.limit(way, "x"))
        self.ys[...] = total.astype(BF)
        self.net.send("y", self.ys, "y", self.yr)

    def result(self):
        total = self.own(0, "o")
        for way in ("+", "-"):
            total = total + self.landed(way, "o", self.limit(way, "o"))
        self.net.recv("y", self.yr, "y")
        return total + self.yr[...].astype(F32)


def kernel(
    q_hbm,
    k_hbm,
    v_hbm,
    seg_hbm,
    start_hbm,
    len_hbm,
    w_hbm,
    gain_hbm,
    gate_hbm,
    up_hbm,
    down_hbm,
    cot_hbm,
    ctx_out,
    talker_out,
    grads_out,
    gk,
    gv,
    gr,
    gc,
    q_raw,
    q_buf,
    ctx_buf,
    w_buf,
    cot_buf,
    seg_buf,
    start_buf,
    len_buf,
    gain_buf,
    gate_w,
    up_w,
    down_w,
    segq,
    bias,
    m_buf,
    acc_buf,
    own_buf,
    out_buf,
    hid,
    d_gate,
    d_up,
    hid_rows,
    g32,
    res,
    b1_refs,
    a1_refs,
    a2_refs,
    b2_refs,
    a3_refs,
    part,
    from_core,
    stage,
    land,
    ys,
    yr,
    send_sems,
    recv_sems,
    local_sems,
):
    net = Net(send_sems, recv_sems)
    z, r = net.z, net.r

    def load(n, src, dst):
        copy = pltpu.make_async_copy(src, dst, local_sems.at[n])
        copy.start()
        return copy

    at_k = pl.ds(pl.multiple_of(r * KROWS, 16), TOK)
    at_aux = pl.ds(pl.multiple_of(r * KROWS + TOK, 16), AUX)
    at_v = pl.ds(pl.multiple_of(r * TOK, 16), TOK)
    at_row = pl.ds(pl.multiple_of(r * SLOTS, 16), SLOTS)
    load_seg = load(0, seg_hbm, seg_buf)
    load_k = load(1, k_hbm.at[0], gk.at[z, at_k])
    load_v = load(2, v_hbm.at[0], gv.at[z, at_v])
    load_q = load(3, q_hbm.at[0], q_raw)
    load_start = load(4, start_hbm, start_buf)
    load_len = load(5, len_hbm, len_buf)
    load_cot = load(6, cot_hbm.at[0], cot_buf)
    load_w = load(7, w_hbm, w_buf)
    load_gain = load(8, gain_hbm, gain_buf)
    load_ffn = [
        load(9, gate_hbm, gate_w),
        load(10, up_hbm, up_w),
        load(11, down_hbm, down_w),
    ]

    barrier = pltpu.get_barrier_semaphore()
    places = ("+", "-", "y", "c", "x+", "x-", "h")
    net.greet(barrier, places)

    load_seg.wait()
    seg_row = seg_buf[...].astype(F32)
    gk[z, at_aux, 0:D] = jnp.broadcast_to(seg_row, (AUX, D)).astype(BF)
    gk[z, at_aux, D : 2 * D] = jnp.zeros((AUX, D), BF)

    keys = Gather(net, "k", gk, True, KROWS)
    vals = Gather(net, "v", gv, False, TOK)
    rows = Gather(net, "r", gr, True, SLOTS)
    cots = Gather(net, "g", gc, False, SLOTS)

    load_k.wait()
    load_v.wait()
    pl.semaphore_wait(barrier, len(places))
    keys.start()
    vals.start()

    segq[...] = jnp.transpose(jnp.broadcast_to(seg_row, (TOK, D)))
    m_buf[...] = jnp.full(m_buf.shape, NEG, F32)
    acc_buf[...] = jnp.zeros(acc_buf.shape, F32)
    load_q.wait()
    for h in range(HEADS):
        q_buf[h] = q_raw[:, h * D : (h + 1) * D]

    load_start.wait()
    load_len.wait()
    start = start_buf[0, net.ctx] - net.ctx * TOK
    length = len_buf[0, net.ctx]
    slot_id = lax.broadcasted_iota(jnp.int32, (SLOTS, TOK), 0)
    place = lax.broadcasted_iota(jnp.int32, (SLOTS, TOK), 1)
    packer = jnp.where((place - start == slot_id) & (slot_id < length), 1.0, 0.0).astype(BF)
    load_cot.wait()
    gc[z, at_row] = jnp.dot(packer, cot_buf[...], preferred_element_type=F32).astype(BF)
    for i in range(NZ):
        for buf in (gr, gc):
            buf[i, 4 * SLOTS :] = jnp.zeros((CHUNK - 4 * SLOTS, TD), BF)

    factor = math.log2(math.e) / math.sqrt(D)

    def attend(d):
        zc = net.zmod(d)

        def work():
            for b in range(4):
                aux = b * KROWS + TOK
                ok = segq[...] == gk[zc, aux : aux + AUX, 0:D].astype(F32)[0:1]
                if d == 0:
                    kpos = lax.broadcasted_iota(jnp.int32, (TOK, D), 1) + (b - r) * TOK
                    qpos = lax.broadcasted_iota(jnp.int32, (TOK, D), 0)
                    ok = ok & (kpos <= qpos)
                bias[:, b * TOK : (b + 1) * TOK] = jnp.where(ok, 0.0, NEG)

            def head(i, carry):
                for kv in range(KV_HEADS):
                    h = i + kv * GROUP
                    lanes = slice(kv * D, (kv + 1) * D)
                    kc = jnp.concatenate(
                        [gk[zc, b * KROWS : b * KROWS + TOK, lanes] for b in range(4)], axis=0
                    )
                    vc = jnp.concatenate([gv[zc, :, lanes], jnp.ones((4 * TOK, D), BF)], axis=1)
                    s = lax.dot_general(q_buf[h], kc, NT, preferred_element_type=F32)
                    s = s * factor + bias[...]
                    m_old = m_buf[h]
                    m_new = jnp.maximum(m_old, jnp.max(s, axis=1, keepdims=True))
                    p = jnp.exp2(s - jnp.concatenate([m_new] * 4, axis=1)).astype(BF)
                    alpha = jnp.exp2(m_old - m_new)
                    m_buf[h] = m_new
                    acc_buf[h] = acc_buf[h] * jnp.concatenate([alpha, alpha], axis=1) + jnp.dot(
                        p, vc, preferred_element_type=F32
                    )
                return carry

            lax.fori_loop(0, GROUP, head, 0, unroll=True)

        if d == 0:
            work()
        else:
            pl.when(zc < z)(work)

    def attend_one(d):
        keys.from_core(d)
        vals.from_core(d)
        attend(d)

    def attend_step(step):
        for d in around(step):
            attend_one(d)

    vals.crosses(0)
    keys.cross(0)
    for step in range(1, 5):
        vals.ring(step, "o")
        keys.ring(step, "ox")
        if step == 3:
            cots.start()
        if step == 4:
            cots.ring(1, "o")
            cots.crosses(0)
            attend_one(-3)
            vals.crosses(4)
            attend_one(3)
        else:
            attend_step(step - 1)
            vals.crosses(step)
        net.settle()
    cots.ring(2, "o")
    cots.crosses(1)
    attend_step(4)

    for h in range(HEADS):
        acc = acc_buf[h]
        ctx_buf[:, h * D : (h + 1) * D] = (acc[:, 0:D] / acc[:, D : 2 * D]).astype(BF)
    load_w.wait()
    load_gain.wait()
    packed = jnp.dot(packer, ctx_buf[...], preferred_element_type=F32).astype(BF)
    own = jnp.dot(packed, w_buf[...], preferred_element_type=F32).astype(BF)
    own_buf[...] = own
    own = own.astype(F32)
    scale = lax.rsqrt(jnp.mean(own * own, axis=-1, keepdims=True) + 1e-06)
    gr[z, at_row] = (own * scale * gain_buf[...]).astype(BF)

    rows.start()
    save_ctx = load(12, ctx_buf, ctx_out)
    for wait in load_ffn:
        wait.wait()

    def ffn_in(d):
        rows.from_core(d)
        cots.from_core(d)
        zc = net.zmod(d)
        at = pl.ds(pl.multiple_of(zc * CHUNK, CHUNK), CHUNK)
        row = gr[zc]
        gate = lax.dot_general(gate_w[...], row, NT, preferred_element_type=F32)
        up = lax.dot_general(up_w[...], row, NT, preferred_element_type=F32)
        d_hidden = lax.dot_general(down_w[...], gc[zc], NT, preferred_element_type=F32)
        sig = jax.nn.sigmoid(gate)
        act = gate * sig
        hidden = act * up
        hid[:, at] = hidden.astype(BF)
        hid_rows[zc] = jnp.transpose(hidden).astype(BF)
        d_gate[:, at] = (d_hidden * up * sig * (1.0 + gate * (1.0 - sig))).astype(BF)
        d_up[:, at] = (d_hidden * act).astype(BF)

    cots.ring(3, "o")
    cots.crosses(2)
    rows.cross(0)
    cots.ring(4, "o")
    cots.crosses(3)
    sums = RowSum(net, part, from_core, stage, land, ys, yr)

    def ffn_out(*shifts):
        for d in shifts:
            zc = net.zmod(d)
            total = jnp.dot(
                hid_rows[zc, 0 : 4 * SLOTS], down_w[...], preferred_element_type=F32
            ).astype(BF)
            for b in range(4):
                part[b % 2, zc, b // 2] = total[b * SLOTS : (b + 1) * SLOTS]
            sums.swap(d)

    rows.ring(1, "ox")
    ffn_in(0)
    ffn_out(0)
    net.settle()
    rows.ring(2, "ox")
    cots.crosses(4)
    ffn_in(-1)
    ffn_in(1)
    ffn_out(-1, 1)
    net.settle()
    rows.ring(3, "ox")
    ffn_in(-2)
    ffn_in(2)
    ffn_out(-2, 2)
    net.settle()
    rows.ring(4, "ox")
    ffn_in(-3)
    ffn_in(3)
    ffn_in(4)

    b1 = HFirst(net, "b1", g32, res, 0, 32, b1_refs)
    a1 = XFirst(net, "a1", g32, res, 256, 32, a1_refs)
    a2 = XFirst(net, "a2", g32, res, 512, 16, a2_refs)
    b2 = HFirst(net, "b2", g32, res, 640, 16, b2_refs)
    a3 = XFirst(net, "a3", g32, res, 768, 16, a3_refs)

    def grad(n, left, right):
        g32[n * FFD : (n + 1) * FFD] = jnp.dot(
            left[...], right[...].reshape(NZ * CHUNK, TD), preferred_element_type=F32
        )

    def swapped(*shifts):
        for d in shifts:
            sums.swapped(d)

    grad(0, hid, gc)
    b1.start()
    ffn_out(4, 3, -3)
    grad(1, d_gate, gr)
    a1.start()
    swapped(4, 3, -3)
    sums.step(1)
    g32[3 * FFD :] = jnp.zeros((GROWS - 3 * FFD, TD), F32)
    grad(2, d_up, gr)
    b2.start()
    a2.start()
    a3.start()
    b1.cross_far()
    a1.relay()
    swapped(2, -2)
    sums.step(2)
    a2.relay()
    a3.relay()
    b1.cross()
    net.settle()
    b1.relay()
    b2.cross_far()
    a1.cross()
    a2.cross()
    a3.cross()
    b2.cross()
    b2.relay()
    swapped(1, -1, 0)
    sums.step(3)
    b1.final()
    net.settle()
    a1.final()
    b2.final()
    a2.final()
    a3.final()
    b1.forward()
    sums.step(4)
    b2.forward()
    a1.spread()
    a2.spread()
    a3.spread()
    b1.spread()
    b2.spread()
    sums.across()
    net.settle()
    a2.forward()
    a3.forward()
    a1.forward()

    place = lax.broadcasted_iota(jnp.int32, (TOK, SLOTS), 0)
    slot_id = lax.broadcasted_iota(jnp.int32, (TOK, SLOTS), 1)
    spread = jnp.where((place - start == slot_id) & (slot_id < length), 1.0, 0.0).astype(BF)
    out_rows = (own_buf[...].astype(F32) + sums.result()).astype(BF)
    out_buf[...] = jnp.dot(spread, out_rows, preferred_element_type=F32).astype(BF)
    save_out = load(13, out_buf, talker_out)

    saves = [save_ctx, save_out]
    for n, grads in enumerate((b1, b2, a2, a3, a1)):
        grads.end()
        at = pl.ds(grads.base, 8 * grads.size)
        saves.append(load(14 + n, res.at[at], grads_out.at[at]))
    net.drain()
    for save in saves:
        save.wait()


def x_first(size):
    shapes = ((NX, 2, size, TD), (6, size, TD), (2, size, TD), (size, TD), (size, TD))
    return [pltpu.VMEM(shape, BF) for shape in shapes]


def h_first(size):
    piece = pltpu.VMEM((NX, size, TD), BF)
    return [
        piece,
        piece,
        pltpu.VMEM((NX, size, TD), F32),
        piece,
        pltpu.VMEM((6, size, TD), BF),
        pltpu.VMEM((2, size, TD), BF),
    ]


def fused(*args):
    hbm = pl.BlockSpec(memory_space=pl.ANY)
    scratch = (
        ((NZ, 4 * KROWS, KW), BF),
        ((NZ, 4 * TOK, KW), BF),
        ((NZ, CHUNK, TD), BF),
        ((NZ, CHUNK, TD), BF),
        ((TOK, QW), BF),
        ((HEADS, TOK, D), BF),
        ((TOK, QW), BF),
        ((QW, TD), BF),
        ((TOK, TD), BF),
        ((1, TOK), jnp.int32),
        pltpu.SMEM((1, 32), jnp.int32),
        pltpu.SMEM((1, 32), jnp.int32),
        ((TD,), F32),
        ((FFD, TD), BF),
        ((FFD, TD), BF),
        ((FFD, TD), BF),
        ((TOK, D), F32),
        ((TOK, 4 * TOK), F32),
        ((HEADS, TOK, D), F32),
        ((HEADS, TOK, 2 * D), F32),
        ((SLOTS, TD), BF),
        ((TOK, TD), BF),
        ((FFD, NZ * CHUNK), BF),
        ((FFD, NZ * CHUNK), BF),
        ((FFD, NZ * CHUNK), BF),
        ((NZ, CHUNK, FFD), BF),
        ((GROWS, TD), F32),
        ((GROWS, TD), BF),
        h_first(32),
        x_first(32),
        x_first(16),
        h_first(16),
        x_first(16),
        ((2, NZ, 2, SLOTS, TD), BF),
        ((NZ, 2, SLOTS, TD), BF),
        ((14, SLOTS, TD), BF),
        ((14, SLOTS, TD), BF),
        ((SLOTS, TD), BF),
        ((SLOTS, TD), BF),
        pltpu.SemaphoreType.DMA((256,)),
        pltpu.SemaphoreType.DMA((256,)),
        pltpu.SemaphoreType.DMA((24,)),
    )
    return pl.pallas_call(
        kernel,
        name="mega",
        out_shape=[
            jax.ShapeDtypeStruct((TOK, QW), BF),
            jax.ShapeDtypeStruct((TOK, TD), BF),
            jax.ShapeDtypeStruct((GROWS, TD), BF),
        ],
        in_specs=[hbm] * len(args),
        out_specs=[hbm] * 3,
        scratch_shapes=[pltpu.VMEM(*s) if isinstance(s, tuple) else s for s in scratch],
        compiler_params=pltpu.CompilerParams(
            collective_id=1, has_side_effects=True, vmem_limit_bytes=VMEM_LIMIT
        ),
    )(*args)


def finish_kernel(ctx_in, talker_in, grads_in, ctx_out, talker_out, down_out, gate_out, up_out, low, wide, ctx_buf, talker_buf, sems):
    def move(n, src, dst):
        copy = pltpu.make_async_copy(src, dst, sems.at[n])
        copy.start()
        return copy

    step = 128
    loads = [
        move(n, grads_in.at[pl.ds(n * step, step)], low.at[pl.ds(n * step, step)])
        for n in range(GROWS // step)
    ]
    hops = [
        (move(7, ctx_in, ctx_buf), 12, ctx_buf, ctx_out.at[0]),
        (move(8, talker_in, talker_buf), 13, talker_buf, talker_out.at[0]),
    ]
    moves = []
    for hop, n, src, dst in hops:
        hop.wait()
        moves.append(move(n, src, dst))
    outs = [down_out, gate_out, up_out]
    for n, load in enumerate(loads):
        load.wait()
        wide[n * step : (n + 1) * step] = low[n * step : (n + 1) * step].astype(F32)
        done = 3 - len(outs)
        if outs and (n + 1) * step >= (done + 1) * FFD:
            moves.append(move(9 + done, wide.at[pl.ds(done * FFD, FFD)], outs.pop(0)))
    for copy in moves:
        copy.wait()


def finish(context, talker, grads):
    hbm = pl.BlockSpec(memory_space=pl.ANY)
    grad = jax.ShapeDtypeStruct((FFD, TD), F32)
    return pl.pallas_call(
        finish_kernel,
        name="finish",
        out_shape=[
            jax.ShapeDtypeStruct((1, TOK, QW), BF),
            jax.ShapeDtypeStruct((1, TOK, TD), BF),
            grad,
            grad,
            grad,
        ],
        in_specs=[hbm] * 3,
        out_specs=[hbm] * 5,
        scratch_shapes=[
            pltpu.VMEM((GROWS, TD), BF),
            pltpu.VMEM((GROWS, TD), F32),
            pltpu.VMEM((TOK, QW), BF),
            pltpu.VMEM((TOK, TD), BF),
            pltpu.SemaphoreType.DMA((16,)),
        ],
        compiler_params=pltpu.CompilerParams(vmem_limit_bytes=VMEM_LIMIT),
    )(context, talker, grads)


def shards(*args):
    context, talker, grad_down, grad_gate, grad_up = finish(*fused(*args))
    return (context, talker, grad_gate, grad_up, grad_down)


def solution(mesh):
    in_specs = (
        P("grp", "ctx", None),
        P("grp", "ctx", None),
        P("grp", "ctx", None),
        P("grp", "ctx"),
        P("grp", None),
        P("grp", None),
        P(),
        P(),
        P("ctx", None),
        P("ctx", None),
        P("ctx", None),
        P("grp", "ctx", None),
    )
    out_specs = (
        P("grp", "ctx", None),
        P("grp", "ctx", None),
        P("ctx", None),
        P("ctx", None),
        P("ctx", None),
    )
    return jax.shard_map(shards, mesh=mesh, in_specs=in_specs, out_specs=out_specs, check_vma=False)
```

```python
import math

import jax
import jax.numpy as jnp
from jax import lax
from jax.experimental import pallas as pl
from jax.experimental.pallas import tpu as pltpu
from jax.sharding import PartitionSpec as P

HEADS = 14
KV_HEADS = 2
GROUP = HEADS // KV_HEADS
D = 128
TOK = 128
TD = 896
QW = HEADS * D
KW = KV_HEADS * D
SLOTS = 48
NZ = 8
NX = 4
FFD = 296
GROWS = 896
AUX = 16
CHUNK = 256
KROWS = TOK + AUX
NEG = -1e30
MESH = pl.DeviceIdType.MESH
BF = jnp.bfloat16
F32 = jnp.float32
NT = (((1,), (1,)), ((), ()))
VMEM_LIMIT = 63 << 20


class Net:
    def __init__(self, send_sems, recv_sems):
        c = lax.axis_index("ctx")
        g = lax.axis_index("grp")
        self.ctx = c
        self.z = c // 4
        self.r = c % 4
        self.y = self.r // 2
        self.k = self.r % 2
        self.x = g // 2
        self.h = g % 2
        self.send_sems = send_sems
        self.recv_sems = recv_sems
        self.ids = {}
        self.sent = []
        self.older = []

    def zmod(self, d):
        return lax.rem(self.z + d + NZ, NZ)

    def xmod(self, d):
        return lax.rem(self.x + d + NX, NX)

    def dev(self, where):
        z, y, k, x, h = self.z, self.y, self.k, self.x, self.h
        if where == "+":
            z = self.zmod(1)
        elif where == "-":
            z = self.zmod(-1)
        elif where == "y":
            y = 1 - y
        elif where == "c":
            k = 1 - k
        elif where == "x+":
            x = self.xmod(1)
        elif where == "x-":
            x = self.xmod(-1)
        elif where == "h":
            h = 1 - h
        return (z * 4 + y * 2 + k, x * 2 + h)

    def greet(self, barrier, places):
        for where in places:
            pl.semaphore_signal(
                barrier, inc=1, device_id=self.dev(where), device_id_type=MESH
            )

    def copy(self, key, src, dst, where):
        n = self.ids.setdefault(key, len(self.ids))
        return pltpu.make_async_remote_copy(
            src_ref=src,
            dst_ref=dst,
            send_sem=self.send_sems.at[n],
            recv_sem=self.recv_sems.at[n],
            device_id=self.dev(where),
            device_id_type=MESH,
        )

    def send(self, key, src, where, dst=None):
        copy = self.copy(key, src, src if dst is None else dst, where)
        copy.start()
        self.sent.append(copy)

    def recv(self, key, ref, where):
        self.copy(key, ref, ref, where).wait_recv()

    def settle(self):
        for copy in self.older:
            copy.wait_send()
        self.older, self.sent = self.sent, []

    def drain(self):
        self.settle()
        self.settle()


class Gather:
    def __init__(self, net, name, buf, early, size):
        self.net, self.name, self.buf, self.early, self.size = net, name, buf, early, size

    def slot(self, d, lane, other_core=False):
        net = self.net
        y = net.y if lane == "o" else 1 - net.y
        k = 1 - net.k if other_core else net.k
        return self.buf.at[net.zmod(d), pl.ds(pl.multiple_of((y * 2 + k) * self.size, 16), self.size)]

    def limit(self, way, lane):
        return 4 if (way == "+") == (lane == "o") else 3

    def to_core(self, d, lane):
        self.net.send((self.name, "c", d, lane), self.slot(d, lane), "c")

    def to_z(self, way, lane, step):
        d = -(step - 1) if way == "+" else step - 1
        self.net.send((self.name, way, lane, step), self.slot(d, lane), way)

    def to_y(self, d):
        self.net.send((self.name, "y", d), self.slot(d, "o"), "y")

    def start(self):
        if self.early:
            self.to_y(0)
        self.to_z("+", "o", 1)
        self.to_z("-", "o", 1)
        if not self.early:
            self.to_y(0)
        self.to_core(0, "o")

    def cross(self, d):
        self.net.recv((self.name, "y", d), self.slot(d, "x"), "y")
        if self.early:
            self.to_z("+", "x", 1)
            self.to_z("-", "x", 1)
        self.to_core(d, "x")

    def arrive(self, way, lane, step):
        top = self.limit(way, lane)
        if step > top:
            return
        d = -step if way == "+" else step
        if d == -4:
            d = 4
        self.net.recv((self.name, way, lane, step), self.slot(d, lane), way)
        if step < top:
            self.to_z(way, lane, step + 1)
        if not self.early:
            self.to_y(d)
        self.to_core(d, lane)

    def ring(self, step, lanes):
        for lane in lanes:
            for way in ("+", "-"):
                self.arrive(way, lane, step)

    def crosses(self, step):
        if not self.early:
            for d in around(step):
                self.cross(d)

    def from_core(self, d):
        for lane in ("o", "x"):
            self.net.recv(
                (self.name, "c", d, lane), self.slot(d, lane, other_core=True), "c"
            )


def around(step):
    if step == 0:
        return (0,)
    if step == 4:
        return (4,)
    return (-step, step)


class GradSum:
    def __init__(self, net, name, g32, res, base, size, refs):
        self.net, self.name, self.g32, self.res = net, name, g32, res
        self.base, self.size = base, size
        self.refs = refs

    def send(self, key, src, where, dst=None):
        self.net.send((self.name, key), src, where, dst)

    def recv(self, key, ref, where):
        self.net.recv((self.name, key), ref, where)


class XFirst(GradSum):
    def rows(self, x, h):
        return pl.ds(pl.multiple_of(self.base + (x * 2 + h) * self.size, 16), self.size)

    def start(self):
        net = self.net
        first, land = self.refs[:2]
        for i in range(NX):
            for h in range(2):
                at = self.base + (i * 2 + h) * self.size
                first[i, h] = self.g32[at : at + self.size].astype(BF)
        far = net.xmod(2)
        self.send("1+", first.at[far, 0], "x+", land.at[0])
        self.send("1-", first.at[far, 1], "x-", land.at[1])
        self.send("2+", first.at[net.xmod(1), 1], "x+", land.at[2])
        self.send("2-", first.at[net.xmod(-1), 0], "x-", land.at[3])

    def relay(self):
        net = self.net
        land, second = self.refs[1:3]
        for n, (way, d, half) in enumerate((("+", 1, 0), ("-", -1, 1))):
            self.recv("1" + way, land.at[n], "x" + way)
            own = self.g32[self.rows(net.xmod(d), half)]
            second[n] = (own + land[n].astype(F32)).astype(BF)
            self.send("3" + way, second.at[n], "x" + way, land.at[4 + n])

    def cross(self):
        net = self.net
        land, _, over, back = self.refs[1:]
        self.recv("2+", land.at[2], "x+")
        self.recv("2-", land.at[3], "x-")
        self.recv("3+", land.at[4], "x+")
        self.recv("3-", land.at[5], "x-")
        for half, (one, two) in enumerate(((3, 4), (2, 5))):
            rows = self.rows(net.x, half)
            self.g32[rows] = self.g32[rows] + land[one].astype(F32) + land[two].astype(F32)
        over[...] = self.g32[self.rows(net.x, 1 - net.h)].astype(BF)
        self.send("h", over, "h", back)

    def final(self):
        net = self.net
        back = self.refs[4]
        self.recv("h", back, "h")
        rows = self.rows(net.x, net.h)
        self.res[rows] = (self.g32[rows] + back[...].astype(F32)).astype(BF)
        for key, where in (("e0", "h"), ("e1+", "x+"), ("e1-", "x-")):
            self.send(key, self.res.at[rows], where)

    def spread(self):
        net = self.net
        rows = self.res.at[self.rows(net.x, 1 - net.h)]
        self.recv("e0", rows, "h")
        self.send("e2+", rows, "x+")
        self.send("e2-", rows, "x-")

    def forward(self):
        net = self.net
        for way, d, half in (("+", -1, 0), ("-", 1, 1)):
            x = net.xmod(d)
            self.recv("e1" + way, self.res.at[self.rows(x, net.h)], "x" + way)
            self.recv("e2" + way, self.res.at[self.rows(x, 1 - net.h)], "x" + way)
            self.send("f" + way, self.res.at[self.rows(x, half)], "x" + way)

    def end(self):
        net = self.net
        for way, half in (("+", 0), ("-", 1)):
            self.recv("f" + way, self.res.at[self.rows(net.xmod(2), half)], "x" + way)


class HFirst(GradSum):
    def part(self, half):
        low = self.size // 32 * 16 or self.size
        return (0, low) if half == 0 else (low, self.size - low)

    def rows(self, h, x, half=None):
        at, size = (0, self.size) if half is None else self.part(half)
        return pl.ds(pl.multiple_of(self.base + (h * NX + x) * self.size + at, 16), size)

    def ways(self, plan):
        return [m for m in plan if self.part(m[-1])[1]]

    def start(self):
        net = self.net
        first, land = self.refs[:2]
        for i in range(NX):
            first[i] = self.g32[self.rows(1 - net.h, i)].astype(BF)
        for d in (2, 1, -1, 0):
            x = net.xmod(d)
            self.send(("0", d), first.at[x], "h", land.at[x])

    def pair(self, d):
        net = self.net
        back, total, second = self.refs[1:4]
        x = net.xmod(d)
        self.recv(("0", d), back.at[x], "h")
        value = self.g32[self.rows(net.h, x)] + back[x].astype(F32)
        total[x] = value
        second[x] = value.astype(BF)

    def pass_on(self, n, key, way, d, half):
        second, ring = self.refs[3:5]
        if self.part(half)[1]:
            at = pl.ds(*self.part(half))
            self.send(key, second.at[self.net.xmod(d), at], "x" + way, ring.at[n, at])

    def cross_far(self):
        self.pair(2)
        self.pass_on(0, "1+", "+", 2, 0)
        self.pass_on(1, "1-", "-", 2, 1)

    def cross(self):
        self.pair(1)
        self.pass_on(2, "2+", "+", 1, 1)
        self.pair(-1)
        self.pass_on(3, "2-", "-", -1, 0)
        self.pair(0)

    def relay(self):
        net = self.net
        total, _, ring, third = self.refs[2:]
        for n, way, d, half in self.ways(((0, "+", 1, 0), (1, "-", -1, 1))):
            at = pl.ds(*self.part(half))
            self.recv("1" + way, ring.at[n, at], "x" + way)
            third[n, at] = (total[net.xmod(d), at] + ring[n, at].astype(F32)).astype(BF)
            self.send("3" + way, third.at[n, at], "x" + way, ring.at[4 + n, at])

    def final(self):
        net = self.net
        total, _, ring = self.refs[2:5]
        plan = ((2, "2+", "+", 1), (3, "2-", "-", 0), (4, "3+", "+", 0), (5, "3-", "-", 1))
        for n, key, way, half in self.ways(plan):
            self.recv(key, ring.at[n, pl.ds(*self.part(half))], "x" + way)
        for one, two, half in self.ways(((3, 4, 0), (2, 5, 1))):
            at = pl.ds(*self.part(half))
            value = total[net.x, at] + ring[one, at].astype(F32) + ring[two, at].astype(F32)
            self.res[self.rows(net.h, net.x, half)] = value.astype(BF)
        rows = self.res.at[self.rows(net.h, net.x)]
        for key, where in (("q+", "x+"), ("q-", "x-"), ("p0", "h")):
            self.send(key, rows, where)

    def forward(self):
        net = self.net
        for n, (way, d, half) in enumerate((("+", -1, 0), ("-", 1, 1))):
            x = net.xmod(d)
            rows = self.res.at[self.rows(net.h, x)]
            self.recv("q" + way, rows, "x" + way)
            if self.part(half)[1]:
                self.send("s" + way, self.res.at[self.rows(net.h, x, half)], "x" + way)
            self.send("p%d" % (n + 1), rows, "h")

    def spread(self):
        net = self.net
        x = net.xmod(2)
        for way, half in self.ways((("+", 0), ("-", 1))):
            self.recv("s" + way, self.res.at[self.rows(net.h, x, half)], "x" + way)
        self.send("p3", self.res.at[self.rows(net.h, x)], "h")

    def end(self):
        net = self.net
        for n, d in enumerate((0, -1, 1, 2)):
            self.recv("p%d" % n, self.res.at[self.rows(1 - net.h, net.xmod(d))], "h")


class RowSum:
    def __init__(self, net, part, from_core, stage, land, ys, yr):
        self.net, self.part, self.from_core = net, part, from_core
        self.stage, self.land, self.ys, self.yr = stage, land, ys, yr
        self.at = {}
        for way in ("+", "-"):
            for lane in ("o", "x"):
                for step in range(1, self.limit(way, lane) + 1):
                    self.at[way, lane, step] = len(self.at)

    def limit(self, way, lane):
        return 4 if (way == "+") == (lane == "o") else 3

    def swap(self, d):
        net = self.net
        z = net.zmod(d)
        net.send(("c", d), self.part.at[1 - net.k, z], "c", self.from_core.at[z])

    def swapped(self, d):
        self.net.recv(("c", d), self.from_core.at[self.net.zmod(d)], "c")

    def own(self, d, lane):
        net = self.net
        z = net.zmod(d)
        y = net.y if lane == "o" else 1 - net.y
        return self.part[net.k, z, y].astype(F32) + self.from_core[z, y].astype(F32)

    def landed(self, way, lane, step):
        n = self.at[way, lane, step]
        self.net.recv(("z", way, lane, step), self.land.at[n], way)
        return self.land[n].astype(F32)

    def step(self, step):
        for lane in ("o", "x"):
            for way in ("+", "-"):
                top = self.limit(way, lane)
                if step > top:
                    continue
                left = top - step + 1
                d = left if way == "+" or left == 4 else -left
                total = self.own(d, lane)
                if step > 1:
                    total = total + self.landed(way, lane, step - 1)
                n = self.at[way, lane, step]
                self.stage[n] = total.astype(BF)
                self.net.send(("z", way, lane, step), self.stage.at[n], way, self.land.at[n])

    def across(self):
        total = self.own(0, "x")
        for way in ("+", "-"):
            total = total + self.landed(way, "x", self.limit(way, "x"))
        self.ys[...] = total.astype(BF)
        self.net.send("y", self.ys, "y", self.yr)

    def result(self):
        total = self.own(0, "o")
        for way in ("+", "-"):
            total = total + self.landed(way, "o", self.limit(way, "o"))
        self.net.recv("y", self.yr, "y")
        return total + self.yr[...].astype(F32)


def kernel(
    q_hbm,
    k_hbm,
    v_hbm,
    seg_hbm,
    start_hbm,
    len_hbm,
    w_hbm,
    gain_hbm,
    gate_hbm,
    up_hbm,
    down_hbm,
    cot_hbm,
    ctx_out,
    talker_out,
    grads_out,
    gk,
    gv,
    gr,
    gc,
    q_raw,
    q_buf,
    ctx_buf,
    w_buf,
    cot_buf,
    seg_buf,
    start_buf,
    len_buf,
    gain_buf,
    gate_w,
    up_w,
    down_w,
    segq,
    bias,
    m_buf,
    acc_buf,
    own_buf,
    out_buf,
    hid,
    d_gate,
    d_up,
    hid_rows,
    g32,
    res,
    b1_refs,
    a1_refs,
    a2_refs,
    b2_refs,
    a3_refs,
    part,
    from_core,
    stage,
    land,
    ys,
    yr,
    send_sems,
    recv_sems,
    local_sems,
):
    net = Net(send_sems, recv_sems)
    z, r = net.z, net.r

    def load(n, src, dst):
        copy = pltpu.make_async_copy(src, dst, local_sems.at[n])
        copy.start()
        return copy

    at_k = pl.ds(pl.multiple_of(r * KROWS, 16), TOK)
    at_aux = pl.ds(pl.multiple_of(r * KROWS + TOK, 16), AUX)
    at_v = pl.ds(pl.multiple_of(r * TOK, 16), TOK)
    at_row = pl.ds(pl.multiple_of(r * SLOTS, 16), SLOTS)
    load_seg = load(0, seg_hbm, seg_buf)
    load_k = load(1, k_hbm.at[0], gk.at[z, at_k])
    load_v = load(2, v_hbm.at[0], gv.at[z, at_v])
    load_q = load(3, q_hbm.at[0], q_raw)
    load_start = load(4, start_hbm, start_buf)
    load_len = load(5, len_hbm, len_buf)
    load_cot = load(6, cot_hbm.at[0], cot_buf)
    load_w = load(7, w_hbm, w_buf)
    load_gain = load(8, gain_hbm, gain_buf)
    load_ffn = [
        load(9, gate_hbm, gate_w),
        load(10, up_hbm, up_w),
        load(11, down_hbm, down_w),
    ]

    barrier = pltpu.get_barrier_semaphore()
    places = ("+", "-", "y", "c", "x+", "x-", "h")
    net.greet(barrier, places)

    load_seg.wait()
    seg_row = seg_buf[...].astype(F32)
    gk[z, at_aux, 0:D] = jnp.broadcast_to(seg_row, (AUX, D)).astype(BF)
    gk[z, at_aux, D : 2 * D] = jnp.zeros((AUX, D), BF)

    keys = Gather(net, "k", gk, True, KROWS)
    vals = Gather(net, "v", gv, False, TOK)
    rows = Gather(net, "r", gr, True, SLOTS)
    cots = Gather(net, "g", gc, False, SLOTS)

    load_k.wait()
    load_v.wait()
    pl.semaphore_wait(barrier, len(places))
    keys.start()
    vals.start()

    segq[...] = jnp.transpose(jnp.broadcast_to(seg_row, (TOK, D)))
    m_buf[...] = jnp.full(m_buf.shape, NEG, F32)
    acc_buf[...] = jnp.zeros(acc_buf.shape, F32)
    load_q.wait()
    for h in range(HEADS):
        q_buf[h] = q_raw[:, h * D : (h + 1) * D]

    load_start.wait()
    load_len.wait()
    start = start_buf[0, net.ctx] - net.ctx * TOK
    length = len_buf[0, net.ctx]
    slot_id = lax.broadcasted_iota(jnp.int32, (SLOTS, TOK), 0)
    place = lax.broadcasted_iota(jnp.int32, (SLOTS, TOK), 1)
    packer = jnp.where((place - start == slot_id) & (slot_id < length), 1.0, 0.0).astype(BF)
    load_cot.wait()
    gc[z, at_row] = jnp.dot(packer, cot_buf[...], preferred_element_type=F32).astype(BF)
    for i in range(NZ):
        for buf in (gr, gc):
            buf[i, 4 * SLOTS :] = jnp.zeros((CHUNK - 4 * SLOTS, TD), BF)

    factor = math.log2(math.e) / math.sqrt(D)

    def attend(d):
        zc = net.zmod(d)

        def work():
            for b in range(4):
                aux = b * KROWS + TOK
                ok = segq[...] == gk[zc, aux : aux + AUX, 0:D].astype(F32)[0:1]
                if d == 0:
                    kpos = lax.broadcasted_iota(jnp.int32, (TOK, D), 1) + (b - r) * TOK
                    qpos = lax.broadcasted_iota(jnp.int32, (TOK, D), 0)
                    ok = ok & (kpos <= qpos)
                bias[:, b * TOK : (b + 1) * TOK] = jnp.where(ok, 0.0, NEG)

            def head(i, carry):
                for kv in range(KV_HEADS):
                    h = i + kv * GROUP
                    lanes = slice(kv * D, (kv + 1) * D)
                    kc = jnp.concatenate(
                        [gk[zc, b * KROWS : b * KROWS + TOK, lanes] for b in range(4)], axis=0
                    )
                    vc = jnp.concatenate([gv[zc, :, lanes], jnp.ones((4 * TOK, D), BF)], axis=1)
                    s = lax.dot_general(q_buf[h], kc, NT, preferred_element_type=F32)
                    s = s * factor + bias[...]
                    m_old = m_buf[h]
                    m_new = jnp.maximum(m_old, jnp.max(s, axis=1, keepdims=True))
                    p = jnp.exp2(s - jnp.concatenate([m_new] * 4, axis=1)).astype(BF)
                    alpha = jnp.exp2(m_old - m_new)
                    m_buf[h] = m_new
                    acc_buf[h] = acc_buf[h] * jnp.concatenate([alpha, alpha], axis=1) + jnp.dot(
                        p, vc, preferred_element_type=F32
                    )
                return carry

            lax.fori_loop(0, GROUP, head, 0, unroll=True)

        if d == 0:
            work()
        else:
            pl.when(zc < z)(work)

    def attend_one(d):
        keys.from_core(d)
        vals.from_core(d)
        attend(d)

    def attend_step(step):
        for d in around(step):
            attend_one(d)

    vals.crosses(0)
    keys.cross(0)
    for step in range(1, 5):
        vals.ring(step, "o")
        keys.ring(step, "ox")
        if step == 3:
            cots.start()
        if step == 4:
            cots.ring(1, "o")
            cots.crosses(0)
            attend_one(-3)
            vals.crosses(4)
            attend_one(3)
        else:
            attend_step(step - 1)
            vals.crosses(step)
        net.settle()
    cots.ring(2, "o")
    cots.crosses(1)
    attend_step(4)

    for h in range(HEADS):
        acc = acc_buf[h]
        ctx_buf[:, h * D : (h + 1) * D] = (acc[:, 0:D] / acc[:, D : 2 * D]).astype(BF)
    load_w.wait()
    load_gain.wait()
    packed = jnp.dot(packer, ctx_buf[...], preferred_element_type=F32).astype(BF)
    own = jnp.dot(packed, w_buf[...], preferred_element_type=F32).astype(BF)
    own_buf[...] = own
    own = own.astype(F32)
    scale = lax.rsqrt(jnp.mean(own * own, axis=-1, keepdims=True) + 1e-06)
    gr[z, at_row] = (own * scale * gain_buf[...]).astype(BF)

    rows.start()
    save_ctx = load(12, ctx_buf, ctx_out)
    for wait in load_ffn:
        wait.wait()

    def ffn_in(d):
        rows.from_core(d)
        cots.from_core(d)
        zc = net.zmod(d)
        at = pl.ds(pl.multiple_of(zc * CHUNK, CHUNK), CHUNK)
        row = gr[zc]
        gate = lax.dot_general(gate_w[...], row, NT, preferred_element_type=F32)
        up = lax.dot_general(up_w[...], row, NT, preferred_element_type=F32)
        d_hidden = lax.dot_general(down_w[...], gc[zc], NT, preferred_element_type=F32)
        sig = jax.nn.sigmoid(gate)
        act = gate * sig
        hidden = act * up
        hid[:, at] = hidden.astype(BF)
        hid_rows[zc] = jnp.transpose(hidden).astype(BF)
        d_gate[:, at] = (d_hidden * up * sig * (1.0 + gate * (1.0 - sig))).astype(BF)
        d_up[:, at] = (d_hidden * act).astype(BF)

    cots.ring(3, "o")
    cots.crosses(2)
    rows.cross(0)
    cots.ring(4, "o")
    cots.crosses(3)
    sums = RowSum(net, part, from_core, stage, land, ys, yr)

    def ffn_out(*shifts):
        for d in shifts:
            zc = net.zmod(d)
            total = jnp.dot(
                hid_rows[zc, 0 : 4 * SLOTS], down_w[...], preferred_element_type=F32
            ).astype(BF)
            for b in range(4):
                part[b % 2, zc, b // 2] = total[b * SLOTS : (b + 1) * SLOTS]
            sums.swap(d)

    rows.ring(1, "ox")
    ffn_in(0)
    ffn_out(0)
    net.settle()
    rows.ring(2, "ox")
    cots.crosses(4)
    ffn_in(-1)
    ffn_in(1)
    ffn_out(-1, 1)
    net.settle()
    rows.ring(3, "ox")
    ffn_in(-2)
    ffn_in(2)
    ffn_out(-2, 2)
    ffn_in(-3)
    ffn_in(3)
    net.settle()
    rows.ring(4, "ox")
    ffn_out(3, -3)
    ffn_in(4)

    b1 = HFirst(net, "b1", g32, res, 0, 32, b1_refs)
    a1 = XFirst(net, "a1", g32, res, 256, 32, a1_refs)
    a2 = XFirst(net, "a2", g32, res, 512, 16, a2_refs)
    b2 = HFirst(net, "b2", g32, res, 640, 16, b2_refs)
    a3 = XFirst(net, "a3", g32, res, 768, 16, a3_refs)

    def grad(n, left, right):
        g32[n * FFD : (n + 1) * FFD] = jnp.dot(
            left[...], right[...].reshape(NZ * CHUNK, TD), preferred_element_type=F32
        )

    def swapped(*shifts):
        for d in shifts:
            sums.swapped(d)

    grad(0, hid, gc)
    b1.start()
    ffn_out(4)
    grad(1, d_gate, gr)
    a1.start()
    swapped(4, 3, -3)
    sums.step(1)
    g32[3 * FFD :] = jnp.zeros((GROWS - 3 * FFD, TD), F32)
    grad(2, d_up, gr)
    b2.start()
    a2.start()
    a3.start()
    b1.cross_far()
    a1.relay()
    swapped(2, -2)
    sums.step(2)
    a2.relay()
    a3.relay()
    b1.cross()
    net.settle()
    b1.relay()
    b2.cross_far()
    a1.cross()
    a2.cross()
    a3.cross()
    b2.cross()
    b2.relay()
    swapped(1, -1, 0)
    sums.step(3)
    b1.final()
    net.settle()
    a1.final()
    b2.final()
    a2.final()
    a3.final()
    b1.forward()
    sums.step(4)
    b2.forward()
    a1.spread()
    a2.spread()
    a3.spread()
    b1.spread()
    b2.spread()
    sums.across()
    net.settle()
    a2.forward()
    a3.forward()
    a1.forward()

    place = lax.broadcasted_iota(jnp.int32, (TOK, SLOTS), 0)
    slot_id = lax.broadcasted_iota(jnp.int32, (TOK, SLOTS), 1)
    spread = jnp.where((place - start == slot_id) & (slot_id < length), 1.0, 0.0).astype(BF)
    out_rows = (own_buf[...].astype(F32) + sums.result()).astype(BF)
    out_buf[...] = jnp.dot(spread, out_rows, preferred_element_type=F32).astype(BF)
    save_out = load(13, out_buf, talker_out)

    saves = [save_ctx, save_out]
    for n, grads in enumerate((b1, b2, a2, a3, a1)):
        grads.end()
        at = pl.ds(grads.base, 8 * grads.size)
        saves.append(load(14 + n, res.at[at], grads_out.at[at]))
    net.drain()
    for save in saves:
        save.wait()


def x_first(size):
    shapes = ((NX, 2, size, TD), (6, size, TD), (2, size, TD), (size, TD), (size, TD))
    return [pltpu.VMEM(shape, BF) for shape in shapes]


def h_first(size):
    piece = pltpu.VMEM((NX, size, TD), BF)
    return [
        piece,
        piece,
        pltpu.VMEM((NX, size, TD), F32),
        piece,
        pltpu.VMEM((6, size, TD), BF),
        pltpu.VMEM((2, size, TD), BF),
    ]


def fused(*args):
    hbm = pl.BlockSpec(memory_space=pl.ANY)
    scratch = (
        ((NZ, 4 * KROWS, KW), BF),
        ((NZ, 4 * TOK, KW), BF),
        ((NZ, CHUNK, TD), BF),
        ((NZ, CHUNK, TD), BF),
        ((TOK, QW), BF),
        ((HEADS, TOK, D), BF),
        ((TOK, QW), BF),
        ((QW, TD), BF),
        ((TOK, TD), BF),
        ((1, TOK), jnp.int32),
        pltpu.SMEM((1, 32), jnp.int32),
        pltpu.SMEM((1, 32), jnp.int32),
        ((TD,), F32),
        ((FFD, TD), BF),
        ((FFD, TD), BF),
        ((FFD, TD), BF),
        ((TOK, D), F32),
        ((TOK, 4 * TOK), F32),
        ((HEADS, TOK, D), F32),
        ((HEADS, TOK, 2 * D), F32),
        ((SLOTS, TD), BF),
        ((TOK, TD), BF),
        ((FFD, NZ * CHUNK), BF),
        ((FFD, NZ * CHUNK), BF),
        ((FFD, NZ * CHUNK), BF),
        ((NZ, CHUNK, FFD), BF),
        ((GROWS, TD), F32),
        ((GROWS, TD), BF),
        h_first(32),
        x_first(32),
        x_first(16),
        h_first(16),
        x_first(16),
        ((2, NZ, 2, SLOTS, TD), BF),
        ((NZ, 2, SLOTS, TD), BF),
        ((14, SLOTS, TD), BF),
        ((14, SLOTS, TD), BF),
        ((SLOTS, TD), BF),
        ((SLOTS, TD), BF),
        pltpu.SemaphoreType.DMA((256,)),
        pltpu.SemaphoreType.DMA((256,)),
        pltpu.SemaphoreType.DMA((24,)),
    )
    return pl.pallas_call(
        kernel,
        name="mega",
        out_shape=[
            jax.ShapeDtypeStruct((TOK, QW), BF),
            jax.ShapeDtypeStruct((TOK, TD), BF),
            jax.ShapeDtypeStruct((GROWS, TD), BF),
        ],
        in_specs=[hbm] * len(args),
        out_specs=[hbm] * 3,
        scratch_shapes=[pltpu.VMEM(*s) if isinstance(s, tuple) else s for s in scratch],
        compiler_params=pltpu.CompilerParams(
            collective_id=1, has_side_effects=True, vmem_limit_bytes=VMEM_LIMIT
        ),
    )(*args)


def finish_kernel(ctx_in, talker_in, grads_in, ctx_out, talker_out, down_out, gate_out, up_out, low, wide, ctx_buf, talker_buf, sems):
    def move(n, src, dst):
        copy = pltpu.make_async_copy(src, dst, sems.at[n])
        copy.start()
        return copy

    step = 128
    loads = [
        move(n, grads_in.at[pl.ds(n * step, step)], low.at[pl.ds(n * step, step)])
        for n in range(GROWS // step)
    ]
    hops = [
        (move(7, ctx_in, ctx_buf), 12, ctx_buf, ctx_out.at[0]),
        (move(8, talker_in, talker_buf), 13, talker_buf, talker_out.at[0]),
    ]
    moves = []
    for hop, n, src, dst in hops:
        hop.wait()
        moves.append(move(n, src, dst))
    outs = [down_out, gate_out, up_out]
    for n, load in enumerate(loads):
        load.wait()
        wide[n * step : (n + 1) * step] = low[n * step : (n + 1) * step].astype(F32)
        done = 3 - len(outs)
        if outs and (n + 1) * step >= (done + 1) * FFD:
            moves.append(move(9 + done, wide.at[pl.ds(done * FFD, FFD)], outs.pop(0)))
    for copy in moves:
        copy.wait()


def finish(context, talker, grads):
    hbm = pl.BlockSpec(memory_space=pl.ANY)
    grad = jax.ShapeDtypeStruct((FFD, TD), F32)
    return pl.pallas_call(
        finish_kernel,
        name="finish",
        out_shape=[
            jax.ShapeDtypeStruct((1, TOK, QW), BF),
            jax.ShapeDtypeStruct((1, TOK, TD), BF),
            grad,
            grad,
            grad,
        ],
        in_specs=[hbm] * 3,
        out_specs=[hbm] * 5,
        scratch_shapes=[
            pltpu.VMEM((GROWS, TD), BF),
            pltpu.VMEM((GROWS, TD), F32),
            pltpu.VMEM((TOK, QW), BF),
            pltpu.VMEM((TOK, TD), BF),
            pltpu.SemaphoreType.DMA((16,)),
        ],
        compiler_params=pltpu.CompilerParams(vmem_limit_bytes=VMEM_LIMIT),
    )(context, talker, grads)


def shards(*args):
    context, talker, grad_down, grad_gate, grad_up = finish(*fused(*args))
    return (context, talker, grad_gate, grad_up, grad_down)


def solution(mesh):
    in_specs = (
        P("grp", "ctx", None),
        P("grp", "ctx", None),
        P("grp", "ctx", None),
        P("grp", "ctx"),
        P("grp", None),
        P("grp", None),
        P(),
        P(),
        P("ctx", None),
        P("ctx", None),
        P("ctx", None),
        P("grp", "ctx", None),
    )
    out_specs = (
        P("grp", "ctx", None),
        P("grp", "ctx", None),
        P("ctx", None),
        P("ctx", None),
        P("ctx", None),
    )
    return jax.shard_map(shards, mesh=mesh, in_specs=in_specs, out_specs=out_specs, check_vma=False)
```
